32 devices in a mesh: groups: 2 (over x), seq: 8 (over z, y), head: 2 (over core).
Axes of the slice: x: 2, y: 2, z: 4, core: 2. Of those that a mesh axis runs over, the one named last changes fastest.
Arguments:
- tokens: bfloat16 [4096, 1024], P(('groups', 'seq')), parts along dimension 0, may hold values from -6 to 6
- norm_gain: float32 [1024], replicated, may hold values from 1 to 5
- w_qkv: bfloat16 [3, 1024, 1024], P(None, None, 'head'), may hold values from -0.1875 to 0.1875
- w_out: bfloat16 [1024, 1024], P('head'), may hold values from -0.1875 to 0.1875
- readout_weight: bfloat16 [1024, 128], replicated, may hold values from -0.1875 to 0.1875
- targets: float32 [512, 128], P('groups'), parts along dimension 0, may hold values from -6 to 6
- key_blocks: int32 [32, 4], P('groups'), parts along dimension 0, may hold values from 0 to 15, as said below
- list_len: int32 [32], P('groups'), parts along dimension 0, may hold values from 1 to 4
- voxel_panel: int32 [4096, 1], P('groups'), parts along dimension 0, may hold values from 0 to 255
Outputs:
- grad_tokens: float32 [4096, 1024], P(('groups', 'seq'), 'head'), parts along dimension 0
- loss_mean: float32 [2], P('groups'), parts along dimension 0
The draws below stay inside these ranges and needn't reach their ends.
There are 2 independent parts, one for each index of `groups`. The reference program is written for one: setup_inputs(seed, part) draws one part's arguments, and reference() takes and returns one part's arrays. A program takes and returns all parts, laid end to end along the dimension named above; an argument that names none is the same for every part. Nothing has to cross between parts.
Inputs may be any that keep to these rules, and one draw needn't show every extreme that they name: `key_blocks`: each row holds distinct block numbers; every number k in row b has k div (2) within one of b div (2). `voxel_panel`: every panel 0 to 255 holds at least one token of its district.
All inputs are finite; a program needn't handle non-finite values.
Results may differ from the reference program's by a relative error of at most 0.035.
The reference program's roundings to bfloat16 on the way count: a program that leaves them out, or rounds other values in their place, can miss the bound.
Values may be sent and summed in bfloat16 or wider, within the bound.
No kernel may reach another device: no remote copies, remote signals or barrier semaphores. Data moves between devices by JAX's collectives and lax.ppermute only.
A program may use at most 128 MiB of HBM per device.

```python
import math
import jax
import jax.numpy as jnp
from jax import lax

D = 1024
HEADS = 16
HD = 64
BLK = 128
LIST = 4
R = 128
TOK_DEV = 256
TOKENS = 2048
NB = 16
PANELS = 256


def draw_tokens(key, part):
    first = jax.random.fold_in(key, 0)
    return jnp.clip(jax.random.normal(first, (TOKENS, D), jnp.float32), -6.0, 6.0).astype(jnp.bfloat16)


def draw_w_qkv(key, part):
    first = jax.random.fold_in(key, 0)
    return (jnp.clip(jax.random.normal(first, (3, D, D), jnp.float32), -6.0, 6.0) * D ** (-0.5)).astype(jnp.bfloat16)


def draw_norm_gain(key, part):
    unit = jax.random.uniform(key, (D,), jnp.float32)
    return jnp.exp(unit * jnp.log(3.0))


def draw_key_blocks(key, part):
    per_stretch = TOK_DEV // BLK
    blocks = jnp.arange(NB, dtype=jnp.int32)
    stretch = blocks // per_stretch
    offsets = jnp.arange(3 * per_stretch, dtype=jnp.int32)
    candidate = (stretch[:, None] - 1) * per_stretch + offsets[None, :]
    usable = (candidate >= 0) & (candidate < NB)
    scores = jax.random.randint(key, (NB, 3 * per_stretch), 0, 1 << 20) * (3 * per_stretch) + offsets[None, :]
    scores = jnp.where(usable, scores, -1)
    picked_scores, picked = lax.top_k(scores, LIST)
    return jnp.take_along_axis(candidate, picked, axis=1).astype(jnp.int32)


def draw_list_len(key, part):
    lengths = jax.random.randint(key, (NB,), 1, LIST + 1)
    lengths = lengths.at[0].set(LIST).at[1].set(1)
    return lengths.astype(jnp.int32)


def level_of(rng, shape, cuts, least, largest):
    def one(axis_at, shards_of):
        heights = jax.random.uniform(jax.random.fold_in(jax.random.fold_in(rng, 6), axis_at), (shards_of,), jnp.float32, least / len(cuts), largest / len(cuts))
        return jnp.repeat(jnp.exp(heights), shape[axis_at] // shards_of).reshape((-1,) + (1,) * (len(shape) - axis_at - 1))

    gain = one(*cuts[0])
    for cut in cuts[1:]:
        gain = gain * one(*cut)
    return gain


def distinct(stream_key, rows, amount, top, lift):
    ranking = jax.random.permutation(jax.random.fold_in(stream_key, 1), amount)
    favour = ranking
    for power in range(3):
        favour = favour * favour // amount
    favour = favour * lift // amount
    chance = jax.random.randint(jax.random.fold_in(stream_key, 2), (rows, amount), 0, 4096) + favour
    sure = jax.random.permutation(jax.random.fold_in(stream_key, 3), rows)[jnp.arange(amount) % rows]
    chance = jnp.where(jnp.arange(rows)[:, None] == sure[None, :], 1 << 14, chance)
    score = chance * amount + jnp.arange(amount)
    return lax.top_k(score.astype(jnp.int32), top)[1].astype(jnp.int32)


def scatter_about(key, shape, deviation, most, cuts=(), kind=jnp.bfloat16):
    entries = jax.random.normal(key, shape, jnp.float32) * deviation
    if len(cuts) > 0:
        entries = level_of(key, shape, cuts, -0.22, 0.18) * entries
    return jnp.clip(entries, min=-most, max=most).astype(kind)


def setup_inputs(seed: int = 0, part: int = 0) -> dict:
    seeds = jax.random.split(jax.random.key(seed), 10)
    part_keys = jax.random.split(jax.random.fold_in(seeds[9], part), 10)
    return {
        "tokens": draw_tokens(jax.random.fold_in(jax.random.fold_in(seeds[9], part), 71), part),
        "norm_gain": draw_norm_gain(jax.random.fold_in(seeds[9], 71), part),
        "w_qkv": draw_w_qkv(jax.random.fold_in(seeds[9], 71), part),
        "w_out": scatter_about(seeds[3], (D, D), D ** -0.5, 0.1875, ((0, 2),)),
        "readout_weight": scatter_about(seeds[4], (D, R), D ** -0.5, 0.1875),
        "targets": scatter_about(part_keys[5], (PANELS, R), 1.0, 6.0, (), jnp.float32),
        "key_blocks": draw_key_blocks(jax.random.fold_in(jax.random.fold_in(seeds[9], part), 71), part),
        "list_len": draw_list_len(jax.random.fold_in(jax.random.fold_in(seeds[9], part), 71), part),
        "voxel_panel": distinct(part_keys[8], TOKENS, PANELS, 1, 64),
    }


def softmax_weights(queries, key_rows, live_keys, score_scale):
    scores = jnp.einsum('...qd,...kd->...qk', queries.astype(jnp.float32), key_rows.astype(jnp.float32)) * score_scale
    scores = jnp.where(live_keys, scores, -1e+30)
    top_score = lax.optimization_barrier(jnp.max(scores, axis=-1, keepdims=True))
    expo = jnp.where(live_keys, jnp.exp(scores - top_score), jnp.float32(0.0))
    return expo / lax.optimization_barrier(jnp.sum(expo, axis=-1, keepdims=True))

def attend_back(queries, key_rows, value_matrix, weight, attended_rows, output_gradient, score_scale):
    grad_weight = jnp.einsum('...qd,...kd->...qk', output_gradient.astype(jnp.float32), value_matrix.astype(jnp.float32))
    row_delta = lax.optimization_barrier(jnp.sum(output_gradient.astype(jnp.float32) * attended_rows.astype(jnp.float32), axis=-1, keepdims=True))
    grad_score = (weight * (grad_weight - row_delta) * score_scale).astype(jnp.bfloat16)
    grad_query = jnp.einsum('...qk,...kd->...qd', grad_score.astype(jnp.float32), key_rows.astype(jnp.float32)).astype(jnp.bfloat16)
    grad_key = jnp.einsum('...qk,...qd->...kd', grad_score.astype(jnp.float32), queries.astype(jnp.float32))
    second_weight = weight.astype(jnp.bfloat16)
    grad_value = jnp.einsum('...qk,...qd->...kd', second_weight.astype(jnp.float32), output_gradient.astype(jnp.float32))
    return (grad_query, grad_key, grad_value)

def reference(tokens, norm_gain, w_qkv, w_out, readout_weight, targets, key_blocks, list_len, voxel_panel):
    score_scale = 1.0 / math.sqrt(HD)
    inputs = tokens.astype(jnp.float32)
    root_mean = jnp.sqrt(lax.optimization_barrier(jnp.mean(inputs * inputs, axis=-1, keepdims=True)) + 1e-05)
    normed = (inputs * norm_gain / root_mean).astype(jnp.bfloat16)
    projected_rows = jnp.stack([jnp.dot(normed, w_qkv[part], preferred_element_type=jnp.float32) for part in range(3)]).astype(jnp.bfloat16)
    block_count = TOKENS // BLK
    live_slots = jnp.arange(LIST)[None, :] < list_len[:, None]
    live_keys = jnp.repeat(live_slots, BLK, axis=1)[:, None, :]
    flat_lists = key_blocks.reshape(-1)

    def head_parts(head):
        first = (head * HD).astype(jnp.int32)
        pieces = [lax.dynamic_slice_in_dim(projected_rows[part], first, HD, 1) for part in range(3)]
        queries = pieces[0].reshape(block_count, BLK, HD)
        key_rows = pieces[1].reshape(block_count, BLK, HD)[key_blocks].reshape(block_count, LIST * BLK, HD)
        value_matrix = pieces[2].reshape(block_count, BLK, HD)[key_blocks].reshape(block_count, LIST * BLK, HD)
        return (queries, key_rows, value_matrix)

    def head_forward(head):
        queries, key_rows, value_matrix = head_parts(head)
        second_weight = softmax_weights(queries, key_rows, live_keys, score_scale).astype(jnp.bfloat16)
        attended_rows = jnp.einsum('ucn,unj->ucj', second_weight.astype(jnp.float32), value_matrix.astype(jnp.float32)).astype(jnp.bfloat16)
        return attended_rows.reshape(TOKENS, HD)
    attended_rows = lax.map(head_forward, jnp.arange(HEADS, dtype=jnp.int32))
    attended_flat = attended_rows.transpose(1, 0, 2).reshape(TOKENS, D)
    readout_mix = jnp.dot(w_out, readout_weight, preferred_element_type=jnp.float32).astype(jnp.bfloat16)
    read_rows = jnp.dot(attended_flat, readout_mix, preferred_element_type=jnp.float32)
    panel_ids = voxel_panel[:, 0]
    counts = jax.ops.segment_sum(jnp.ones((TOKENS,), jnp.float32), panel_ids, num_segments=PANELS)
    panel_sums = jax.ops.segment_sum(read_rows, panel_ids, num_segments=PANELS)
    residual = panel_sums / counts[:, None] - targets
    loss_mean = 0.5 * jnp.sum(counts[:, None] * residual * residual) / (TOKENS * R)
    grad_read = residual[panel_ids]
    attended_gradient = jnp.dot(grad_read, readout_mix.astype(jnp.float32).T, precision=lax.Precision.HIGHEST).astype(jnp.bfloat16)

    def head_backward(head):
        queries, key_rows, value_matrix = head_parts(head)
        weight = softmax_weights(queries, key_rows, live_keys, score_scale)
        first = (head * HD).astype(jnp.int32)
        output_gradient = lax.dynamic_slice_in_dim(attended_gradient, first, HD, 1).reshape(block_count, BLK, HD)
        own_out = attended_rows[head].reshape(block_count, BLK, HD)
        grad_query, grad_key, grad_value = attend_back(queries, key_rows, value_matrix, weight, own_out, output_gradient, score_scale)
        key_total = jnp.zeros((block_count, BLK, HD), jnp.float32).at[flat_lists].add(grad_key.reshape(block_count * LIST, BLK, HD))
        value_total = jnp.zeros((block_count, BLK, HD), jnp.float32).at[flat_lists].add(grad_value.reshape(block_count * LIST, BLK, HD))
        return jnp.stack([grad_query.reshape(TOKENS, HD), key_total.astype(jnp.bfloat16).reshape(TOKENS, HD), value_total.astype(jnp.bfloat16).reshape(TOKENS, HD)])
    head_grads = lax.map(head_backward, jnp.arange(HEADS, dtype=jnp.int32))
    grad_proj = head_grads.transpose(1, 2, 0, 3).reshape(3, TOKENS, D)
    grad_normed = jnp.dot(grad_proj[0], w_qkv[0].T, preferred_element_type=jnp.float32)
    grad_normed = grad_normed + jnp.dot(grad_proj[1], w_qkv[1].T, preferred_element_type=jnp.float32)
    grad_normed = grad_normed + jnp.dot(grad_proj[2], w_qkv[2].T, preferred_element_type=jnp.float32)
    scaled = norm_gain * grad_normed
    gradient = scaled / root_mean - inputs * lax.optimization_barrier(jnp.sum(inputs * scaled, axis=-1, keepdims=True)) / (D * root_mean ** 3)
    return (gradient, loss_mean.reshape(1))
```

```python
import functools
import math

import jax
import jax.numpy as jnp
import numpy as np
from jax import lax
from jax.experimental import pallas as pl
from jax.experimental.pallas import tpu as pltpu
from jax.sharding import PartitionSpec as P

HD = 64
BLK = 128
LIST = 4
PAIR = 2 * HD
F32 = jnp.float32
BF16 = jnp.bfloat16
DEAD = 1e30
QUERY_STEP = np.array([0, 0, 1, 1, -1, -1], np.int32)
KEY_STEP = np.array(
    [[0, 0, 1, 1, -1, -1]] * 2 + [[0, 0, 1, 1, 2, 2]] * 2 + [[0, 0, -1, -1, -2, -2]] * 2, np.int32
)
VMEM_LIMIT = 40 * 1024 * 1024

NN = (((1,), (0,)), ((), ()))
NT = (((1,), (1,)), ((), ()))
TN = (((0,), (0,)), ((), ()))


def dot(a, b, dims, precision=None):
    return lax.dot_general(a, b, dims, precision=precision, preferred_element_type=F32)


def params():
    return pltpu.CompilerParams(
        vmem_limit_bytes=VMEM_LIMIT, dimension_semantics=("arbitrary",)
    )


def project_kernel(first, x_ref, gain_ref, w_ref, out_ref, normed):
    part = pl.program_id(0)

    @pl.when(part == 0)
    def _():
        inputs = x_ref[...].astype(F32)
        root_mean = jnp.sqrt(jnp.mean(inputs * inputs, axis=-1, keepdims=True) + 1e-05)
        normed[...] = (inputs * gain_ref[...] / root_mean).astype(BF16)

    rows = dot(normed[...], w_ref[0], NN).astype(BF16)
    scale = jnp.where(part + first == 0, 1.0 / math.sqrt(HD), 1.0)
    out_ref[0] = (rows.astype(F32) * scale).astype(BF16)


def project(tokens, gain, w_qkv, first):
    rows, width = tokens.shape
    parts, cols = 3 - first, w_qkv.shape[2]
    return pl.pallas_call(
        functools.partial(project_kernel, first),
        grid=(parts,),
        in_specs=[
            pl.BlockSpec((rows, width), lambda c: (0, 0)),
            pl.BlockSpec((1, width), lambda c: (0, 0)),
            pl.BlockSpec((1, width, cols), lambda c: (c + first, 0, 0)),
        ],
        out_specs=pl.BlockSpec((1, rows, cols), lambda c: (c, 0, 0)),
        out_shape=jax.ShapeDtypeStruct((parts, rows, cols), BF16),
        scratch_shapes=[pltpu.VMEM((rows, width), BF16)],
        compiler_params=params(),
        cost_estimate=pl.CostEstimate(
            flops=2 * rows * width * cols * parts,
            bytes_accessed=parts * width * cols * 2 + rows * width * 2,
            transcendentals=rows,
        ),
        name="project",
    )(tokens, gain, w_qkv)


def two_heads(tile):
    lane = lax.broadcasted_iota(jnp.int32, tile.shape, 1)
    zero = jnp.zeros_like(tile)
    return jnp.concatenate(
        [jnp.where(lane < HD, tile, zero), jnp.where(lane >= HD, tile, zero)], axis=0
    )


def fold_heads(pair_t):
    return jnp.concatenate([pair_t[:HD, :BLK], pair_t[HD:, BLK:]], axis=0)


def attend(bias_ref, row, key_rows, values_t, query_tile):
    scores = dot(key_rows, two_heads(query_tile), NT)
    blocks = [scores[k * BLK : (k + 1) * BLK] for k in range(6)]
    tops = [
        jnp.max(blocks[k], axis=0, keepdims=True) - bias_ref[row, k] for k in range(6)
    ]
    top = functools.reduce(jnp.maximum, tops)
    expo = [jnp.exp(blocks[k] - (top + bias_ref[row, k])) for k in range(6)]
    total = functools.reduce(jnp.add, [jnp.sum(e, axis=0, keepdims=True) for e in expo])
    inverse = 1.0 / total
    weight = jnp.concatenate([(e * inverse).astype(BF16) for e in expo], axis=0)
    attended_t = fold_heads(dot(values_t, weight, NN)).astype(BF16)
    return weight, attended_t


def own_kernel(
    pairs, bias_ref, own_ref, near_ref, far_ref, mix_ref, weight_ref, att_ref, keep_ref, send_ref, read
):
    pair = pl.program_id(0)
    keys = jnp.concatenate([own_ref[1], near_ref[1], far_ref[1]], axis=0)
    values_t = jnp.concatenate([own_ref[2], near_ref[2], far_ref[2]], axis=0).T

    @pl.when(pair == 0)
    def _():
        read[...] = jnp.zeros_like(read)

    for b in range(2):
        rows = slice(b * BLK, (b + 1) * BLK)
        weight, attended_t = attend(bias_ref, b, keys, values_t, own_ref[0, rows, :])
        weight_ref[0, b] = weight
        att_ref[0, b] = attended_t
        read[rows, :] += dot(attended_t, mix_ref[...], TN)

    @pl.when(pair == pairs - 1)
    def _():
        half = read.shape[1] // 2
        keep_ref[...] = read[:, :half]
        send_ref[...] = read[:, half:]


def side_kernel(bias_ref, own_ref, a1_ref, b1_ref, a2_ref, b2_ref, weight_ref, att_ref):
    own_rows = own_ref.shape[1]
    for side, (one, two) in enumerate(((a1_ref, a2_ref), (b1_ref, b2_ref))):
        keys = jnp.concatenate([own_ref[1], one[1], two[0]], axis=0)
        values_t = jnp.concatenate([own_ref[2], one[2], two[1]], axis=0).T
        for b in range(2):
            rows = slice(b * BLK, (b + 1) * BLK)
            at = 2 * side + b
            weight, attended_t = attend(bias_ref, 2 + at, keys, values_t, one[0, rows, :])
            weight_ref[0, at] = weight[:own_rows]
            att_ref[0, at] = attended_t


def back_kernel(
    pairs,
    core_ref,
    resid_a_ref,
    resid_b_ref,
    hot_ref,
    mix_ref,
    own_ref,
    a1_ref,
    b1_ref,
    own_weight_ref,
    own_att_ref,
    side_weight_ref,
    side_att_ref,
    w_ref,
    tokens_ref,
    gain_ref,
    keep_ref,
    send_ref,
    sum_ref,
    residual,
    total,
):
    pair = pl.program_id(0)

    @pl.when(pair == 0)
    def _():
        residual[...] = jnp.concatenate([resid_a_ref[...], resid_b_ref[...]], axis=1)
        total[...] = jnp.zeros_like(total)

    panel_grad = dot(
        residual[...], mix_ref[...].astype(F32), NT, lax.Precision.HIGHEST
    ).astype(BF16)
    out_grad = dot(hot_ref[...], panel_grad, NN)
    keys = jnp.concatenate([own_ref[1], a1_ref[1], b1_ref[1]], axis=0)
    values = jnp.concatenate([own_ref[2], a1_ref[2], b1_ref[2]], axis=0)
    keys_t = keys.T
    own_rows = own_ref.shape[1]
    grad_key = jnp.zeros((own_rows, PAIR), F32)
    grad_value = jnp.zeros((own_rows, PAIR), F32)
    grad_query = []
    for i in range(6):
        source = (own_ref, a1_ref, b1_ref)[i // 2]
        rows = slice((i % 2) * BLK, (i % 2 + 1) * BLK)
        grad_tile = out_grad[i * BLK : (i + 1) * BLK]
        attended_t = own_att_ref[0, i] if i < 2 else side_att_ref[0, i - 2]
        product = grad_tile.T * attended_t.astype(F32)
        delta = jnp.concatenate(
            [
                jnp.sum(product[:HD], axis=0, keepdims=True),
                jnp.sum(product[HD:], axis=0, keepdims=True),
            ],
            axis=1,
        )
        grad_pair = two_heads(grad_tile.astype(BF16))
        query_pair = two_heads(source[0, rows, :])
        if i < 2:
            weight = own_weight_ref[0, i]
            grad_weight = dot(values, grad_pair, NT)
        else:
            weight = side_weight_ref[0, i - 2]
            grad_weight = dot(values[:own_rows], grad_pair, NT)
        grad_score = (weight.astype(F32) * (grad_weight - delta)).astype(BF16)
        if i < 2:
            grad_query_t = fold_heads(dot(keys_t, grad_score, NN)) * (1.0 / math.sqrt(HD))
            grad_query.append(grad_query_t.T.astype(BF16))
        grad_key += dot(grad_score[:own_rows], query_pair, NN)
        grad_value += dot(weight[:own_rows], grad_pair, NN)
    grad_proj = (
        jnp.concatenate(grad_query, axis=0),
        grad_key.astype(BF16),
        grad_value.astype(BF16),
    )
    half = total.shape[2]
    for h in range(2):
        part = total[h]
        for c in range(3):
            part += dot(grad_proj[c], w_ref[c, h * half : (h + 1) * half, :], NT)
        total[h] = part

    @pl.when(pair == pairs - 1)
    def _():
        row_sum = jnp.zeros((own_rows, 1), F32)
        for h in range(2):
            cols = slice(h * half, (h + 1) * half)
            row_sum += jnp.sum(
                tokens_ref[:, cols].astype(F32) * gain_ref[:, cols] * total[h],
                axis=-1,
                keepdims=True,
            )
        core = core_ref[0]
        keep_ref[...] = total[core]
        high = row_sum.astype(BF16)
        low = (row_sum - high.astype(F32)).astype(BF16)
        send_ref[:, :half] = total[1 - core].astype(BF16)
        lane = lax.broadcasted_iota(jnp.int32, (own_rows, BLK), 1)
        send_ref[:, half:] = jnp.where(lane < HD, high.astype(F32), low.astype(F32)).astype(BF16)
        sum_ref[...] = jnp.broadcast_to(row_sum, sum_ref.shape)


def pair_spec(parts, rows):
    return pl.BlockSpec((parts, rows, PAIR), lambda p: (0, 0, p))


def whole_spec(shape):
    return pl.BlockSpec(shape, lambda p: (0,) * len(shape))


def lead_spec(shape):
    return pl.BlockSpec((1,) + shape, lambda p: (p,) + (0,) * len(shape))


SMEM_SPEC = pl.BlockSpec(memory_space=pltpu.SMEM)


def local(
    tokens, norm_gain, w_qkv, w_out, readout_weight, targets, key_blocks, list_len, voxel_panel
):
    tok_rows, width = tokens.shape
    cols = w_qkv.shape[2]
    pairs = cols // PAIR
    panels, readout = targets.shape
    half_read = readout // 2
    half_width = width // 2
    seq_count = lax.axis_size("seq")
    seq_index = lax.axis_index("seq")
    core = lax.axis_index("head")
    step = 2 * core - 1
    all_tokens = voxel_panel.shape[0]
    block_count = all_tokens // BLK
    per = tok_rows // BLK
    core_swap = [(0, 1), (1, 0)]

    def shifted(far):
        return [
            (2 * s, 2 * (s + far)) for s in range(seq_count - far)
        ] + [(2 * (s + far) + 1, 2 * s + 1) for s in range(seq_count - far)]

    a1_tokens = lax.ppermute(tokens, ("seq", "head"), shifted(1))
    a2_tokens = lax.ppermute(tokens, ("seq", "head"), shifted(2))
    b1_tokens = lax.ppermute(a1_tokens, "head", core_swap)
    b2_tokens = lax.ppermute(a2_tokens, "head", core_swap)

    gain = norm_gain.reshape(1, width)
    own = project(tokens, gain, w_qkv, 0)
    mix = jnp.dot(w_out, readout_weight, preferred_element_type=F32).astype(BF16)
    mix = jnp.where(core == 0, mix, jnp.roll(mix, half_read, axis=1))
    own_targets = lax.dynamic_slice_in_dim(targets, core * half_read, half_read, 1)

    panel_ids = voxel_panel[:, 0]
    panel_range = jnp.arange(panels, dtype=jnp.int32)
    hits = panel_range[:, None] == panel_ids[None, :]
    counts = jnp.sum(hits.astype(F32), axis=1, keepdims=True)

    def stretch_rows(array, offset, rows):
        stretch = seq_index + offset
        start = jnp.clip(stretch, 0, seq_count - 1) * rows
        return lax.dynamic_slice_in_dim(array, start, rows, 0)

    def inside(offset):
        stretch = seq_index + offset
        return (stretch >= 0) & (stretch < seq_count)

    offsets = (jnp.int32(0), step, -step)
    local_ids = jnp.concatenate(
        [
            jnp.where(inside(o), stretch_rows(panel_ids, o, tok_rows), -1)
            for o in offsets
        ]
    )
    hot = (local_ids[:, None] == panel_range[None, :]).astype(BF16)
    lists = jnp.concatenate([stretch_rows(key_blocks, o, per) for o in offsets])
    lengths = jnp.concatenate([stretch_rows(list_len, o, per) for o in offsets])
    outside = jnp.concatenate(
        [jnp.broadcast_to(~inside(o), (per,)) for o in offsets]
    )
    parity = jnp.asarray(np.tile(np.arange(2, dtype=np.int32), 3))
    candidates = (seq_index + step * jnp.asarray(KEY_STEP)) * per + parity[None, :]
    slot_live = jnp.arange(LIST)[None, :] < lengths[:, None]
    live = jnp.any(
        (lists[:, None, :] == candidates[:, :, None]) & slot_live[:, None, :], axis=-1
    )
    bias = jnp.where(live | outside[:, None], 0.0, DEAD).astype(F32)

    a1 = project(a1_tokens, gain, w_qkv, 0)
    b1 = project(b1_tokens, gain, w_qkv, 0)

    own_weight, own_att, read_keep, read_send = pl.pallas_call(
        functools.partial(own_kernel, pairs),
        grid=(pairs,),
        in_specs=[SMEM_SPEC]
        + [pair_spec(3, tok_rows)] * 3
        + [pl.BlockSpec((PAIR, readout), lambda p: (p, 0))],
        out_specs=[
            lead_spec((2, 3 * tok_rows, 2 * BLK)),
            lead_spec((2, PAIR, BLK)),
            whole_spec((tok_rows, half_read)),
            whole_spec((tok_rows, half_read)),
        ],
        out_shape=[
            jax.ShapeDtypeStruct((pairs, 2, 3 * tok_rows, 2 * BLK), BF16),
            jax.ShapeDtypeStruct((pairs, 2, PAIR, BLK), BF16),
            jax.ShapeDtypeStruct((tok_rows, half_read), F32),
            jax.ShapeDtypeStruct((tok_rows, half_read), F32),
        ],
        scratch_shapes=[pltpu.VMEM((tok_rows, readout), F32)],
        compiler_params=params(),
        name="attend_own",
    )(bias, own, a1, b1, mix)

    read_half = read_keep + lax.ppermute(read_send, "head", core_swap)
    read_rows = read_half.astype(BF16)
    all_rows = lax.all_to_all(
        jnp.broadcast_to(read_rows[None], (seq_count, tok_rows, half_read)), "seq", 0, 0
    ).reshape(all_tokens, half_read)

    a2 = project(a2_tokens, gain, w_qkv, 1)
    b2 = project(b2_tokens, gain, w_qkv, 1)
    side_weight, side_att = pl.pallas_call(
        side_kernel,
        grid=(pairs,),
        in_specs=[SMEM_SPEC] + [pair_spec(3, tok_rows)] * 3 + [pair_spec(2, tok_rows)] * 2,
        out_specs=[lead_spec((4, tok_rows, 2 * BLK)), lead_spec((4, PAIR, BLK))],
        out_shape=[
            jax.ShapeDtypeStruct((pairs, 4, tok_rows, 2 * BLK), BF16),
            jax.ShapeDtypeStruct((pairs, 4, PAIR, BLK), BF16),
        ],
        compiler_params=params(),
        cost_estimate=pl.CostEstimate(
            flops=pairs * 4 * 2 * 2 * 768 * 256 * 128,
            bytes_accessed=8 * 2**20,
            transcendentals=pairs * 4 * 768 * 256,
        ),
        name="attend_sides",
    )(bias, own, a1, b1, a2, b2)

    if panels * all_tokens <= 2**22:
        sums = jnp.dot(hits.astype(BF16), all_rows, preferred_element_type=F32)
    else:
        sums = jax.ops.segment_sum(all_rows.astype(F32), panel_ids, num_segments=panels)
    resid_a = sums / counts - own_targets
    resid_b = lax.ppermute(resid_a, "head", core_swap)

    keep, send, row_sum = pl.pallas_call(
        functools.partial(back_kernel, pairs),
        grid=(pairs,),
        in_specs=[
            SMEM_SPEC,
            whole_spec((panels, half_read)),
            whole_spec((panels, half_read)),
            whole_spec((3 * tok_rows, panels)),
            pl.BlockSpec((PAIR, readout), lambda p: (p, 0)),
            pair_spec(3, tok_rows),
            pair_spec(3, tok_rows),
            pair_spec(3, tok_rows),
            lead_spec((2, 3 * tok_rows, 2 * BLK)),
            lead_spec((2, PAIR, BLK)),
            lead_spec((4, tok_rows, 2 * BLK)),
            lead_spec((4, PAIR, BLK)),
            pair_spec(3, width),
            whole_spec((tok_rows, width)),
            whole_spec((1, width)),
        ],
        out_specs=[
            whole_spec((tok_rows, half_width)),
            whole_spec((tok_rows, half_width + BLK)),
            whole_spec((tok_rows, BLK)),
        ],
        out_shape=[
            jax.ShapeDtypeStruct((tok_rows, half_width), F32),
            jax.ShapeDtypeStruct((tok_rows, half_width + BLK), BF16),
            jax.ShapeDtypeStruct((tok_rows, BLK), F32),
        ],
        scratch_shapes=[
            pltpu.VMEM((panels, readout), F32),
            pltpu.VMEM((2, tok_rows, half_width), F32),
        ],
        compiler_params=params(),
        name="back",
    )(
        core.astype(jnp.int32).reshape(1),
        resid_a,
        resid_b,
        hot,
        mix,
        own,
        a1,
        b1,
        own_weight,
        own_att,
        side_weight,
        side_att,
        w_qkv,
        tokens,
        gain,
    )
    other = lax.ppermute(send, "head", core_swap)
    loss_mean = (
        0.5
        * (jnp.sum(counts * resid_a * resid_a) + jnp.sum(counts * resid_b * resid_b))
        / (all_tokens * readout)
    )
    inputs = tokens.astype(F32)
    root_mean = jnp.sqrt(jnp.mean(inputs * inputs, axis=-1, keepdims=True) + 1e-05)
    half_inputs = lax.dynamic_slice_in_dim(tokens, core * half_width, half_width, 1).astype(F32)
    half_gain = lax.dynamic_slice_in_dim(gain, core * half_width, half_width, 1)
    grad_normed = keep + other[:, :half_width].astype(F32)
    other_sum = other[:, half_width : half_width + 1].astype(F32) + other[:, -1:].astype(F32)
    full_sum = row_sum[:, :1] + other_sum
    gradient = half_gain * grad_normed / root_mean - half_inputs * full_sum / (
        width * root_mean**3
    )
    return (gradient, loss_mean.reshape(1))


def solution(mesh):
    return jax.shard_map(
        local,
        mesh=mesh,
        in_specs=(
            P(("groups", "seq"), None),
            P(),
            P(None, None, "head"),
            P("head", None),
            P(),
            P("groups", None),
            P("groups", None),
            P("groups"),
            P("groups", None),
        ),
        out_specs=(P(("groups", "seq"), "head"), P("groups")),
        check_vma=False,
    )
```

```python
import functools
import math

import jax
import jax.numpy as jnp
import numpy as np
from jax import lax
from jax.experimental import pallas as pl
from jax.experimental.pallas import tpu as pltpu
from jax.sharding import PartitionSpec as P

HD = 64
BLK = 128
LIST = 4
PAIR = 2 * HD
GROUP = 2
F32 = jnp.float32
BF16 = jnp.bfloat16
DEAD = 1e30
SCALE = 1.0 / math.sqrt(HD)
KEY_STEP = np.array([[0, 1, -1], [0, 1, 2], [0, -1, -2]], np.int32)
MIB = 1024 * 1024

NN = (((1,), (0,)), ((), ()))
NT = (((1,), (1,)), ((), ()))
TN = (((0,), (0,)), ((), ()))


def dot(a, b, dims, precision=None):
    return lax.dot_general(a, b, dims, precision=precision, preferred_element_type=F32)


def params(mib):
    return pltpu.CompilerParams(
        vmem_limit_bytes=mib * MIB, dimension_semantics=("arbitrary",)
    )


def inverse_root(inputs):
    return 1.0 / jnp.sqrt(jnp.mean(inputs * inputs, axis=-1, keepdims=True) + 1e-05)


def project_kernel(first, x_ref, gain_ref, w_ref, out_ref, normed):
    part = pl.program_id(0)

    @pl.when(part == 0)
    def _():
        inputs = x_ref[...].astype(F32)
        normed[...] = (inputs * gain_ref[...] * inverse_root(inputs)).astype(BF16)

    rows = dot(normed[...], w_ref[0], NN).astype(BF16)
    scale = jnp.where(part + first == 0, SCALE, 1.0)
    out_ref[0] = (rows.astype(F32) * scale).astype(BF16)


def project(tokens, gain, w_qkv, first):
    rows, width = tokens.shape
    parts, cols = 3 - first, w_qkv.shape[2]
    return pl.pallas_call(
        functools.partial(project_kernel, first),
        grid=(parts,),
        in_specs=[
            pl.BlockSpec((rows, width), lambda c: (0, 0)),
            pl.BlockSpec((1, width), lambda c: (0, 0)),
            pl.BlockSpec((1, width, cols), lambda c: (c + first, 0, 0)),
        ],
        out_specs=pl.BlockSpec((1, rows, cols), lambda c: (c, 0, 0)),
        out_shape=jax.ShapeDtypeStruct((parts, rows, cols), BF16),
        scratch_shapes=[pltpu.VMEM((rows, width), BF16)],
        compiler_params=params(12),
        cost_estimate=pl.CostEstimate(
            flops=2 * rows * width * cols * parts,
            bytes_accessed=parts * width * cols * 2 + rows * width * 2,
            transcendentals=rows,
        ),
        name="project",
    )(tokens, gain, w_qkv)


def pair_cols(p):
    return slice(p * PAIR, (p + 1) * PAIR)


def two_heads(tile):
    lane = lax.broadcasted_iota(jnp.int32, tile.shape, 1)
    zero = jnp.zeros_like(tile)
    return jnp.concatenate(
        [jnp.where(lane < HD, tile, zero), jnp.where(lane >= HD, tile, zero)], axis=0
    )


def fold_heads(pair_t):
    half = pair_t.shape[1] // 2
    return jnp.concatenate([pair_t[:HD, :half], pair_t[HD:, half:]], axis=0)


def soften(bias_ref, stretch, scores):
    count = scores.shape[0] // BLK
    blocks = [scores[k * BLK : (k + 1) * BLK] for k in range(count)]
    biases = [bias_ref[stretch, k : k + 1, :] for k in range(count)]
    tops = [jnp.max(b, axis=0, keepdims=True) - d for b, d in zip(blocks, biases)]
    top = functools.reduce(jnp.maximum, tops)
    expo = [jnp.exp(b - (top + d)) for b, d in zip(blocks, biases)]
    total = functools.reduce(jnp.add, [jnp.sum(e, axis=0, keepdims=True) for e in expo])
    inverse = 1.0 / total
    return jnp.concatenate([(e * inverse).astype(BF16) for e in expo], axis=0)


def own_kernel(
    steps, bias_ref, own_ref, a1_ref, b1_ref, mix_ref, weight_ref, att_ref, keep_ref, send_ref, read
):
    step = pl.program_id(0)

    @pl.when(step == 0)
    def _():
        read[...] = jnp.zeros_like(read)

    stretches = (own_ref, a1_ref, b1_ref)
    scores = []
    for p in range(GROUP):
        keys = jnp.concatenate([r[1, :, pair_cols(p)] for r in stretches], axis=0)
        scores.append(dot(keys, two_heads(own_ref[0, :, pair_cols(p)]), NT))
    weights = []
    for p in range(GROUP):
        weights.append(soften(bias_ref, 0, scores[p]))
        weight_ref[p] = weights[p]
    attended = []
    for p in range(GROUP):
        values = jnp.concatenate([r[2, :, pair_cols(p)] for r in stretches], axis=0)
        attended.append(fold_heads(dot(values, weights[p], TN)).astype(BF16))
        att_ref[p] = attended[p]
    read[...] += dot(mix_ref[...], jnp.concatenate(attended, axis=0), NN)

    @pl.when(step == steps - 1)
    def _():
        half = read.shape[0] // 2
        keep_ref[...] = read[:half]
        send_ref[...] = read[half:]


def side_kernel(bias_ref, own_ref, a1_ref, b1_ref, a2_ref, b2_ref, weight_ref, att_ref):
    own_rows = own_ref.shape[1]
    jobs = [(p, side) for p in range(GROUP) for side in range(2)]
    near, far = (a1_ref, b1_ref), (a2_ref, b2_ref)

    def stack(p, side, part):
        cols = pair_cols(p)
        return jnp.concatenate(
            [own_ref[part, :, cols], near[side][part, :, cols], far[side][part - 1, :, cols]],
            axis=0,
        )

    scores = [
        dot(stack(p, side, 1), two_heads(near[side][0, :, pair_cols(p)]), NT) for p, side in jobs
    ]
    weights = []
    for (p, side), score in zip(jobs, scores):
        weights.append(soften(bias_ref, 1 + side, score))
        weight_ref[p, side] = weights[-1][:own_rows]
    for (p, side), weight in zip(jobs, weights):
        att_ref[p, side] = fold_heads(dot(stack(p, side, 2), weight, TN)).astype(BF16)


def spread_kernel(keep_ref, got_ref, out_ref):
    rows = (keep_ref[...] + got_ref[...]).astype(BF16)
    for s in range(out_ref.shape[0]):
        out_ref[s] = rows


def pool_kernel(steps, rows_ref, ids_ref, counts_ref, targets_ref, out_ref, sums):
    step = pl.program_id(0)
    panels = out_ref.shape[1]
    count, _, tok_rows = rows_ref.shape

    @pl.when(step == 0)
    def _():
        sums[...] = jnp.zeros_like(sums)

    panel = lax.broadcasted_iota(jnp.int32, (panels, count * tok_rows), 0)
    hits = jnp.where(panel == ids_ref[...], 1.0, 0.0).astype(BF16)
    rows = jnp.concatenate([rows_ref[s] for s in range(count)], axis=1)
    sums[...] += dot(rows, hits, NT)

    @pl.when(step == steps - 1)
    def _():
        out_ref[...] = sums[...] / counts_ref[...] - targets_ref[...]


def back_kernel(
    steps,
    core_ref,
    resid_a_ref,
    resid_b_ref,
    counts_ref,
    hot_ref,
    mix_ref,
    own_ref,
    a1_ref,
    b1_ref,
    own_weight_ref,
    own_att_ref,
    side_weight_ref,
    side_att_ref,
    w_ref,
    tokens_ref,
    gain_ref,
    keep_ref,
    send_ref,
    stat_ref,
    loss_ref,
    residual,
    total,
):
    step = pl.program_id(0)
    half_read = resid_a_ref.shape[0]
    own_rows = own_ref.shape[1]

    @pl.when(step == 0)
    def _():
        residual[:half_read] = resid_a_ref[...]
        residual[half_read:] = resid_b_ref[...]
        total[...] = jnp.zeros_like(total)
        loss_ref[...] = jnp.broadcast_to(
            jnp.sum(counts_ref[...] * residual[...] * residual[...], keepdims=True),
            loss_ref.shape,
        )

    panel_grad = dot(
        residual[...], mix_ref[...].astype(F32), TN, lax.Precision.HIGHEST
    ).astype(BF16)
    out_grad = dot(hot_ref[...], panel_grad, NN)
    stretches = (own_ref, a1_ref, b1_ref)
    grads, weights, deltas, changes = [], [], [], []
    for p in range(GROUP):
        values = jnp.concatenate([r[2, :, pair_cols(p)] for r in stretches], axis=0)
        grads.append([])
        changes.append([])
        for t in range(3):
            grad_tile = out_grad[t * own_rows : (t + 1) * own_rows, pair_cols(p)]
            grads[p].append(two_heads(grad_tile.astype(BF16)))
            seen = values if t == 0 else values[:own_rows]
            changes[p].append(dot(seen, grads[p][t], NT))
    for p in range(GROUP):
        deltas.append([])
        for t in range(3):
            grad_tile = out_grad[t * own_rows : (t + 1) * own_rows, pair_cols(p)]
            attended = own_att_ref[p] if t == 0 else side_att_ref[p, t - 1]
            product = grad_tile.T * attended.astype(F32)
            deltas[p].append(
                jnp.concatenate(
                    [
                        jnp.sum(product[:HD], axis=0, keepdims=True),
                        jnp.sum(product[HD:], axis=0, keepdims=True),
                    ],
                    axis=1,
                )
            )
    scores = []
    for p in range(GROUP):
        weights.append([own_weight_ref[p], side_weight_ref[p, 0], side_weight_ref[p, 1]])
        scores.append(
            [
                (weights[p][t].astype(F32) * (changes[p][t] - deltas[p][t])).astype(BF16)
                for t in range(3)
            ]
        )
    grad_proj = [[], [], []]
    for p in range(GROUP):
        keys = jnp.concatenate([r[1, :, pair_cols(p)] for r in stretches], axis=0)
        grad_query = fold_heads(dot(keys, scores[p][0], TN)) * SCALE
        grad_proj[0].append(grad_query.T.astype(BF16))
        queries = jnp.concatenate([two_heads(r[0, :, pair_cols(p)]) for r in stretches], axis=0)
        own_scores = jnp.concatenate([s[:own_rows] for s in scores[p]], axis=1)
        grad_proj[1].append(dot(own_scores, queries, NN).astype(BF16))
        own_weights = jnp.concatenate([w[:own_rows] for w in weights[p]], axis=1)
        grad_proj[2].append(dot(own_weights, jnp.concatenate(grads[p], axis=0), NN).astype(BF16))
    flat = jnp.concatenate([g for part in grad_proj for g in part], axis=1)
    half = total.shape[2]
    for h in range(2):
        w_part = jnp.concatenate([w_ref[c, h * half : (h + 1) * half, :] for c in range(3)], axis=1)
        total[h] += dot(flat, w_part, NT)

    @pl.when(step == steps - 1)
    def _():
        inputs = tokens_ref[...].astype(F32)
        scaled = inputs * gain_ref[...]
        row_sum = jnp.zeros((own_rows, 1), F32)
        for h in range(2):
            row_sum += jnp.sum(
                scaled[:, h * half : (h + 1) * half] * total[h], axis=-1, keepdims=True
            )
        core = core_ref[0]
        keep_ref[...] = total[core]
        high = row_sum.astype(BF16).astype(F32)
        lane = lax.broadcasted_iota(jnp.int32, (own_rows, BLK), 1)
        send_ref[:, :half] = total[1 - core].astype(BF16)
        send_ref[:, half:] = jnp.where(lane < HD, high, row_sum - high).astype(BF16)
        stat_ref[...] = jnp.where(lane < HD, row_sum, inverse_root(inputs))


def final_kernel(core_ref, keep_ref, got_ref, stat_ref, tokens_ref, gain_ref, out_ref):
    half = keep_ref.shape[1]
    cols = pl.ds(pl.multiple_of(core_ref[0] * half, half), half)
    got_sum = got_ref[:, half : half + 1].astype(F32) + got_ref[:, half + HD : half + HD + 1].astype(F32)
    row_sum = stat_ref[:, :1] + got_sum
    inverse = stat_ref[:, HD : HD + 1]
    grad_normed = keep_ref[...] + got_ref[:, :half].astype(F32)
    shrink = row_sum * (inverse * inverse * inverse) * (0.5 / half)
    out_ref[...] = (
        gain_ref[:, cols] * grad_normed * inverse - tokens_ref[:, cols].astype(F32) * shrink
    )


def pair_spec(parts, rows):
    return pl.BlockSpec((parts, rows, GROUP * PAIR), lambda p: (0, 0, p))


def whole_spec(shape):
    return pl.BlockSpec(shape, lambda p: (0,) * len(shape))


def lead_spec(shape):
    return pl.BlockSpec((GROUP,) + shape, lambda p: (p,) + (0,) * len(shape))


SMEM_SPEC = pl.BlockSpec(memory_space=pltpu.SMEM)


def local(
    tokens, norm_gain, w_qkv, w_out, readout_weight, targets, key_blocks, list_len, voxel_panel
):
    tok_rows, width = tokens.shape
    cols = w_qkv.shape[2]
    pairs = cols // PAIR
    steps = pairs // GROUP
    panels, readout = targets.shape
    half_read = readout // 2
    half_width = width // 2
    seq_count = lax.axis_size("seq")
    seq_index = lax.axis_index("seq")
    core = lax.axis_index("head")
    side_step = 2 * core - 1
    all_tokens = voxel_panel.shape[0]
    per = tok_rows // BLK
    core_swap = [(0, 1), (1, 0)]

    def shifted(far):
        return [
            (2 * s, 2 * (s + far)) for s in range(seq_count - far)
        ] + [(2 * (s + far) + 1, 2 * s + 1) for s in range(seq_count - far)]

    a1_tokens = lax.ppermute(tokens, ("seq", "head"), shifted(1))
    a2_tokens = lax.ppermute(tokens, ("seq", "head"), shifted(2))

    gain = norm_gain.reshape(1, width)
    own = project(tokens, gain, w_qkv, 0)
    mix = jnp.dot(
        readout_weight.T, w_out.T, preferred_element_type=F32
    ).astype(BF16)
    mix = jnp.where(core == 0, mix, jnp.roll(mix, half_read, axis=0))
    own_targets = lax.dynamic_slice_in_dim(targets, core * half_read, half_read, 1).T

    panel_ids = voxel_panel[:, 0]
    panel_range = jnp.arange(panels, dtype=jnp.int32)
    counts = jnp.sum(
        (panel_range[:, None] == panel_ids[None, :]).astype(F32), axis=1
    ).reshape(1, panels)

    def stretch_rows(array, offset, rows):
        stretch = seq_index + offset
        start = jnp.clip(stretch, 0, seq_count - 1) * rows
        return lax.dynamic_slice_in_dim(array, start, rows, 0)

    def inside(offset):
        stretch = seq_index + offset
        return (stretch >= 0) & (stretch < seq_count)

    offsets = (jnp.int32(0), side_step, -side_step)
    local_ids = jnp.concatenate(
        [jnp.where(inside(o), stretch_rows(panel_ids, o, tok_rows), -1) for o in offsets]
    )
    hot = (local_ids[:, None] == panel_range[None, :]).astype(BF16)
    lists = jnp.stack([stretch_rows(key_blocks, o, per) for o in offsets])
    lengths = jnp.stack([stretch_rows(list_len, o, per) for o in offsets])
    outside = jnp.stack([~inside(o) for o in offsets])
    candidates = (
        (seq_index + side_step * jnp.asarray(KEY_STEP))[:, :, None] * per
        + jnp.arange(per, dtype=jnp.int32)
    ).reshape(3, 3 * per)
    slot_live = jnp.arange(LIST) < lengths[..., None]
    live = jnp.any(
        (lists[:, None] == candidates[:, :, None, None]) & slot_live[:, None], axis=-1
    )
    bias = jnp.where(live | outside[:, None, None], 0.0, DEAD).astype(F32)
    bias = jnp.tile(jnp.repeat(bias, BLK, axis=2), (1, 1, 2))

    a2 = project(a2_tokens, gain, w_qkv, 1)
    b2_tokens = lax.ppermute(a2_tokens, "head", core_swap)
    b2 = project(b2_tokens, gain, w_qkv, 1)

    a1_tokens, own, a2, b2, mix, own_targets, counts, hot, bias = lax.optimization_barrier(
        (a1_tokens, own, a2, b2, mix, own_targets, counts, hot, bias)
    )
    b1_tokens = lax.ppermute(a1_tokens, "head", core_swap)
    a1 = project(a1_tokens, gain, w_qkv, 0)
    b1 = project(b1_tokens, gain, w_qkv, 0)

    bias_spec = whole_spec(bias.shape)
    mix_spec = pl.BlockSpec((readout, GROUP * PAIR), lambda p: (0, p))
    own_weight, own_att, read_keep, read_send = pl.pallas_call(
        functools.partial(own_kernel, steps),
        grid=(steps,),
        in_specs=[bias_spec] + [pair_spec(3, tok_rows)] * 3 + [mix_spec],
        out_specs=[
            lead_spec((3 * tok_rows, 2 * tok_rows)),
            lead_spec((PAIR, tok_rows)),
            whole_spec((half_read, tok_rows)),
            whole_spec((half_read, tok_rows)),
        ],
        out_shape=[
            jax.ShapeDtypeStruct((pairs, 3 * tok_rows, 2 * tok_rows), BF16),
            jax.ShapeDtypeStruct((pairs, PAIR, tok_rows), BF16),
            jax.ShapeDtypeStruct((half_read, tok_rows), F32),
            jax.ShapeDtypeStruct((half_read, tok_rows), F32),
        ],
        scratch_shapes=[pltpu.VMEM((readout, tok_rows), F32)],
        compiler_params=params(24),
        name="attend_own",
    )(bias, own, a1, b1, mix)

    read_got = lax.ppermute(read_send, "head", core_swap)
    spread = pl.pallas_call(
        spread_kernel,
        out_shape=jax.ShapeDtypeStruct((seq_count, half_read, tok_rows), BF16),
        compiler_params=pltpu.CompilerParams(vmem_limit_bytes=8 * MIB),
        name="spread",
    )(read_keep, read_got)
    all_rows = lax.all_to_all(spread, "seq", 0, 0)

    side_weight, side_att = pl.pallas_call(
        side_kernel,
        grid=(steps,),
        in_specs=[bias_spec] + [pair_spec(3, tok_rows)] * 3 + [pair_spec(2, tok_rows)] * 2,
        out_specs=[lead_spec((2, tok_rows, 2 * tok_rows)), lead_spec((2, PAIR, tok_rows))],
        out_shape=[
            jax.ShapeDtypeStruct((pairs, 2, tok_rows, 2 * tok_rows), BF16),
            jax.ShapeDtypeStruct((pairs, 2, PAIR, tok_rows), BF16),
        ],
        compiler_params=params(28),
        cost_estimate=pl.CostEstimate(
            flops=pairs * 4 * 2 * 2 * 768 * 256 * 128,
            bytes_accessed=8 * MIB,
            transcendentals=pairs * 4 * 768 * 256,
        ),
        name="attend_sides",
    )(bias, own, a1, b1, a2, b2)
    all_rows, side_weight, side_att = lax.optimization_barrier((all_rows, side_weight, side_att))

    batch = min(seq_count, 8)
    pool_steps = seq_count // batch
    resid_a = pl.pallas_call(
        functools.partial(pool_kernel, pool_steps),
        grid=(pool_steps,),
        in_specs=[
            pl.BlockSpec((batch, half_read, tok_rows), lambda s: (s, 0, 0)),
            pl.BlockSpec((1, batch * tok_rows), lambda s: (0, s)),
            whole_spec((1, panels)),
            whole_spec((half_read, panels)),
        ],
        out_specs=whole_spec((half_read, panels)),
        out_shape=jax.ShapeDtypeStruct((half_read, panels), F32),
        scratch_shapes=[pltpu.VMEM((half_read, panels), F32)],
        compiler_params=params(12 + panels // 64),
        name="pool",
    )(all_rows, voxel_panel.reshape(1, all_tokens), counts, own_targets)
    resid_b = lax.ppermute(resid_a, "head", core_swap)

    core_index = core.astype(jnp.int32).reshape(1)
    keep, send, stats, loss = pl.pallas_call(
        functools.partial(back_kernel, steps),
        grid=(steps,),
        in_specs=[
            SMEM_SPEC,
            whole_spec((half_read, panels)),
            whole_spec((half_read, panels)),
            whole_spec((1, panels)),
            whole_spec((3 * tok_rows, panels)),
            mix_spec,
            pair_spec(3, tok_rows),
            pair_spec(3, tok_rows),
            pair_spec(3, tok_rows),
            lead_spec((3 * tok_rows, 2 * tok_rows)),
            lead_spec((PAIR, tok_rows)),
            lead_spec((2, tok_rows, 2 * tok_rows)),
            lead_spec((2, PAIR, tok_rows)),
            pair_spec(3, width),
            whole_spec((tok_rows, width)),
            whole_spec((1, width)),
        ],
        out_specs=[
            whole_spec((tok_rows, half_width)),
            whole_spec((tok_rows, half_width + BLK)),
            whole_spec((tok_rows, BLK)),
            whole_spec((1, BLK)),
        ],
        out_shape=[
            jax.ShapeDtypeStruct((tok_rows, half_width), F32),
            jax.ShapeDtypeStruct((tok_rows, half_width + BLK), BF16),
            jax.ShapeDtypeStruct((tok_rows, BLK), F32),
            jax.ShapeDtypeStruct((1, BLK), F32),
        ],
        scratch_shapes=[
            pltpu.VMEM((readout, panels), F32),
            pltpu.VMEM((2, tok_rows, half_width), F32),
        ],
        compiler_params=params(30 + panels // 128),
        name="back",
    )(
        core_index,
        resid_a,
        resid_b,
        counts,
        hot,
        mix,
        own,
        a1,
        b1,
        own_weight,
        own_att,
        side_weight,
        side_att,
        w_qkv,
        tokens,
        gain,
    )
    got = lax.ppermute(send, "head", core_swap)
    loss_mean = 0.5 * loss[0, :1] / (all_tokens * readout)
    gradient = pl.pallas_call(
        final_kernel,
        in_specs=[SMEM_SPEC] + [pl.BlockSpec(memory_space=pltpu.VMEM)] * 5,
        out_shape=jax.ShapeDtypeStruct((tok_rows, half_width), F32),
        compiler_params=pltpu.CompilerParams(vmem_limit_bytes=8 * MIB),
        name="final",
    )(core_index, keep, got, stats, tokens, gain)
    return (gradient, loss_mean)


def solution(mesh):
    return jax.shard_map(
        local,
        mesh=mesh,
        in_specs=(
            P(("groups", "seq"), None),
            P(),
            P(None, None, "head"),
            P("head", None),
            P(),
            P("groups", None),
            P("groups", None),
            P("groups"),
            P("groups", None),
        ),
        out_specs=(P(("groups", "seq"), "head"), P("groups")),
        check_vma=False,
    )
```

```python
import functools
import math

import jax
import jax.numpy as jnp
import numpy as np
from jax import lax
from jax.experimental import pallas as pl
from jax.experimental.pallas import tpu as pltpu
from jax.sharding import PartitionSpec as P

HD = 64
BLK = 128
LIST = 4
PAIR = 2 * HD
GROUP = 2
F32 = jnp.float32
BF16 = jnp.bfloat16
DEAD = 1e30
SCALE = 1.0 / math.sqrt(HD)
KEY_STEP = np.array([[0, 1, -1], [0, 1, 2], [0, -1, -2]], np.int32)
MIB = 1024 * 1024

NN = (((1,), (0,)), ((), ()))
NT = (((1,), (1,)), ((), ()))
TN = (((0,), (0,)), ((), ()))


def dot(a, b, dims, precision=None):
    return lax.dot_general(a, b, dims, precision=precision, preferred_element_type=F32)


def params(*semantics, mib=52):
    return pltpu.CompilerParams(vmem_limit_bytes=mib * MIB, dimension_semantics=semantics or None)


def inverse_root(inputs):
    return 1.0 / jnp.sqrt(jnp.mean(inputs * inputs, axis=-1, keepdims=True) + 1e-05)


def normalise(x_ref, gain_ref):
    inputs = x_ref[...].astype(F32)
    return (inputs * gain_ref[...] * inverse_root(inputs)).astype(BF16)


def project_rows(normed, w_part, part):
    rows = dot(normed, w_part, NN).astype(BF16)
    scale = jnp.where(part == 0, SCALE, 1.0)
    return (rows.astype(F32) * scale).astype(BF16)


def first_kernel(
    place_ref, lists_ref, lengths_ref, ids_ref, w_out_ref, read_ref, targets_ref, x_ref, gain_ref, w_ref,
    bias_ref, hot_ref, mix_ref, own_targets_ref, own_ref, flipped, normed,
):
    part = pl.program_id(0)

    @pl.when(part == 0)
    def _():
        normed[...] = normalise(x_ref, gain_ref)

    own_ref[0] = project_rows(normed[...], w_ref[0], part)

    @pl.when(part == 0)
    def _():
        prepare(
            place_ref, lists_ref, lengths_ref, ids_ref, w_out_ref, read_ref, targets_ref,
            bias_ref, hot_ref, mix_ref, own_targets_ref, flipped,
        )


def prepare(
    place_ref, lists_ref, lengths_ref, ids_ref, w_out_ref, read_ref, targets_ref,
    bias_ref, hot_ref, mix_ref, own_targets_ref, flipped,
):
    seq_index, core, seq_count = place_ref[0], place_ref[1], place_ref[2]
    side = 2 * core - 1
    half_read = own_targets_ref.shape[0]
    panels, tok_rows = hot_ref.shape[0], hot_ref.shape[1] // 3
    per = tok_rows // BLK
    mix = dot(w_out_ref[...], read_ref[...], NN).T
    flip = jnp.concatenate([mix[half_read:], mix[:half_read]], axis=0)
    mix_ref[...] = jnp.where(core == 0, mix, flip).astype(BF16)
    flipped[...] = targets_ref[...].T
    own_targets_ref[...] = flipped[pl.ds(pl.multiple_of(core * half_read, half_read), half_read), :]
    panel = lax.broadcasted_iota(jnp.int32, (panels, tok_rows), 0)
    column = lax.broadcasted_iota(jnp.int32, (1, 2 * tok_rows), 1)
    for t, move in enumerate((0, 1, -1)):
        stretch = seq_index + side * move
        inside = (stretch >= 0) & (stretch < seq_count)
        stretch = jnp.clip(stretch, 0, seq_count - 1)
        ids = ids_ref[:, pl.ds(pl.multiple_of(stretch * tok_rows, tok_rows), tok_rows)]
        hits = (panel == ids) & inside
        hot_ref[:, t * tok_rows : (t + 1) * tok_rows] = jnp.where(hits, 1.0, 0.0).astype(BF16)
        for k in range(3 * per):
            key_block = (seq_index + side * int(KEY_STEP[t, k // per])) * per + k % per
            row = jnp.zeros((1, 2 * tok_rows), F32)
            for b in range(per):
                query_block = stretch * per + b
                live = jnp.logical_not(inside)
                for j in range(LIST):
                    live = live | (
                        (lists_ref[j, query_block] == key_block) & (j < lengths_ref[query_block])
                    )
                off = jnp.where(live, 0.0, DEAD)
                row = jnp.where((column // BLK) % per == b, off, row)
            bias_ref[t, k : k + 1, :] = row


def far_kernel(a2_ref, b2_top_ref, b2_low_ref, gain_ref, w_ref, out_a_ref, out_b_ref, normed):
    rows = a2_ref.shape[0]
    piece = b2_top_ref.shape[0]

    @pl.when(pl.program_id(0) == 0)
    def _():
        normed[:rows] = normalise(a2_ref, gain_ref)
        normed[rows : rows + piece] = normalise(b2_top_ref, gain_ref)
        normed[rows + piece :] = normalise(b2_low_ref, gain_ref)

    both = dot(normed[...], w_ref[0], NN).astype(BF16)
    out_a_ref[0] = both[:rows]
    out_b_ref[0] = both[rows:]


def pair_cols(p):
    return slice(p * PAIR, (p + 1) * PAIR)


def two_heads(tile):
    lane = lax.broadcasted_iota(jnp.int32, tile.shape, 1)
    zero = jnp.zeros_like(tile)
    return jnp.concatenate(
        [jnp.where(lane < HD, tile, zero), jnp.where(lane >= HD, tile, zero)], axis=0
    )


def fold_heads(pair_t):
    half = pair_t.shape[1] // 2
    return jnp.concatenate([pair_t[:HD, :half], pair_t[HD:, half:]], axis=0)


def soften(bias_ref, stretch, scores):
    count = scores.shape[0] // BLK
    blocks = [scores[k * BLK : (k + 1) * BLK] for k in range(count)]
    biases = [bias_ref[stretch, k : k + 1, :] for k in range(count)]
    tops = [jnp.max(b, axis=0, keepdims=True) - d for b, d in zip(blocks, biases)]
    top = functools.reduce(jnp.maximum, tops)
    expo = [jnp.exp(b - (top + d)) for b, d in zip(blocks, biases)]
    total = functools.reduce(jnp.add, [jnp.sum(e, axis=0, keepdims=True) for e in expo])
    inverse = 1.0 / total
    return jnp.concatenate([(e * inverse).astype(BF16) for e in expo], axis=0)


def near_kernel(
    steps, bias_ref, own_ref, mix_ref, a1x_ref, b1x_ref, gain_ref, w_ref,
    a1_ref, b1_ref, weight_ref, att_ref, keep_ref, send_ref, normed, read,
):
    step = pl.program_id(0)
    rows = own_ref.shape[1]

    @pl.when(step == 0)
    def _():
        read[...] = jnp.zeros_like(read)
        normed[:rows] = normalise(a1x_ref, gain_ref)
        normed[rows:] = normalise(b1x_ref, gain_ref)

    near = {}
    for c in (1, 2, 0):
        near[c] = project_rows(normed[...], w_ref[c], c)
        a1_ref[c] = near[c][:rows]
        b1_ref[c] = near[c][rows:]
    scores = []
    for p in range(GROUP):
        keys = jnp.concatenate([own_ref[1, :, pair_cols(p)], near[1][:, pair_cols(p)]], axis=0)
        scores.append(dot(keys, two_heads(own_ref[0, :, pair_cols(p)]), NT))
    weights = []
    for p in range(GROUP):
        weights.append(soften(bias_ref, 0, scores[p]))
        weight_ref[p] = weights[p]
    attended = []
    for p in range(GROUP):
        values = jnp.concatenate([own_ref[2, :, pair_cols(p)], near[2][:, pair_cols(p)]], axis=0)
        attended.append(fold_heads(dot(values, weights[p], TN)).astype(BF16))
        att_ref[p] = attended[p]
    read[...] += dot(mix_ref[...], jnp.concatenate(attended, axis=0), NN)

    @pl.when(step == steps - 1)
    def _():
        half = read.shape[0] // 2
        keep_ref[...] = read[:half]
        send_ref[...] = read[half:]


def side_kernel(bias_ref, own_ref, a1_ref, b1_ref, a2_ref, b2_ref, weight_ref, att_ref):
    own_rows = own_ref.shape[1]
    jobs = [(p, side) for p in range(GROUP) for side in range(2)]
    near, far = (a1_ref, b1_ref), (a2_ref, b2_ref)

    def stack(p, side, part):
        cols = pair_cols(p)
        return jnp.concatenate(
            [own_ref[part, :, cols], near[side][part, :, cols], far[side][part - 1, :, cols]],
            axis=0,
        )

    scores = [
        dot(stack(p, side, 1), two_heads(near[side][0, :, pair_cols(p)]), NT) for p, side in jobs
    ]
    weights = []
    for (p, side), score in zip(jobs, scores):
        weights.append(soften(bias_ref, 1 + side, score))
        weight_ref[p, side] = weights[-1][:own_rows]
    for (p, side), weight in zip(jobs, weights):
        att_ref[p, side] = fold_heads(dot(stack(p, side, 2), weight, TN)).astype(BF16)


def spread_kernel(keep_ref, got_ref, out_ref):
    rows = (keep_ref[...] + got_ref[...]).astype(BF16)
    for s in range(out_ref.shape[0]):
        out_ref[s] = rows


def pool_kernel(steps, rows_ref, ids_ref, targets_ref, out_ref, counts_ref, sums):
    step = pl.program_id(0)
    half_read, panels = out_ref.shape
    count, _, tok_rows = rows_ref.shape

    @pl.when(step == 0)
    def _():
        sums[...] = jnp.zeros_like(sums)

    panel = lax.broadcasted_iota(jnp.int32, (panels, count * tok_rows), 0)
    hits = jnp.where(panel == ids_ref[...], 1.0, 0.0).astype(BF16)
    rows = jnp.concatenate([rows_ref[s] for s in range(count)], axis=1)
    rows = jnp.concatenate([rows, jnp.ones((16, count * tok_rows), BF16)], axis=0)
    sums[...] += dot(rows, hits, NT)

    @pl.when(step == steps - 1)
    def _():
        counts = sums[half_read : half_read + 1]
        out_ref[...] = sums[:half_read] / counts - targets_ref[...]
        counts_ref[...] = counts


def back_kernel(
    core_ref, resid_a_ref, resid_b_ref, counts_ref, hot_ref, mix_ref, gain_ref, *refs
):
    sources, (keep_ref, send_ref, stat_ref, loss_ref) = refs[:9], refs[9:13]
    buffers, arrived = refs[13:22], refs[22]
    copies = [
        pltpu.make_async_copy(source, buffer, arrived.at[n])
        for n, (source, buffer) in enumerate(zip(sources, buffers))
    ]
    for copy in copies:
        copy.start()
    own_ref, a1_ref, b1_ref, own_att_ref, side_att_ref, own_w_ref, side_w_ref, w_ref, tokens_ref = buffers
    own_rows = own_ref.shape[1]
    pairs = own_ref.shape[2] // PAIR
    residual = jnp.concatenate([resid_a_ref[...], resid_b_ref[...]], axis=0)
    loss_ref[...] = jnp.broadcast_to(
        jnp.sum(counts_ref[...] * residual * residual, keepdims=True), loss_ref.shape
    )
    panel_grad = dot(mix_ref[...].astype(F32), residual, TN, lax.Precision.HIGHEST).astype(BF16)
    out_grad = dot(panel_grad, hot_ref[...], NN).astype(BF16)
    stretches = (own_ref, a1_ref, b1_ref)

    def tile_of(p, t):
        return out_grad[pair_cols(p), t * own_rows : (t + 1) * own_rows]

    def open_pair(p):
        values = jnp.concatenate([r[2, :, pair_cols(p)] for r in stretches], axis=0)
        grads, changes = [], []
        for t in range(3):
            tile = tile_of(p, t)
            none = jnp.zeros((HD, own_rows), BF16)
            grads.append(
                jnp.concatenate(
                    [
                        jnp.concatenate([tile[:HD], none], axis=0),
                        jnp.concatenate([none, tile[HD:]], axis=0),
                    ],
                    axis=1,
                )
            )
            changes.append(dot(values if t == 0 else values[:own_rows], grads[t], NN))
        return grads, changes

    def score_pair(p, changes):
        scores = []
        for t in range(3):
            attended = own_att_ref[p] if t == 0 else side_att_ref[p, t - 1]
            product = tile_of(p, t).astype(F32) * attended.astype(F32)
            delta = jnp.concatenate(
                [
                    jnp.sum(product[:HD], axis=0, keepdims=True),
                    jnp.sum(product[HD:], axis=0, keepdims=True),
                ],
                axis=1,
            )
            weight = own_w_ref[p] if t == 0 else side_w_ref[p, t - 1]
            scores.append((weight.astype(F32) * (changes[t] - delta)).astype(BF16))
        return scores

    def close_pair(p, grads, scores):
        keys = jnp.concatenate([r[1, :, pair_cols(p)] for r in stretches], axis=0)
        grad_query = fold_heads(dot(keys, scores[0], TN)) * SCALE
        queries = jnp.concatenate([two_heads(r[0, :, pair_cols(p)]) for r in stretches], axis=0)
        own_scores = jnp.concatenate([s[:own_rows] for s in scores], axis=1)
        grad_key = dot(own_scores, queries, NN)
        own_weights = jnp.concatenate(
            [own_w_ref[p, :own_rows], side_w_ref[p, 0], side_w_ref[p, 1]], axis=1
        )
        grad_value = dot(own_weights, jnp.concatenate(grads, axis=1), NT)
        return grad_query.T.astype(BF16), grad_key.astype(BF16), grad_value.astype(BF16)

    for copy in copies[:3]:
        copy.wait()
    opened = open_pair(0)
    for copy in copies[3:7]:
        copy.wait()
    grad_proj = []
    for p in range(pairs):
        grads, changes = opened
        if p + 1 < pairs:
            opened = open_pair(p + 1)
        grad_proj.append(close_pair(p, grads, score_pair(p, changes)))
    flat = jnp.concatenate([grad_proj[p][c] for c in range(3) for p in range(pairs)], axis=1)
    for copy in copies[7:]:
        copy.wait()
    half = keep_ref.shape[1]
    inputs = tokens_ref[...].astype(F32)
    scaled = inputs * gain_ref[...]
    row_sum = jnp.zeros((own_rows, 1), F32)
    parts = []
    for h in range(2):
        rows = slice(h * half, (h + 1) * half)
        w_part = jnp.concatenate([w_ref[c, rows, :] for c in range(3)], axis=1)
        parts.append(dot(flat, w_part, NT))
        row_sum += jnp.sum(scaled[:, rows] * parts[h], axis=-1, keepdims=True)
    first = core_ref[0] == 0
    keep_ref[...] = jnp.where(first, parts[0], parts[1])
    send_ref[:, :half] = jnp.where(first, parts[1], parts[0]).astype(BF16)
    high = row_sum.astype(BF16).astype(F32)
    lane = lax.broadcasted_iota(jnp.int32, (own_rows, BLK), 1)
    send_ref[:, half:] = jnp.where(lane < HD, high, row_sum - high).astype(BF16)
    stat_ref[...] = jnp.where(lane < HD, row_sum, inverse_root(inputs))


def final_kernel(core_ref, keep_ref, got_ref, stat_ref, tokens_ref, gain_ref, out_ref):
    half = keep_ref.shape[1]
    cols = pl.ds(pl.multiple_of(core_ref[0] * half, half), half)
    got_sum = got_ref[:, half : half + 1].astype(F32) + got_ref[:, half + HD : half + HD + 1].astype(F32)
    row_sum = stat_ref[:, :1] + got_sum
    inverse = stat_ref[:, HD : HD + 1]
    grad_normed = keep_ref[...] + got_ref[:, :half].astype(F32)
    shrink = row_sum * (inverse * inverse * inverse) * (0.5 / half)
    out_ref[...] = (
        gain_ref[:, cols] * grad_normed * inverse - tokens_ref[:, cols].astype(F32) * shrink
    )


def pair_spec(parts, rows):
    return pl.BlockSpec((parts, rows, GROUP * PAIR), lambda p: (0, 0, p))


def whole_spec(shape):
    return pl.BlockSpec(shape, lambda p: (0,) * len(shape))


def lead_spec(shape):
    return pl.BlockSpec((GROUP,) + shape, lambda p: (p,) + (0,) * len(shape))


SMEM_SPEC = pl.BlockSpec(memory_space=pltpu.SMEM)


def local(
    tokens, norm_gain, w_qkv, w_out, readout_weight, targets, key_blocks, list_len, voxel_panel
):
    tok_rows, width = tokens.shape
    cols = w_qkv.shape[2]
    pairs = cols // PAIR
    steps = pairs // GROUP
    panels, readout = targets.shape
    half_read = readout // 2
    half_width = width // 2
    seq_count = lax.axis_size("seq")
    seq_index = lax.axis_index("seq")
    core = lax.axis_index("head")
    side_step = 2 * core - 1
    all_tokens = voxel_panel.shape[0]
    per = tok_rows // BLK
    core_swap = [(0, 1), (1, 0)]

    def shifted(far):
        return [
            (2 * s, 2 * (s + far)) for s in range(seq_count - far)
        ] + [(2 * (s + far) + 1, 2 * s + 1) for s in range(seq_count - far)]

    a1_tokens = lax.ppermute(tokens, ("seq", "head"), shifted(1))
    a2_tokens = lax.ppermute(tokens, ("seq", "head"), shifted(2))

    gain = norm_gain.reshape(1, width)
    flat_ids = voxel_panel.reshape(1, all_tokens)
    place = jnp.stack([seq_index, core, jnp.int32(seq_count)]).astype(jnp.int32)
    vmem = pl.BlockSpec(memory_space=pltpu.VMEM)
    whole_tokens = whole_spec((tok_rows, width))
    whole_gain = whole_spec((1, width))
    bias_spec = whole_spec((3, 3 * per, 2 * tok_rows))
    bias, hot, mix, own_targets, own = pl.pallas_call(
        first_kernel,
        grid=(3,),
        in_specs=[SMEM_SPEC] * 3
        + [
            whole_spec((1, all_tokens)),
            whole_spec(w_out.shape),
            whole_spec(readout_weight.shape),
            whole_spec(targets.shape),
            whole_tokens,
            whole_gain,
            pl.BlockSpec((1, width, cols), lambda c: (c, 0, 0)),
        ],
        out_specs=[
            bias_spec,
            whole_spec((panels, 3 * tok_rows)),
            whole_spec((readout, cols)),
            whole_spec((half_read, panels)),
            pl.BlockSpec((1, tok_rows, cols), lambda c: (c, 0, 0)),
        ],
        out_shape=[
            jax.ShapeDtypeStruct((3, 3 * per, 2 * tok_rows), F32),
            jax.ShapeDtypeStruct((panels, 3 * tok_rows), BF16),
            jax.ShapeDtypeStruct((readout, cols), BF16),
            jax.ShapeDtypeStruct((half_read, panels), F32),
            jax.ShapeDtypeStruct((3, tok_rows, cols), BF16),
        ],
        scratch_shapes=[pltpu.VMEM((readout, panels), F32), pltpu.VMEM((tok_rows, width), BF16)],
        compiler_params=params("arbitrary", mib=60),
        cost_estimate=pl.CostEstimate(flops=2**31, bytes_accessed=6 * MIB, transcendentals=0),
        name="first",
    )(
        place, key_blocks.T, list_len, flat_ids, w_out, readout_weight, targets, tokens, gain, w_qkv
    )

    a2_tokens, own = lax.optimization_barrier((a2_tokens, own))
    piece = tok_rows // 2
    b2_top = lax.ppermute(a2_tokens[:piece], "head", core_swap)
    b2_low = lax.ppermute(a2_tokens[piece:], "head", core_swap)
    a2, b2 = pl.pallas_call(
        far_kernel,
        grid=(2,),
        in_specs=[
            whole_tokens,
            whole_spec((piece, width)),
            whole_spec((piece, width)),
            whole_gain,
            pl.BlockSpec((1, width, cols), lambda c: (c + 1, 0, 0)),
        ],
        out_specs=[pl.BlockSpec((1, tok_rows, cols), lambda c: (c, 0, 0))] * 2,
        out_shape=[jax.ShapeDtypeStruct((2, tok_rows, cols), BF16)] * 2,
        scratch_shapes=[pltpu.VMEM((2 * tok_rows, width), BF16)],
        compiler_params=params("arbitrary"),
        cost_estimate=pl.CostEstimate(flops=2**20, bytes_accessed=4 * MIB, transcendentals=0),
        name="far",
    )(a2_tokens, b2_top, b2_low, gain, w_qkv)

    a1_tokens, own, a2, b2, mix, own_targets, hot, bias = lax.optimization_barrier(
        (a1_tokens, own, a2, b2, mix, own_targets, hot, bias)
    )
    b1_tokens = lax.ppermute(a1_tokens, "head", core_swap)
    mix_spec = pl.BlockSpec((readout, GROUP * PAIR), lambda p: (0, p))
    a1, b1, own_weight, own_att, read_keep, read_send = pl.pallas_call(
        functools.partial(near_kernel, steps),
        grid=(steps,),
        in_specs=[
            bias_spec,
            pair_spec(3, tok_rows),
            mix_spec,
            whole_tokens,
            whole_tokens,
            whole_gain,
            pair_spec(3, width),
        ],
        out_specs=[
            pair_spec(3, tok_rows),
            pair_spec(3, tok_rows),
            lead_spec((3 * tok_rows, 2 * tok_rows)),
            lead_spec((PAIR, tok_rows)),
            whole_spec((half_read, tok_rows)),
            whole_spec((half_read, tok_rows)),
        ],
        out_shape=[
            jax.ShapeDtypeStruct((3, tok_rows, cols), BF16),
            jax.ShapeDtypeStruct((3, tok_rows, cols), BF16),
            jax.ShapeDtypeStruct((pairs, 3 * tok_rows, 2 * tok_rows), BF16),
            jax.ShapeDtypeStruct((pairs, PAIR, tok_rows), BF16),
            jax.ShapeDtypeStruct((half_read, tok_rows), F32),
            jax.ShapeDtypeStruct((half_read, tok_rows), F32),
        ],
        scratch_shapes=[
            pltpu.VMEM((2 * tok_rows, width), BF16),
            pltpu.VMEM((readout, tok_rows), F32),
        ],
        compiler_params=params("arbitrary"),
        name="near",
    )(bias, own, mix, a1_tokens, b1_tokens, gain, w_qkv)

    read_got = lax.ppermute(read_send, "head", core_swap)
    spread = pl.pallas_call(
        spread_kernel,
        out_shape=jax.ShapeDtypeStruct((seq_count, half_read, tok_rows), BF16),
        compiler_params=params(),
        name="spread",
    )(read_keep, read_got)
    all_rows = lax.all_to_all(spread, "seq", 0, 0)

    side_weight, side_att = pl.pallas_call(
        side_kernel,
        grid=(steps,),
        in_specs=[bias_spec] + [pair_spec(3, tok_rows)] * 3 + [pair_spec(2, tok_rows)] * 2,
        out_specs=[lead_spec((2, tok_rows, 2 * tok_rows)), lead_spec((2, PAIR, tok_rows))],
        out_shape=[
            jax.ShapeDtypeStruct((pairs, 2, tok_rows, 2 * tok_rows), BF16),
            jax.ShapeDtypeStruct((pairs, 2, PAIR, tok_rows), BF16),
        ],
        compiler_params=params("arbitrary"),
        cost_estimate=pl.CostEstimate(
            flops=pairs * 4 * 2 * 2 * 768 * 256 * 128,
            bytes_accessed=8 * MIB,
            transcendentals=pairs * 4 * 768 * 256,
        ),
        name="attend_sides",
    )(bias, own, a1, b1, a2, b2)
    all_rows, side_weight, side_att = lax.optimization_barrier((all_rows, side_weight, side_att))

    batch = min(seq_count, 8)
    pool_steps = seq_count // batch
    resid_a, counts = pl.pallas_call(
        functools.partial(pool_kernel, pool_steps),
        grid=(pool_steps,),
        in_specs=[
            pl.BlockSpec((batch, half_read, tok_rows), lambda s: (s, 0, 0)),
            pl.BlockSpec((1, batch * tok_rows), lambda s: (0, s)),
            whole_spec((half_read, panels)),
        ],
        out_specs=[whole_spec((half_read, panels)), whole_spec((1, panels))],
        out_shape=[
            jax.ShapeDtypeStruct((half_read, panels), F32),
            jax.ShapeDtypeStruct((1, panels), F32),
        ],
        scratch_shapes=[pltpu.VMEM((half_read + 16, panels), F32)],
        compiler_params=params("arbitrary"),
        name="pool",
    )(all_rows, flat_ids, own_targets)
    resid_b = lax.ppermute(resid_a, "head", core_swap)

    core_index = place[1:2]
    sources = (own, a1, b1, own_att, side_att, own_weight, side_weight, w_qkv, tokens)
    keep, send, stats, loss = pl.pallas_call(
        back_kernel,
        in_specs=[SMEM_SPEC] + [vmem] * 6 + [pl.BlockSpec(memory_space=pl.ANY)] * len(sources),
        out_specs=[vmem] * 4,
        out_shape=[
            jax.ShapeDtypeStruct((tok_rows, half_width), F32),
            jax.ShapeDtypeStruct((tok_rows, half_width + BLK), BF16),
            jax.ShapeDtypeStruct((tok_rows, BLK), F32),
            jax.ShapeDtypeStruct((1, BLK), F32),
        ],
        scratch_shapes=[pltpu.VMEM(a.shape, a.dtype) for a in sources]
        + [pltpu.SemaphoreType.DMA((len(sources),))],
        compiler_params=params(),
        name="back",
    )(core_index, resid_a, resid_b, counts, hot, mix, gain, *sources)
    got = lax.ppermute(send, "head", core_swap)
    loss_mean = 0.5 * loss[0, :1] / (all_tokens * readout)
    gradient = pl.pallas_call(
        final_kernel,
        in_specs=[SMEM_SPEC] + [pl.BlockSpec(memory_space=pltpu.VMEM)] * 5,
        out_shape=jax.ShapeDtypeStruct((tok_rows, half_width), F32),
        compiler_params=params(),
        name="final",
    )(core_index, keep, got, stats, tokens, gain)
    return (gradient, loss_mean)


def solution(mesh):
    return jax.shard_map(
        local,
        mesh=mesh,
        in_specs=(
            P(("groups", "seq"), None),
            P(),
            P(None, None, "head"),
            P("head", None),
            P(),
            P("groups", None),
            P("groups", None),
            P("groups"),
            P("groups", None),
        ),
        out_specs=(P(("groups", "seq"), "head"), P("groups")),
        check_vma=False,
    )
```

```python
import functools
import math

import jax
import jax.numpy as jnp
import numpy as np
from jax import lax
from jax.experimental import pallas as pl
from jax.experimental.pallas import tpu as pltpu
from jax.sharding import PartitionSpec as P

HD = 64
BLK = 128
LIST = 4
PAIR = 2 * HD
F32 = jnp.float32
BF16 = jnp.bfloat16
DEAD = 1e30
SCALE = 1.0 / math.sqrt(HD)
KEY_STEP = np.array([[0, 1, -1], [0, 1, 2], [0, -1, -2]], np.int32)
MIB = 1024 * 1024

NN = (((1,), (0,)), ((), ()))
NT = (((1,), (1,)), ((), ()))
TN = (((0,), (0,)), ((), ()))


def dot(a, b, dims, precision=None):
    return lax.dot_general(a, b, dims, precision=precision, preferred_element_type=F32)


def params(*semantics, mib=52):
    return pltpu.CompilerParams(vmem_limit_bytes=mib * MIB, dimension_semantics=semantics or None)


def inverse_root(inputs):
    return 1.0 / jnp.sqrt(jnp.mean(inputs * inputs, axis=-1, keepdims=True) + 1e-05)


def normalise(x_ref, gain_ref):
    inputs = x_ref[...].astype(F32)
    return (inputs * gain_ref[...] * inverse_root(inputs)).astype(BF16)


def project_rows(normed, w_part, part):
    rows = dot(normed, w_part, NN).astype(BF16)
    scale = jnp.where(part == 0, SCALE, 1.0)
    return (rows.astype(F32) * scale).astype(BF16)


def first_kernel(
    place_ref, lists_ref, lengths_ref, ids_ref, w_out_ref, read_ref, targets_ref, x_ref, gain_ref, w_ref,
    bias_ref, hot_ref, mix_ref, own_targets_ref, own_ref, flipped, normed,
):
    part = pl.program_id(0)

    @pl.when(part == 0)
    def _():
        normed[...] = normalise(x_ref, gain_ref)

    own_ref[0] = project_rows(normed[...], w_ref[0], part)

    @pl.when(part == 0)
    def _():
        prepare(
            place_ref, lists_ref, lengths_ref, ids_ref, w_out_ref, read_ref, targets_ref,
            bias_ref, hot_ref, mix_ref, own_targets_ref, flipped,
        )


def prepare(
    place_ref, lists_ref, lengths_ref, ids_ref, w_out_ref, read_ref, targets_ref,
    bias_ref, hot_ref, mix_ref, own_targets_ref, flipped,
):
    seq_index, core, seq_count = place_ref[0], place_ref[1], place_ref[2]
    side = 2 * core - 1
    half_read = own_targets_ref.shape[0]
    panels, tok_rows = hot_ref.shape[0], hot_ref.shape[1] // 3
    per = tok_rows // BLK
    mix = dot(w_out_ref[...], read_ref[...], NN).T
    flip = jnp.concatenate([mix[half_read:], mix[:half_read]], axis=0)
    mix_ref[...] = jnp.where(core == 0, mix, flip).astype(BF16)
    flipped[...] = targets_ref[...].T
    own_targets_ref[...] = flipped[pl.ds(pl.multiple_of(core * half_read, half_read), half_read), :]
    panel = lax.broadcasted_iota(jnp.int32, (panels, tok_rows), 0)
    column = lax.broadcasted_iota(jnp.int32, (1, 2 * tok_rows), 1)
    for t, move in enumerate((0, 1, -1)):
        stretch = seq_index + side * move
        inside = (stretch >= 0) & (stretch < seq_count)
        stretch = jnp.clip(stretch, 0, seq_count - 1)
        ids = ids_ref[:, pl.ds(pl.multiple_of(stretch * tok_rows, tok_rows), tok_rows)]
        hits = (panel == ids) & inside
        hot_ref[:, t * tok_rows : (t + 1) * tok_rows] = jnp.where(hits, 1.0, 0.0).astype(BF16)
        for k in range(3 * per):
            key_block = (seq_index + side * int(KEY_STEP[t, k // per])) * per + k % per
            row = jnp.zeros((1, 2 * tok_rows), F32)
            for b in range(per):
                query_block = stretch * per + b
                live = jnp.logical_not(inside)
                for j in range(LIST):
                    live = live | (
                        (lists_ref[j, query_block] == key_block) & (j < lengths_ref[query_block])
                    )
                off = jnp.where(live, 0.0, DEAD)
                row = jnp.where((column // BLK) % per == b, off, row)
            bias_ref[t, k : k + 1, :] = row


def pair_cols(p):
    return slice(p * PAIR, (p + 1) * PAIR)


def two_heads(tile):
    lane = lax.broadcasted_iota(jnp.int32, tile.shape, 1)
    zero = jnp.zeros_like(tile)
    return jnp.concatenate(
        [jnp.where(lane < HD, tile, zero), jnp.where(lane >= HD, tile, zero)], axis=0
    )


def fold_heads(pair_t):
    half = pair_t.shape[1] // 2
    return jnp.concatenate([pair_t[:HD, :half], pair_t[HD:, half:]], axis=0)


def soften(bias_ref, stretch, scores):
    count = scores.shape[0] // BLK
    blocks = [scores[k * BLK : (k + 1) * BLK] for k in range(count)]
    biases = [bias_ref[stretch, k : k + 1, :] for k in range(count)]
    tops = [jnp.max(b, axis=0, keepdims=True) - d for b, d in zip(blocks, biases)]
    top = functools.reduce(jnp.maximum, tops)
    expo = [jnp.exp(b - (top + d)) for b, d in zip(blocks, biases)]
    total = functools.reduce(jnp.add, [jnp.sum(e, axis=0, keepdims=True) for e in expo])
    inverse = 1.0 / total
    return jnp.concatenate([(e * inverse).astype(BF16) for e in expo], axis=0)


def start_all(copies):
    for copy in copies:
        copy.start()
    return copies


def wait_all(copies):
    for copy in copies:
        copy.wait()


def near_kernel(
    bias_ref, mix_ref, a1x_ref, b1x_ref, gain_ref, own_hbm, w_hbm,
    a1_hbm, b1_hbm, weight_hbm, att_ref, keep_ref, send_ref,
    own_ref, w_ref, near_ref, weight_ref, arrived, sent,
):
    rows = own_ref.shape[1]
    pairs = own_ref.shape[2] // PAIR
    order = (1, 2, 0)
    w_in = {c: pltpu.make_async_copy(w_hbm.at[c], w_ref.at[c], arrived.at[c]) for c in order}
    own_in = pltpu.make_async_copy(own_hbm, own_ref, arrived.at[3])
    start_all([w_in[1], own_in, w_in[2], w_in[0]])
    normed = jnp.concatenate([normalise(a1x_ref, gain_ref), normalise(b1x_ref, gain_ref)], axis=0)
    out = []

    def project(c):
        w_in[c].wait()
        near_ref[c] = project_rows(normed, w_ref[c], c)
        for side, target in enumerate((a1_hbm, b1_hbm)):
            source = near_ref.at[c, pl.ds(side * rows, rows)]
            out.append(pltpu.make_async_copy(source, target.at[c], sent.at[2 * c + side]))
            out[-1].start()

    def stack(c, p):
        return jnp.concatenate([own_ref[c, :, pair_cols(p)], near_ref[c, :, pair_cols(p)]], axis=0)

    def score(p):
        return dot(stack(1, p), two_heads(own_ref[0, :, pair_cols(p)]), NT)

    project(1)
    own_in.wait()
    scores = {0: score(0)}
    project(2)
    attended = []
    for p in range(pairs):
        if p + 1 < pairs:
            scores[p + 1] = score(p + 1)
        weight = soften(bias_ref, 0, scores[p])
        weight_ref[p] = weight
        out.append(pltpu.make_async_copy(weight_ref.at[p], weight_hbm.at[p], sent.at[6 + p]))
        out[-1].start()
        if p == pairs - 1:
            project(0)
        attended.append(fold_heads(dot(stack(2, p), weight, TN)).astype(BF16))
        att_ref[p] = attended[p]
    read = dot(mix_ref[...], jnp.concatenate(attended, axis=0), NN)
    half = keep_ref.shape[0]
    keep_ref[...] = read[:half]
    send_ref[...] = read[half:]
    wait_all(out)


def side_kernel(
    bias_ref, a2x_ref, b2x_ref, gain_ref, own_hbm, a1_hbm, b1_hbm, w_hbm, weight_hbm, att_ref,
    own_ref, a1_ref, b1_ref, w_ref, far_ref, weight_ref, arrived, sent,
):
    rows = own_ref.shape[1]
    pairs = own_ref.shape[2] // PAIR
    w_in = [
        pltpu.make_async_copy(w_hbm.at[c + 1], w_ref.at[c], arrived.at[c]) for c in range(2)
    ]
    rows_in = [
        pltpu.make_async_copy(source, target, arrived.at[2 + n])
        for n, (source, target) in enumerate(
            ((own_hbm, own_ref), (a1_hbm, a1_ref), (b1_hbm, b1_ref))
        )
    ]
    start_all([w_in[0]] + rows_in + [w_in[1]])
    normed = jnp.concatenate([normalise(a2x_ref, gain_ref), normalise(b2x_ref, gain_ref)], axis=0)
    near = (a1_ref, b1_ref)
    out = []

    def project(c):
        w_in[c].wait()
        far_ref[c] = dot(normed, w_ref[c], NN).astype(BF16)

    def stack(c, p, side):
        cols = pair_cols(p)
        far = far_ref[c - 1, side * rows : (side + 1) * rows, cols]
        return jnp.concatenate([own_ref[c, :, cols], near[side][c, :, cols], far], axis=0)

    def score(p, side):
        return dot(stack(1, p, side), two_heads(near[side][0, :, pair_cols(p)]), NT)

    project(0)
    wait_all(rows_in)
    jobs = [(p, side) for p in range(pairs) for side in range(2)]
    scores = {jobs[0]: score(*jobs[0])}
    project(1)
    for n, (p, side) in enumerate(jobs):
        if n + 1 < len(jobs):
            scores[jobs[n + 1]] = score(*jobs[n + 1])
        weight = soften(bias_ref, 1 + side, scores[p, side])
        weight_ref[p, side] = weight[:rows]
        out.append(
            pltpu.make_async_copy(weight_ref.at[p, side], weight_hbm.at[p, side], sent.at[n])
        )
        out[-1].start()
        att_ref[p, side] = fold_heads(dot(stack(2, p, side), weight, TN)).astype(BF16)
    wait_all(out)


def spread_kernel(keep_ref, got_ref, out_ref):
    rows = (keep_ref[...] + got_ref[...]).astype(BF16)
    for s in range(out_ref.shape[0]):
        out_ref[s] = rows


def pool_kernel(steps, rows_ref, ids_ref, targets_ref, out_ref, counts_ref, sums):
    step = pl.program_id(0)
    half_read, panels = out_ref.shape
    count, _, tok_rows = rows_ref.shape

    @pl.when(step == 0)
    def _():
        sums[...] = jnp.zeros_like(sums)

    panel = lax.broadcasted_iota(jnp.int32, (panels, count * tok_rows), 0)
    hits = jnp.where(panel == ids_ref[...], 1.0, 0.0).astype(BF16)
    rows = jnp.concatenate([rows_ref[s] for s in range(count)], axis=1)
    rows = jnp.concatenate([rows, jnp.ones((16, count * tok_rows), BF16)], axis=0)
    sums[...] += dot(rows, hits, NT)

    @pl.when(step == steps - 1)
    def _():
        counts = sums[half_read : half_read + 1]
        out_ref[...] = sums[:half_read] / counts - targets_ref[...]
        counts_ref[...] = counts


def back_kernel(
    core_ref, resid_a_ref, resid_b_ref, counts_ref, hot_ref, mix_ref, gain_ref, *refs
):
    sources, (keep_ref, send_ref, stat_ref, loss_ref) = refs[:9], refs[9:13]
    buffers, arrived = refs[13:22], refs[22]
    own_ref, a1_ref, b1_ref, own_att_ref, side_att_ref, own_w_ref, side_w_ref, w_ref, tokens_ref = buffers
    pairs = own_ref.shape[2] // PAIR
    copies = [
        pltpu.make_async_copy(sources[n], buffers[n], arrived.at[n]) for n in (0, 1, 2, 3, 4, 7, 8)
    ]
    weight_in = [
        [
            pltpu.make_async_copy(
                sources[n].at[p], buffers[n].at[p], arrived.at[9 + 2 * p + n - 5]
            )
            for n in (5, 6)
        ]
        for p in range(pairs)
    ]
    start_all(copies[:5] + [copy for pair in weight_in for copy in pair] + copies[5:])
    own_rows = own_ref.shape[1]
    residual = jnp.concatenate([resid_a_ref[...], resid_b_ref[...]], axis=0)
    loss_ref[...] = jnp.broadcast_to(
        jnp.sum(counts_ref[...] * residual * residual, keepdims=True), loss_ref.shape
    )
    panel_grad = dot(mix_ref[...].astype(F32), residual, TN, lax.Precision.HIGHEST).astype(BF16)
    out_grad = dot(panel_grad, hot_ref[...], NN).astype(BF16)
    stretches = (own_ref, a1_ref, b1_ref)

    def tile_of(p, t):
        return out_grad[pair_cols(p), t * own_rows : (t + 1) * own_rows]

    def open_pair(p):
        values = jnp.concatenate([r[2, :, pair_cols(p)] for r in stretches], axis=0)
        grads, changes = [], []
        for t in range(3):
            tile = tile_of(p, t)
            none = jnp.zeros((HD, own_rows), BF16)
            grads.append(
                jnp.concatenate(
                    [
                        jnp.concatenate([tile[:HD], none], axis=0),
                        jnp.concatenate([none, tile[HD:]], axis=0),
                    ],
                    axis=1,
                )
            )
            changes.append(dot(values if t == 0 else values[:own_rows], grads[t], NN))
        return grads, changes

    def score_pair(p, changes):
        scores = []
        for t in range(3):
            attended = own_att_ref[p] if t == 0 else side_att_ref[p, t - 1]
            product = tile_of(p, t).astype(F32) * attended.astype(F32)
            delta = jnp.concatenate(
                [
                    jnp.sum(product[:HD], axis=0, keepdims=True),
                    jnp.sum(product[HD:], axis=0, keepdims=True),
                ],
                axis=1,
            )
            weight = own_w_ref[p] if t == 0 else side_w_ref[p, t - 1]
            scores.append((weight.astype(F32) * (changes[t] - delta)).astype(BF16))
        return scores

    def close_pair(p, grads, scores):
        keys = jnp.concatenate([r[1, :, pair_cols(p)] for r in stretches], axis=0)
        grad_query = fold_heads(dot(keys, scores[0], TN)) * SCALE
        queries = jnp.concatenate([two_heads(r[0, :, pair_cols(p)]) for r in stretches], axis=0)
        own_scores = jnp.concatenate([s[:own_rows] for s in scores], axis=1)
        grad_key = dot(own_scores, queries, NN)
        own_weights = jnp.concatenate(
            [own_w_ref[p, :own_rows], side_w_ref[p, 0], side_w_ref[p, 1]], axis=1
        )
        grad_value = dot(own_weights, jnp.concatenate(grads, axis=1), NT)
        return grad_query.T.astype(BF16), grad_key.astype(BF16), grad_value.astype(BF16)

    wait_all(copies[:3])
    opened = open_pair(0)
    wait_all(copies[3:5])
    grad_proj = []
    for p in range(pairs):
        grads, changes = opened
        if p + 1 < pairs:
            opened = open_pair(p + 1)
        wait_all(weight_in[p])
        grad_proj.append(close_pair(p, grads, score_pair(p, changes)))
    flat = jnp.concatenate([grad_proj[p][c] for c in range(3) for p in range(pairs)], axis=1)
    wait_all(copies[5:])
    half = keep_ref.shape[1]
    inputs = tokens_ref[...].astype(F32)
    scaled = inputs * gain_ref[...]
    row_sum = jnp.zeros((own_rows, 1), F32)
    parts = []
    for h in range(2):
        rows = slice(h * half, (h + 1) * half)
        w_part = jnp.concatenate([w_ref[c, rows, :] for c in range(3)], axis=1)
        parts.append(dot(flat, w_part, NT))
        row_sum += jnp.sum(scaled[:, rows] * parts[h], axis=-1, keepdims=True)
    first = core_ref[0] == 0
    keep_ref[...] = jnp.where(first, parts[0], parts[1])
    send_ref[:, :half] = jnp.where(first, parts[1], parts[0]).astype(BF16)
    high = row_sum.astype(BF16).astype(F32)
    lane = lax.broadcasted_iota(jnp.int32, (own_rows, BLK), 1)
    send_ref[:, half:] = jnp.where(lane < HD, high, row_sum - high).astype(BF16)
    stat_ref[...] = jnp.where(lane < HD, row_sum, inverse_root(inputs))


def final_kernel(core_ref, keep_ref, got_ref, stat_ref, tokens_ref, gain_ref, out_ref):
    half = keep_ref.shape[1]
    cols = pl.ds(pl.multiple_of(core_ref[0] * half, half), half)
    got_sum = got_ref[:, half : half + 1].astype(F32) + got_ref[:, half + HD : half + HD + 1].astype(F32)
    row_sum = stat_ref[:, :1] + got_sum
    inverse = stat_ref[:, HD : HD + 1]
    grad_normed = keep_ref[...] + got_ref[:, :half].astype(F32)
    shrink = row_sum * (inverse * inverse * inverse) * (0.5 / half)
    out_ref[...] = (
        gain_ref[:, cols] * grad_normed * inverse - tokens_ref[:, cols].astype(F32) * shrink
    )


def whole_spec(shape):
    return pl.BlockSpec(shape, lambda p: (0,) * len(shape))


SMEM_SPEC = pl.BlockSpec(memory_space=pltpu.SMEM)


def local(
    tokens, norm_gain, w_qkv, w_out, readout_weight, targets, key_blocks, list_len, voxel_panel
):
    tok_rows, width = tokens.shape
    cols = w_qkv.shape[2]
    pairs = cols // PAIR
    panels, readout = targets.shape
    half_read = readout // 2
    half_width = width // 2
    seq_count = lax.axis_size("seq")
    seq_index = lax.axis_index("seq")
    core = lax.axis_index("head")
    side_step = 2 * core - 1
    all_tokens = voxel_panel.shape[0]
    per = tok_rows // BLK
    core_swap = [(0, 1), (1, 0)]

    def shifted(far):
        return [
            (2 * s, 2 * (s + far)) for s in range(seq_count - far)
        ] + [(2 * (s + far) + 1, 2 * s + 1) for s in range(seq_count - far)]

    a1_tokens = lax.ppermute(tokens, ("seq", "head"), shifted(1))
    a2_tokens = lax.ppermute(tokens, ("seq", "head"), shifted(2))

    gain = norm_gain.reshape(1, width)
    flat_ids = voxel_panel.reshape(1, all_tokens)
    place = jnp.stack([seq_index, core, jnp.int32(seq_count)]).astype(jnp.int32)
    vmem = pl.BlockSpec(memory_space=pltpu.VMEM)
    whole_tokens = whole_spec((tok_rows, width))
    whole_gain = whole_spec((1, width))
    bias_spec = whole_spec((3, 3 * per, 2 * tok_rows))
    bias, hot, mix, own_targets, own = pl.pallas_call(
        first_kernel,
        grid=(3,),
        in_specs=[SMEM_SPEC] * 3
        + [
            whole_spec((1, all_tokens)),
            whole_spec(w_out.shape),
            whole_spec(readout_weight.shape),
            whole_spec(targets.shape),
            whole_tokens,
            whole_gain,
            pl.BlockSpec((1, width, cols), lambda c: (c, 0, 0)),
        ],
        out_specs=[
            bias_spec,
            whole_spec((panels, 3 * tok_rows)),
            whole_spec((readout, cols)),
            whole_spec((half_read, panels)),
            pl.BlockSpec((1, tok_rows, cols), lambda c: (c, 0, 0)),
        ],
        out_shape=[
            jax.ShapeDtypeStruct((3, 3 * per, 2 * tok_rows), F32),
            jax.ShapeDtypeStruct((panels, 3 * tok_rows), BF16),
            jax.ShapeDtypeStruct((readout, cols), BF16),
            jax.ShapeDtypeStruct((half_read, panels), F32),
            jax.ShapeDtypeStruct((3, tok_rows, cols), BF16),
        ],
        scratch_shapes=[pltpu.VMEM((readout, panels), F32), pltpu.VMEM((tok_rows, width), BF16)],
        compiler_params=params("arbitrary", mib=60),
        cost_estimate=pl.CostEstimate(flops=2**31, bytes_accessed=6 * MIB, transcendentals=0),
        name="first",
    )(
        place, key_blocks.T, list_len, flat_ids, w_out, readout_weight, targets, tokens, gain, w_qkv
    )

    a1_tokens, own, mix, own_targets, hot, bias = lax.optimization_barrier(
        (a1_tokens, own, mix, own_targets, hot, bias)
    )
    b1_tokens = lax.ppermute(a1_tokens, "head", core_swap)
    a2_tokens, b1_tokens = lax.optimization_barrier((a2_tokens, b1_tokens))
    b2_tokens = lax.ppermute(a2_tokens, "head", core_swap)
    hbm = pl.BlockSpec(memory_space=pl.ANY)
    a1, b1, own_weight, own_att, read_keep, read_send = pl.pallas_call(
        near_kernel,
        in_specs=[vmem] * 5 + [hbm] * 2,
        out_specs=[hbm] * 3 + [vmem] * 3,
        out_shape=[
            jax.ShapeDtypeStruct((3, tok_rows, cols), BF16),
            jax.ShapeDtypeStruct((3, tok_rows, cols), BF16),
            jax.ShapeDtypeStruct((pairs, 3 * tok_rows, 2 * tok_rows), BF16),
            jax.ShapeDtypeStruct((pairs, PAIR, tok_rows), BF16),
            jax.ShapeDtypeStruct((half_read, tok_rows), F32),
            jax.ShapeDtypeStruct((half_read, tok_rows), F32),
        ],
        scratch_shapes=[
            pltpu.VMEM((3, tok_rows, cols), BF16),
            pltpu.VMEM((3, width, cols), BF16),
            pltpu.VMEM((3, 2 * tok_rows, cols), BF16),
            pltpu.VMEM((pairs, 3 * tok_rows, 2 * tok_rows), BF16),
            pltpu.SemaphoreType.DMA((4,)),
            pltpu.SemaphoreType.DMA((6 + pairs,)),
        ],
        compiler_params=params(),
        cost_estimate=pl.CostEstimate(flops=2**33, bytes_accessed=8 * MIB, transcendentals=0),
        name="near",
    )(bias, mix, a1_tokens, b1_tokens, gain, own, w_qkv)

    read_send, b2_tokens = lax.optimization_barrier((read_send, b2_tokens))
    read_got = lax.ppermute(read_send, "head", core_swap)
    spread = pl.pallas_call(
        spread_kernel,
        out_shape=jax.ShapeDtypeStruct((seq_count, half_read, tok_rows), BF16),
        compiler_params=params(),
        name="spread",
    )(read_keep, read_got)
    all_rows = lax.all_to_all(spread, "seq", 0, 0)

    side_weight, side_att = pl.pallas_call(
        side_kernel,
        in_specs=[vmem] * 4 + [hbm] * 4,
        out_specs=[hbm, vmem],
        out_shape=[
            jax.ShapeDtypeStruct((pairs, 2, tok_rows, 2 * tok_rows), BF16),
            jax.ShapeDtypeStruct((pairs, 2, PAIR, tok_rows), BF16),
        ],
        scratch_shapes=[pltpu.VMEM((3, tok_rows, cols), BF16)] * 3
        + [
            pltpu.VMEM((2, width, cols), BF16),
            pltpu.VMEM((2, 2 * tok_rows, cols), BF16),
            pltpu.VMEM((pairs, 2, tok_rows, 2 * tok_rows), BF16),
            pltpu.SemaphoreType.DMA((5,)),
            pltpu.SemaphoreType.DMA((2 * pairs,)),
        ],
        compiler_params=params(),
        cost_estimate=pl.CostEstimate(flops=2**33, bytes_accessed=8 * MIB, transcendentals=0),
        name="attend_sides",
    )(bias, a2_tokens, b2_tokens, gain, own, a1, b1, w_qkv)
    all_rows, side_weight, side_att = lax.optimization_barrier((all_rows, side_weight, side_att))

    batch = min(seq_count, 8)
    pool_steps = seq_count // batch
    resid_a, counts = pl.pallas_call(
        functools.partial(pool_kernel, pool_steps),
        grid=(pool_steps,),
        in_specs=[
            pl.BlockSpec((batch, half_read, tok_rows), lambda s: (s, 0, 0)),
            pl.BlockSpec((1, batch * tok_rows), lambda s: (0, s)),
            whole_spec((half_read, panels)),
        ],
        out_specs=[whole_spec((half_read, panels)), whole_spec((1, panels))],
        out_shape=[
            jax.ShapeDtypeStruct((half_read, panels), F32),
            jax.ShapeDtypeStruct((1, panels), F32),
        ],
        scratch_shapes=[pltpu.VMEM((half_read + 16, panels), F32)],
        compiler_params=params("arbitrary"),
        name="pool",
    )(all_rows, flat_ids, own_targets)
    resid_b = lax.ppermute(resid_a, "head", core_swap)

    core_index = place[1:2]
    sources = (own, a1, b1, own_att, side_att, own_weight, side_weight, w_qkv, tokens)
    keep, send, stats, loss = pl.pallas_call(
        back_kernel,
        in_specs=[SMEM_SPEC] + [vmem] * 6 + [hbm] * len(sources),
        out_specs=[vmem] * 4,
        out_shape=[
            jax.ShapeDtypeStruct((tok_rows, half_width), F32),
            jax.ShapeDtypeStruct((tok_rows, half_width + BLK), BF16),
            jax.ShapeDtypeStruct((tok_rows, BLK), F32),
            jax.ShapeDtypeStruct((1, BLK), F32),
        ],
        scratch_shapes=[pltpu.VMEM(a.shape, a.dtype) for a in sources]
        + [pltpu.SemaphoreType.DMA((len(sources) + 2 * pairs,))],
        compiler_params=params(),
        name="back",
    )(core_index, resid_a, resid_b, counts, hot, mix, gain, *sources)
    got = lax.ppermute(send, "head", core_swap)
    loss_mean = 0.5 * loss[0, :1] / (all_tokens * readout)
    gradient = pl.pallas_call(
        final_kernel,
        in_specs=[SMEM_SPEC] + [pl.BlockSpec(memory_space=pltpu.VMEM)] * 5,
        out_shape=jax.ShapeDtypeStruct((tok_rows, half_width), F32),
        compiler_params=params(),
        name="final",
    )(core_index, keep, got, stats, tokens, gain)
    return (gradient, loss_mean)


def solution(mesh):
    return jax.shard_map(
        local,
        mesh=mesh,
        in_specs=(
            P(("groups", "seq"), None),
            P(),
            P(None, None, "head"),
            P("head", None),
            P(),
            P("groups", None),
            P("groups", None),
            P("groups"),
            P("groups", None),
        ),
        out_specs=(P(("groups", "seq"), "head"), P("groups")),
        check_vma=False,
    )
```

```python
import functools
import math

import jax
import jax.numpy as jnp
import numpy as np
from jax import lax
from jax.experimental import pallas as pl
from jax.experimental.pallas import tpu as pltpu
from jax.sharding import PartitionSpec as P

HD = 64
BLK = 128
LIST = 4
PAIR = 2 * HD
F32 = jnp.float32
BF16 = jnp.bfloat16
DEAD = 1e30
SCALE = 1.0 / math.sqrt(HD)
KEY_STEP = np.array([[0, 1, -1], [0, 1, 2], [0, -1, -2]], np.int32)
MIB = 1024 * 1024

NN = (((1,), (0,)), ((), ()))
NT = (((1,), (1,)), ((), ()))
TN = (((0,), (0,)), ((), ()))


def dot(a, b, dims, precision=None):
    return lax.dot_general(a, b, dims, precision=precision, preferred_element_type=F32)


def params(*semantics, mib=52):
    return pltpu.CompilerParams(vmem_limit_bytes=mib * MIB, dimension_semantics=semantics or None)


def inverse_root(inputs):
    return 1.0 / jnp.sqrt(jnp.mean(inputs * inputs, axis=-1, keepdims=True) + 1e-05)


def normalise(x_ref, gain_ref):
    inputs = x_ref[...].astype(F32)
    return (inputs * gain_ref[...] * inverse_root(inputs)).astype(BF16)


def project_rows(normed, w_part, part):
    rows = dot(normed, w_part, NN).astype(BF16)
    scale = jnp.where(part == 0, SCALE, 1.0)
    return (rows.astype(F32) * scale).astype(BF16)


def first_kernel(
    place_ref, lists_ref, lengths_ref, ids_ref, w_out_ref, read_ref, targets_ref, x_ref, gain_ref, w_ref,
    hot_ref, mix_ref, own_targets_ref, own_ref, inverse_ref, flipped, normed,
):
    part = pl.program_id(0)

    @pl.when(part == 0)
    def _():
        normed[...] = normalise(x_ref, gain_ref)
        inverse_ref[...] = jnp.broadcast_to(
            inverse_root(x_ref[...].astype(F32)), inverse_ref.shape
        )

    own_ref[part] = project_rows(normed[...], w_ref[0], part)

    @pl.when(part == 0)
    def _():
        prepare(
            place_ref, lists_ref, lengths_ref, ids_ref, w_out_ref, read_ref, targets_ref,
            hot_ref, mix_ref, own_targets_ref, own_ref, flipped,
        )


def prepare(
    place_ref, lists_ref, lengths_ref, ids_ref, w_out_ref, read_ref, targets_ref,
    hot_ref, mix_ref, own_targets_ref, own_ref, flipped,
):
    seq_index, core, seq_count = place_ref[0], place_ref[1], place_ref[2]
    side = 2 * core - 1
    half_read = own_targets_ref.shape[0]
    panels, tok_rows = hot_ref.shape[0], hot_ref.shape[1] // 3
    per = tok_rows // BLK
    mix = dot(w_out_ref[...], read_ref[...], NN).T
    flip = jnp.concatenate([mix[half_read:], mix[:half_read]], axis=0)
    mix = jnp.where(core == 0, mix, flip).astype(BF16)
    mix_ref[...] = mix
    readout = mix.shape[0]
    own_ref[3, :readout] = mix
    own_ref[3, readout:] = jnp.zeros((tok_rows - readout, mix.shape[1]), BF16)
    flipped[...] = targets_ref[...].T
    own_targets_ref[...] = flipped[pl.ds(pl.multiple_of(core * half_read, half_read), half_read), :]
    panel = lax.broadcasted_iota(jnp.int32, (panels, tok_rows), 0)
    column = lax.broadcasted_iota(jnp.int32, (1, 2 * tok_rows), 1)
    for t, move in enumerate((0, 1, -1)):
        stretch = seq_index + side * move
        inside = (stretch >= 0) & (stretch < seq_count)
        stretch = jnp.clip(stretch, 0, seq_count - 1)
        ids = ids_ref[:, pl.ds(pl.multiple_of(stretch * tok_rows, tok_rows), tok_rows)]
        hits = (panel == ids) & inside
        hot_ref[:, t * tok_rows : (t + 1) * tok_rows] = jnp.where(hits, 1.0, 0.0).astype(BF16)
        biases = []
        for k in range(3 * per):
            key_block = (seq_index + side * int(KEY_STEP[t, k // per])) * per + k % per
            row = jnp.zeros((1, 2 * tok_rows), F32)
            for b in range(per):
                query_block = stretch * per + b
                live = jnp.logical_not(inside)
                for j in range(LIST):
                    live = live | (
                        (lists_ref[j, query_block] == key_block) & (j < lengths_ref[query_block])
                    )
                off = jnp.where(live, 0.0, DEAD)
                row = jnp.where((column // BLK) % per == b, off, row)
            biases.append(row)
        biases.append(jnp.zeros((16 - 3 * per, 2 * tok_rows), F32))
        own_ref[3, readout + 16 * t : readout + 16 * (t + 1)] = jnp.concatenate(
            biases, axis=0
        ).astype(BF16)


def pair_cols(p):
    return slice(p * PAIR, (p + 1) * PAIR)


def two_heads(tile):
    lane = lax.broadcasted_iota(jnp.int32, tile.shape, 1)
    zero = jnp.zeros_like(tile)
    return jnp.concatenate(
        [jnp.where(lane < HD, tile, zero), jnp.where(lane >= HD, tile, zero)], axis=0
    )


def head_halves(pair_t):
    half = pair_t.shape[1] // 2
    return pair_t[:HD, :half], pair_t[HD:, half:]


def fold_heads(pair_t):
    return jnp.concatenate(head_halves(pair_t), axis=0)


def soften(own_ref, stretch, scores):
    count = scores.shape[0] // BLK
    blocks = [scores[k * BLK : (k + 1) * BLK] for k in range(count)]
    base = own_ref.shape[1] // 2 + 16 * stretch
    bias = own_ref[3, base : base + 16, :].astype(F32)
    biases = [bias[k : k + 1] for k in range(count)]
    tops = [jnp.max(b, axis=0, keepdims=True) - d for b, d in zip(blocks, biases)]
    top = functools.reduce(jnp.maximum, tops)
    expo = [jnp.exp(b - (top + d)) for b, d in zip(blocks, biases)]
    total = functools.reduce(jnp.add, [jnp.sum(e, axis=0, keepdims=True) for e in expo])
    inverse = 1.0 / total
    return jnp.concatenate([(e * inverse).astype(BF16) for e in expo], axis=0)


def start_all(copies):
    for copy in copies:
        copy.start()
    return copies


def wait_all(copies):
    for copy in copies:
        copy.wait()


def near_kernel(
    a1x_ref, b1x_ref, gain_ref, own_hbm, w_hbm,
    a1_hbm, b1_hbm, weight_hbm, keep_ref, send_ref,
    own_ref, w_ref, near_ref, weight_ref, arrived, sent,
):
    rows = own_ref.shape[1]
    pairs = own_ref.shape[2] // PAIR
    order = (1, 2, 0)
    w_in = {c: pltpu.make_async_copy(w_hbm.at[c], w_ref.at[c], arrived.at[c]) for c in order}
    own_in = pltpu.make_async_copy(own_hbm, own_ref, arrived.at[3])
    start_all([w_in[1], own_in, w_in[2], w_in[0]])
    normed = jnp.concatenate([normalise(a1x_ref, gain_ref), normalise(b1x_ref, gain_ref)], axis=0)
    out = []

    def project(c):
        w_in[c].wait()
        near_ref[c] = project_rows(normed, w_ref[c], c)
        for side, target in enumerate((a1_hbm, b1_hbm)):
            source = near_ref.at[c, pl.ds(side * rows, rows)]
            out.append(pltpu.make_async_copy(source, target.at[c], sent.at[2 * c + side]))
            out[-1].start()

    def stack(c, p):
        return jnp.concatenate([own_ref[c, :, pair_cols(p)], near_ref[c, :, pair_cols(p)]], axis=0)

    def score(p):
        return dot(stack(1, p), two_heads(own_ref[0, :, pair_cols(p)]), NT)

    project(1)
    own_in.wait()
    scores = {0: score(0)}
    project(2)
    attended = []
    for p in range(pairs):
        if p + 1 < pairs:
            scores[p + 1] = score(p + 1)
        weight = soften(own_ref, 0, scores[p])
        weight_ref[p, : 3 * rows] = weight
        part = (p, pl.ds(0, 3 * rows))
        out.append(pltpu.make_async_copy(weight_ref.at[part], weight_hbm.at[part], sent.at[6 + p]))
        out[-1].start()
        if p == pairs - 1:
            project(0)
        halves = head_halves(dot(stack(2, p), weight, TN).astype(BF16))
        weight_ref[p, 3 * rows :] = jnp.concatenate(halves, axis=1)
        if p == pairs - 1:
            part = (slice(None), pl.ds(3 * rows, HD))
            out.append(
                pltpu.make_async_copy(weight_ref.at[part], weight_hbm.at[part], sent.at[6 + pairs])
            )
            out[-1].start()
        attended.extend(halves)
    half = keep_ref.shape[0]
    read = dot(own_ref[3, : 2 * half, :], jnp.concatenate(attended, axis=0), NN)
    keep_ref[...] = read[:half]
    send_ref[...] = read[half:]
    wait_all(out)


def side_kernel(
    a2x_ref, b2x_ref, gain_ref, own_hbm, a1_hbm, b1_hbm, w_hbm, weight_hbm,
    own_ref, a1_ref, b1_ref, w_ref, far_ref, weight_ref, arrived, sent,
):
    rows = own_ref.shape[1]
    pairs = own_ref.shape[2] // PAIR
    w_in = [
        pltpu.make_async_copy(w_hbm.at[c + 1], w_ref.at[c], arrived.at[c]) for c in range(2)
    ]
    rows_in = [
        pltpu.make_async_copy(source, target, arrived.at[2 + n])
        for n, (source, target) in enumerate(
            ((own_hbm, own_ref), (a1_hbm, a1_ref), (b1_hbm, b1_ref))
        )
    ]
    start_all([w_in[0]] + rows_in + [w_in[1]])
    normed = jnp.concatenate([normalise(a2x_ref, gain_ref), normalise(b2x_ref, gain_ref)], axis=0)
    near = (a1_ref, b1_ref)
    out = []

    def project(c):
        w_in[c].wait()
        far_ref[c] = dot(normed, w_ref[c], NN).astype(BF16)

    def stack(c, p, side):
        cols = pair_cols(p)
        far = far_ref[c - 1, side * rows : (side + 1) * rows, cols]
        return jnp.concatenate([own_ref[c, :, cols], near[side][c, :, cols], far], axis=0)

    def score(p, side):
        return dot(stack(1, p, side), two_heads(near[side][0, :, pair_cols(p)]), NT)

    project(0)
    wait_all(rows_in)
    jobs = [(p, side) for p in range(pairs) for side in range(2)]
    scores = {jobs[0]: score(*jobs[0])}
    project(1)
    for n, (p, side) in enumerate(jobs):
        if n + 1 < len(jobs):
            scores[jobs[n + 1]] = score(*jobs[n + 1])
        weight = soften(own_ref, 1 + side, scores[p, side])
        weight_ref[p, side, :rows] = weight[:rows]
        halves = head_halves(dot(stack(2, p, side), weight, TN).astype(BF16))
        weight_ref[p, side, rows:] = jnp.concatenate(halves, axis=1)
        out.append(
            pltpu.make_async_copy(weight_ref.at[p, side], weight_hbm.at[p, side], sent.at[n])
        )
        out[-1].start()
    wait_all(out)


def spread_kernel(keep_ref, got_ref, out_ref):
    rows = (keep_ref[...] + got_ref[...]).astype(BF16)
    for s in range(out_ref.shape[0]):
        out_ref[s] = rows


def pool_kernel(steps, rows_ref, ids_ref, targets_ref, out_ref, counts_ref, sums):
    step = pl.program_id(0)
    half_read, panels = out_ref.shape
    count, _, tok_rows = rows_ref.shape

    @pl.when(step == 0)
    def _():
        sums[...] = jnp.zeros_like(sums)

    panel = lax.broadcasted_iota(jnp.int32, (panels, count * tok_rows), 0)
    hits = jnp.where(panel == ids_ref[...], 1.0, 0.0).astype(BF16)
    rows = jnp.concatenate([rows_ref[s] for s in range(count)], axis=1)
    rows = jnp.concatenate([rows, jnp.ones((16, count * tok_rows), BF16)], axis=0)
    sums[...] += dot(rows, hits, NT)

    @pl.when(step == steps - 1)
    def _():
        counts = sums[half_read : half_read + 1]
        out_ref[...] = sums[:half_read] / counts - targets_ref[...]
        counts_ref[...] = counts


def back_kernel(
    core_ref, resid_a_ref, resid_b_ref, counts_ref, hot_ref, mix_ref, gain_ref, *refs
):
    sources, (keep_ref, send_ref, stat_ref, loss_ref) = refs[:7], refs[7:11]
    buffers, arrived = refs[11:18], refs[18]
    own_ref, a1_ref, b1_ref, own_w_ref, side_w_ref, w_ref, tokens_ref = buffers
    pairs = own_ref.shape[2] // PAIR
    slots = iter(range(arrived.shape[0]))

    def fetch(n, index):
        return pltpu.make_async_copy(
            sources[n].at[index], buffers[n].at[index], arrived.at[next(slots)]
        )

    values_in = [fetch(n, pl.ds(2, 1)) for n in range(3)]
    weight_in = [[fetch(n, pl.ds(p, 1)) for n in (3, 4)] for p in range(pairs)]
    rest_in = [fetch(n, pl.ds(0, 2)) for n in range(3)]
    last_in = [fetch(5, pl.ds(0, 3)), fetch(6, pl.ds(0, tokens_ref.shape[0]))]
    start_all(values_in + weight_in[0] + rest_in)
    start_all([copy for pair in weight_in[1:] for copy in pair] + last_in)
    own_rows = own_ref.shape[1]
    residual = jnp.concatenate([resid_a_ref[...], resid_b_ref[...]], axis=0)
    loss_ref[...] = jnp.broadcast_to(
        jnp.sum(counts_ref[...] * residual * residual, keepdims=True), loss_ref.shape
    )
    panel_grad = dot(mix_ref[...].astype(F32), residual, TN, lax.Precision.HIGHEST).astype(BF16)
    out_grad = dot(panel_grad, hot_ref[...], NN).astype(BF16)
    stretches = (own_ref, a1_ref, b1_ref)

    def tile_of(p, t):
        return out_grad[pair_cols(p), t * own_rows : (t + 1) * own_rows]

    def open_job(p, t):
        values = jnp.concatenate(
            [r[2, :, pair_cols(p)] for r in (stretches if t == 0 else stretches[:1])], axis=0
        )
        tile = tile_of(p, t)
        none = jnp.zeros((HD, own_rows), BF16)
        grad = jnp.concatenate(
            [
                jnp.concatenate([tile[:HD], none], axis=0),
                jnp.concatenate([none, tile[HD:]], axis=0),
            ],
            axis=1,
        )
        return grad, dot(values, grad, NN)

    def score_job(p, t, change):
        pack = own_w_ref[p] if t == 0 else side_w_ref[p, t - 1]
        weight, attended = pack[:-HD], pack[-HD:]
        tile = tile_of(p, t)
        flat_tile = jnp.concatenate([tile[:HD], tile[HD:]], axis=1)
        delta = jnp.sum(flat_tile.astype(F32) * attended.astype(F32), axis=0, keepdims=True)
        return (weight.astype(F32) * (change - delta)).astype(BF16)

    def query_of(p, score):
        keys = jnp.concatenate([r[1, :, pair_cols(p)] for r in stretches], axis=0)
        grad_query = fold_heads(dot(keys, score, TN)) * SCALE
        return grad_query.T.astype(BF16)

    def close_job(p, t, grad, score):
        weight = own_w_ref[p, :own_rows] if t == 0 else side_w_ref[p, t - 1, :own_rows]
        queries = two_heads(stretches[t][0, :, pair_cols(p)])
        return dot(score[:own_rows], queries, NN), dot(weight, grad, NT)

    wait_all(values_in)
    jobs = [(p, t) for p in range(pairs) for t in range(3)]
    opened = open_job(*jobs[0])
    grad_proj = []
    for n, (p, t) in enumerate(jobs):
        grad, change = opened
        if n + 1 < len(jobs):
            opened = open_job(*jobs[n + 1])
        if t == 0:
            wait_all(weight_in[p])
        score = score_job(p, t, change)
        if n == 0:
            wait_all(rest_in)
        if t == 0:
            grad_query = query_of(p, score)
            grad_key, grad_value = close_job(p, t, grad, score)
        else:
            more_key, more_value = close_job(p, t, grad, score)
            grad_key, grad_value = grad_key + more_key, grad_value + more_value
        if t == 2:
            grad_proj.append((grad_query, grad_key.astype(BF16), grad_value.astype(BF16)))
    flat = jnp.concatenate([grad_proj[p][c] for c in range(3) for p in range(pairs)], axis=1)
    wait_all(last_in)
    half = keep_ref.shape[1]
    row_sum = jnp.zeros((own_rows, 1), F32)
    core = core_ref[0]
    parts = []
    for h in (core, 1 - core):
        rows = pl.ds(pl.multiple_of(h * half, half), half)
        w_part = jnp.concatenate([w_ref[c, rows, :] for c in range(3)], axis=1)
        parts.append(dot(flat, w_part, NT))
        scaled = tokens_ref[:, rows].astype(F32) * gain_ref[:, rows]
        row_sum += jnp.sum(scaled * parts[-1], axis=-1, keepdims=True)
    keep_ref[...] = parts[0]
    send_ref[:, :half] = parts[1].astype(BF16)
    high = row_sum.astype(BF16).astype(F32)
    lane = lax.broadcasted_iota(jnp.int32, (own_rows, BLK), 1)
    send_ref[:, half:] = jnp.where(lane < HD, high, row_sum - high).astype(BF16)
    stat_ref[...] = jnp.broadcast_to(row_sum, stat_ref.shape)


def final_kernel(
    core_ref, keep_ref, got_ref, stat_ref, inverse_ref, tokens_ref, gain_ref, out_ref
):
    half = keep_ref.shape[1]
    cols = pl.ds(pl.multiple_of(core_ref[0] * half, half), half)
    got_sum = got_ref[:, half : half + 1].astype(F32) + got_ref[:, half + HD : half + HD + 1].astype(F32)
    row_sum = stat_ref[:, :1] + got_sum
    inverse = inverse_ref[:, :1]
    grad_normed = keep_ref[...] + got_ref[:, :half].astype(F32)
    shrink = row_sum * (inverse * inverse * inverse) * (0.5 / half)
    out_ref[...] = (
        gain_ref[:, cols] * grad_normed * inverse - tokens_ref[:, cols].astype(F32) * shrink
    )


def whole_spec(shape):
    return pl.BlockSpec(shape, lambda p: (0,) * len(shape))


SMEM_SPEC = pl.BlockSpec(memory_space=pltpu.SMEM)


def local(
    tokens, norm_gain, w_qkv, w_out, readout_weight, targets, key_blocks, list_len, voxel_panel
):
    tok_rows, width = tokens.shape
    cols = w_qkv.shape[2]
    pairs = cols // PAIR
    panels, readout = targets.shape
    half_read = readout // 2
    half_width = width // 2
    seq_count = lax.axis_size("seq")
    seq_index = lax.axis_index("seq")
    core = lax.axis_index("head")
    side_step = 2 * core - 1
    all_tokens = voxel_panel.shape[0]
    per = tok_rows // BLK
    core_swap = [(0, 1), (1, 0)]

    def shifted(far):
        return [
            (2 * s, 2 * (s + far)) for s in range(seq_count - far)
        ] + [(2 * (s + far) + 1, 2 * s + 1) for s in range(seq_count - far)]

    a1_tokens = lax.ppermute(tokens, ("seq", "head"), shifted(1))
    a2_tokens = lax.ppermute(tokens, ("seq", "head"), shifted(2))

    gain = norm_gain.reshape(1, width)
    flat_ids = voxel_panel.reshape(1, all_tokens)
    place = jnp.stack([seq_index, core, jnp.int32(seq_count)]).astype(jnp.int32)
    vmem = pl.BlockSpec(memory_space=pltpu.VMEM)
    whole_tokens = whole_spec((tok_rows, width))
    whole_gain = whole_spec((1, width))
    hot, mix, own_targets, own, inverse = pl.pallas_call(
        first_kernel,
        grid=(3,),
        in_specs=[SMEM_SPEC] * 3
        + [
            whole_spec((1, all_tokens)),
            whole_spec(w_out.shape),
            whole_spec(readout_weight.shape),
            whole_spec(targets.shape),
            whole_tokens,
            whole_gain,
            pl.BlockSpec((1, width, cols), lambda c: (c, 0, 0)),
        ],
        out_specs=[
            whole_spec((panels, 3 * tok_rows)),
            whole_spec((readout, cols)),
            whole_spec((half_read, panels)),
            whole_spec((4, tok_rows, cols)),
            whole_spec((tok_rows, BLK)),
        ],
        out_shape=[
            jax.ShapeDtypeStruct((panels, 3 * tok_rows), BF16),
            jax.ShapeDtypeStruct((readout, cols), BF16),
            jax.ShapeDtypeStruct((half_read, panels), F32),
            jax.ShapeDtypeStruct((4, tok_rows, cols), BF16),
            jax.ShapeDtypeStruct((tok_rows, BLK), F32),
        ],
        scratch_shapes=[pltpu.VMEM((readout, panels), F32), pltpu.VMEM((tok_rows, width), BF16)],
        compiler_params=params("arbitrary", mib=60),
        cost_estimate=pl.CostEstimate(flops=2**31, bytes_accessed=6 * MIB, transcendentals=0),
        name="first",
    )(
        place, key_blocks.T, list_len, flat_ids, w_out, readout_weight, targets, tokens, gain, w_qkv
    )

    a1_tokens, own, mix, own_targets, hot = lax.optimization_barrier(
        (a1_tokens, own, mix, own_targets, hot)
    )
    b1_tokens = lax.ppermute(a1_tokens, "head", core_swap)
    a2_tokens, b1_tokens = lax.optimization_barrier((a2_tokens, b1_tokens))
    b2_tokens = lax.ppermute(a2_tokens, "head", core_swap)
    hbm = pl.BlockSpec(memory_space=pl.ANY)
    a1, b1, own_weight, read_keep, read_send = pl.pallas_call(
        near_kernel,
        in_specs=[vmem] * 3 + [hbm] * 2,
        out_specs=[hbm] * 3 + [vmem] * 2,
        out_shape=[
            jax.ShapeDtypeStruct((3, tok_rows, cols), BF16),
            jax.ShapeDtypeStruct((3, tok_rows, cols), BF16),
            jax.ShapeDtypeStruct((pairs, 3 * tok_rows + HD, 2 * tok_rows), BF16),
            jax.ShapeDtypeStruct((half_read, tok_rows), F32),
            jax.ShapeDtypeStruct((half_read, tok_rows), F32),
        ],
        scratch_shapes=[
            pltpu.VMEM((4, tok_rows, cols), BF16),
            pltpu.VMEM((3, width, cols), BF16),
            pltpu.VMEM((3, 2 * tok_rows, cols), BF16),
            pltpu.VMEM((pairs, 3 * tok_rows + HD, 2 * tok_rows), BF16),
            pltpu.SemaphoreType.DMA((4,)),
            pltpu.SemaphoreType.DMA((7 + pairs,)),
        ],
        compiler_params=params(),
        cost_estimate=pl.CostEstimate(flops=2**33, bytes_accessed=8 * MIB, transcendentals=0),
        name="near",
    )(a1_tokens, b1_tokens, gain, own, w_qkv)

    read_send, b2_tokens = lax.optimization_barrier((read_send, b2_tokens))
    read_got = lax.ppermute(read_send, "head", core_swap)
    spread = pl.pallas_call(
        spread_kernel,
        out_shape=jax.ShapeDtypeStruct((seq_count, half_read, tok_rows), BF16),
        compiler_params=params(),
        name="spread",
    )(read_keep, read_got)
    all_rows = lax.all_to_all(spread, "seq", 0, 0)

    side_weight = pl.pallas_call(
        side_kernel,
        in_specs=[vmem] * 3 + [hbm] * 4,
        out_specs=hbm,
        out_shape=jax.ShapeDtypeStruct((pairs, 2, tok_rows + HD, 2 * tok_rows), BF16),
        scratch_shapes=[pltpu.VMEM((4, tok_rows, cols), BF16)]
        + [pltpu.VMEM((3, tok_rows, cols), BF16)] * 2
        + [
            pltpu.VMEM((2, width, cols), BF16),
            pltpu.VMEM((2, 2 * tok_rows, cols), BF16),
            pltpu.VMEM((pairs, 2, tok_rows + HD, 2 * tok_rows), BF16),
            pltpu.SemaphoreType.DMA((5,)),
            pltpu.SemaphoreType.DMA((2 * pairs,)),
        ],
        compiler_params=params(),
        cost_estimate=pl.CostEstimate(flops=2**33, bytes_accessed=8 * MIB, transcendentals=0),
        name="attend_sides",
    )(a2_tokens, b2_tokens, gain, own, a1, b1, w_qkv)
    all_rows, side_weight = lax.optimization_barrier((all_rows, side_weight))

    batch = min(seq_count, 8)
    pool_steps = seq_count // batch
    resid_a, counts = pl.pallas_call(
        functools.partial(pool_kernel, pool_steps),
        grid=(pool_steps,),
        in_specs=[
            pl.BlockSpec((batch, half_read, tok_rows), lambda s: (s, 0, 0)),
            pl.BlockSpec((1, batch * tok_rows), lambda s: (0, s)),
            whole_spec((half_read, panels)),
        ],
        out_specs=[whole_spec((half_read, panels)), whole_spec((1, panels))],
        out_shape=[
            jax.ShapeDtypeStruct((half_read, panels), F32),
            jax.ShapeDtypeStruct((1, panels), F32),
        ],
        scratch_shapes=[pltpu.VMEM((half_read + 16, panels), F32)],
        compiler_params=params("arbitrary"),
        name="pool",
    )(all_rows, flat_ids, own_targets)
    resid_b = lax.ppermute(resid_a, "head", core_swap)

    core_index = place[1:2]
    sources = (own, a1, b1, own_weight, side_weight, w_qkv, tokens)
    keep, send, stats, loss = pl.pallas_call(
        back_kernel,
        in_specs=[SMEM_SPEC] + [vmem] * 6 + [hbm] * len(sources),
        out_specs=[vmem] * 4,
        out_shape=[
            jax.ShapeDtypeStruct((tok_rows, half_width), F32),
            jax.ShapeDtypeStruct((tok_rows, half_width + BLK), BF16),
            jax.ShapeDtypeStruct((tok_rows, BLK), F32),
            jax.ShapeDtypeStruct((1, BLK), F32),
        ],
        scratch_shapes=[pltpu.VMEM(a.shape, a.dtype) for a in sources]
        + [pltpu.SemaphoreType.DMA((8 + 2 * pairs,))],
        compiler_params=params(),
        name="back",
    )(core_index, resid_a, resid_b, counts, hot, mix, gain, *sources)
    got = lax.ppermute(send, "head", core_swap)
    loss_mean = 0.5 * loss[0, :1] / (all_tokens * readout)
    gradient = pl.pallas_call(
        final_kernel,
        in_specs=[SMEM_SPEC] + [vmem] * 6,
        out_shape=jax.ShapeDtypeStruct((tok_rows, half_width), F32),
        compiler_params=params(),
        name="final",
    )(core_index, keep, got, stats, inverse, tokens, gain)
    return (gradient, loss_mean)


def solution(mesh):
    return jax.shard_map(
        local,
        mesh=mesh,
        in_specs=(
            P(("groups", "seq"), None),
            P(),
            P(None, None, "head"),
            P("head", None),
            P(),
            P("groups", None),
            P("groups", None),
            P("groups"),
            P("groups", None),
        ),
        out_specs=(P(("groups", "seq"), "head"), P("groups")),
        check_vma=False,
    )
```

```python
import functools
import math

import jax
import jax.numpy as jnp
import numpy as np
from jax import lax
from jax.experimental import pallas as pl
from jax.experimental.pallas import tpu as pltpu
from jax.sharding import PartitionSpec as P

HD = 64
BLK = 128
LIST = 4
PAIR = 2 * HD
F32 = jnp.float32
BF16 = jnp.bfloat16
DEAD = 1e30
SCALE = 1.0 / math.sqrt(HD)
KEY_STEP = np.array([[0, 1, -1], [0, 1, 2], [0, -1, -2]], np.int32)
MIB = 1024 * 1024

NN = (((1,), (0,)), ((), ()))
NT = (((1,), (1,)), ((), ()))
TN = (((0,), (0,)), ((), ()))


def dot(a, b, dims, precision=None):
    return lax.dot_general(a, b, dims, precision=precision, preferred_element_type=F32)


def params(*semantics, mib=52):
    return pltpu.CompilerParams(vmem_limit_bytes=mib * MIB, dimension_semantics=semantics or None)


def inverse_root(inputs):
    return 1.0 / jnp.sqrt(jnp.mean(inputs * inputs, axis=-1, keepdims=True) + 1e-05)


def normalise(x_ref, gain_ref):
    inputs = x_ref[...].astype(F32)
    return (inputs * gain_ref[...] * inverse_root(inputs)).astype(BF16)


def project_rows(normed, w_part, part):
    rows = dot(normed, w_part, NN).astype(BF16)
    scale = jnp.where(part == 0, SCALE, 1.0)
    return (rows.astype(F32) * scale).astype(BF16)


def first_kernel(
    place_ref, lists_ref, lengths_ref, ids_ref, w_out_ref, read_ref, targets_ref, x_ref, gain_ref, w_ref,
    hot_ref, mix_ref, own_targets_ref, own_ref, inverse_ref, flipped, normed,
):
    part = pl.program_id(0)

    @pl.when(part == 0)
    def _():
        normed[...] = normalise(x_ref, gain_ref)
        inverse_ref[...] = jnp.broadcast_to(
            inverse_root(x_ref[...].astype(F32)), inverse_ref.shape
        )

    own_ref[part] = project_rows(normed[...], w_ref[0], part)

    @pl.when(part == 0)
    def _():
        prepare(
            place_ref, lists_ref, lengths_ref, ids_ref, w_out_ref, read_ref, targets_ref,
            hot_ref, mix_ref, own_targets_ref, own_ref, flipped,
        )


def prepare(
    place_ref, lists_ref, lengths_ref, ids_ref, w_out_ref, read_ref, targets_ref,
    hot_ref, mix_ref, own_targets_ref, own_ref, flipped,
):
    seq_index, core, seq_count = place_ref[0], place_ref[1], place_ref[2]
    side = 2 * core - 1
    half_read = own_targets_ref.shape[0]
    panels, tok_rows = hot_ref.shape[0], hot_ref.shape[1] // 3
    per = tok_rows // BLK
    mix = dot(w_out_ref[...], read_ref[...], NN).T
    flip = jnp.concatenate([mix[half_read:], mix[:half_read]], axis=0)
    mix = jnp.where(core == 0, mix, flip).astype(BF16)
    mix_ref[...] = mix
    readout = mix.shape[0]
    own_ref[3, :readout] = mix
    own_ref[3, readout:] = jnp.zeros((tok_rows - readout, mix.shape[1]), BF16)
    flipped[...] = targets_ref[...].T
    own_targets_ref[...] = flipped[pl.ds(pl.multiple_of(core * half_read, half_read), half_read), :]
    panel = lax.broadcasted_iota(jnp.int32, (panels, tok_rows), 0)
    column = lax.broadcasted_iota(jnp.int32, (1, 2 * tok_rows), 1)
    for t, move in enumerate((0, 1, -1)):
        stretch = seq_index + side * move
        inside = (stretch >= 0) & (stretch < seq_count)
        stretch = jnp.clip(stretch, 0, seq_count - 1)
        ids = ids_ref[:, pl.ds(pl.multiple_of(stretch * tok_rows, tok_rows), tok_rows)]
        hits = (panel == ids) & inside
        hot_ref[:, t * tok_rows : (t + 1) * tok_rows] = jnp.where(hits, 1.0, 0.0).astype(BF16)
        biases = []
        for k in range(3 * per):
            key_block = (seq_index + side * int(KEY_STEP[t, k // per])) * per + k % per
            row = jnp.zeros((1, 2 * tok_rows), F32)
            for b in range(per):
                query_block = stretch * per + b
                live = jnp.logical_not(inside)
                for j in range(LIST):
                    live = live | (
                        (lists_ref[j, query_block] == key_block) & (j < lengths_ref[query_block])
                    )
                off = jnp.where(live, 0.0, DEAD)
                row = jnp.where((column // BLK) % per == b, off, row)
            biases.append(row)
        biases.append(jnp.zeros((16 - 3 * per, 2 * tok_rows), F32))
        own_ref[3, readout + 16 * t : readout + 16 * (t + 1)] = jnp.concatenate(
            biases, axis=0
        ).astype(BF16)


def pair_cols(p):
    return slice(p * PAIR, (p + 1) * PAIR)


def two_heads(tile):
    lane = lax.broadcasted_iota(jnp.int32, tile.shape, 1)
    zero = jnp.zeros_like(tile)
    return jnp.concatenate(
        [jnp.where(lane < HD, tile, zero), jnp.where(lane >= HD, tile, zero)], axis=0
    )


def head_halves(pair_t):
    half = pair_t.shape[1] // 2
    return pair_t[:HD, :half], pair_t[HD:, half:]


def fold_heads(pair_t):
    return jnp.concatenate(head_halves(pair_t), axis=0)


def soften(own_ref, stretch, scores):
    count = scores.shape[0] // BLK
    base = own_ref.shape[1] // 2 + 16 * stretch
    bias = own_ref[3, base : base + 16, :].astype(F32)
    weights = []
    for first in range(0, scores.shape[1], BLK):
        cols = slice(first, first + BLK)
        blocks = [scores[k * BLK : (k + 1) * BLK, cols] for k in range(count)]
        biases = [bias[k : k + 1, cols] for k in range(count)]
        tops = [jnp.max(b, axis=0, keepdims=True) - d for b, d in zip(blocks, biases)]
        top = functools.reduce(jnp.maximum, tops)
        expo = [jnp.exp(b - (top + d)) for b, d in zip(blocks, biases)]
        total = functools.reduce(jnp.add, [jnp.sum(e, axis=0, keepdims=True) for e in expo])
        inverse = 1.0 / total
        weights.append(jnp.concatenate([(e * inverse).astype(BF16) for e in expo], axis=0))
    return jnp.concatenate(weights, axis=1)


def start_all(copies):
    for copy in copies:
        copy.start()
    return copies


def wait_all(copies):
    for copy in copies:
        copy.wait()


def near_kernel(
    a1x_ref, b1x_ref, gain_ref, own_hbm, w_hbm,
    a1_hbm, b1_hbm, weight_hbm, keep_ref, send_ref,
    own_ref, w_ref, near_ref, weight_ref, arrived, sent,
):
    rows = own_ref.shape[1]
    pairs = own_ref.shape[2] // PAIR
    order = (1, 2, 0)
    w_in = {c: pltpu.make_async_copy(w_hbm.at[c], w_ref.at[c], arrived.at[c]) for c in order}
    own_in = pltpu.make_async_copy(own_hbm, own_ref, arrived.at[3])
    start_all([w_in[1], own_in, w_in[2], w_in[0]])
    normed = jnp.concatenate([normalise(a1x_ref, gain_ref), normalise(b1x_ref, gain_ref)], axis=0)
    out = []

    def project(c):
        w_in[c].wait()
        near_ref[c] = project_rows(normed, w_ref[c], c)
        for side, target in enumerate((a1_hbm, b1_hbm)):
            source = near_ref.at[c, pl.ds(side * rows, rows)]
            out.append(pltpu.make_async_copy(source, target.at[c], sent.at[2 * c + side]))
            out[-1].start()

    def stack(c, p):
        return jnp.concatenate([own_ref[c, :, pair_cols(p)], near_ref[c, :, pair_cols(p)]], axis=0)

    def score(p):
        return dot(stack(1, p), two_heads(own_ref[0, :, pair_cols(p)]), NT)

    project(1)
    own_in.wait()
    scores = {0: score(0)}
    project(2)
    attended = []
    for p in range(pairs):
        if p + 1 < pairs:
            scores[p + 1] = score(p + 1)
        weight = soften(own_ref, 0, scores[p])
        weight_ref[p, : 3 * rows] = weight
        part = (p, pl.ds(0, 3 * rows))
        out.append(pltpu.make_async_copy(weight_ref.at[part], weight_hbm.at[part], sent.at[6 + p]))
        out[-1].start()
        if p == pairs - 1:
            project(0)
        halves = head_halves(dot(stack(2, p), weight, TN).astype(BF16))
        weight_ref[p, 3 * rows :] = jnp.concatenate(halves, axis=1)
        if p == pairs - 1:
            part = (slice(None), pl.ds(3 * rows, HD))
            out.append(
                pltpu.make_async_copy(weight_ref.at[part], weight_hbm.at[part], sent.at[6 + pairs])
            )
            out[-1].start()
        attended.extend(halves)
    half = keep_ref.shape[0]
    read = dot(own_ref[3, : 2 * half, :], jnp.concatenate(attended, axis=0), NN)
    keep_ref[...] = read[:half]
    send_ref[...] = read[half:]
    wait_all(out)


def side_kernel(
    a2x_ref, b2x_ref, gain_ref, own_hbm, a1_hbm, b1_hbm, w_hbm, weight_hbm,
    own_ref, a1_ref, b1_ref, w_ref, far_ref, weight_ref, arrived, sent,
):
    rows = own_ref.shape[1]
    pairs = own_ref.shape[2] // PAIR
    w_in = [
        pltpu.make_async_copy(w_hbm.at[c + 1], w_ref.at[c], arrived.at[c]) for c in range(2)
    ]
    rows_in = [
        pltpu.make_async_copy(source, target, arrived.at[2 + n])
        for n, (source, target) in enumerate(
            ((own_hbm, own_ref), (a1_hbm, a1_ref), (b1_hbm, b1_ref))
        )
    ]
    start_all([w_in[0]] + rows_in + [w_in[1]])
    normed = jnp.concatenate([normalise(a2x_ref, gain_ref), normalise(b2x_ref, gain_ref)], axis=0)
    near = (a1_ref, b1_ref)
    out = []

    def project(c):
        w_in[c].wait()
        far_ref[c] = dot(normed, w_ref[c], NN).astype(BF16)

    def stack(c, p, side):
        cols = pair_cols(p)
        far = far_ref[c - 1, side * rows : (side + 1) * rows, cols]
        return jnp.concatenate([own_ref[c, :, cols], near[side][c, :, cols], far], axis=0)

    def score(p, side):
        return dot(stack(1, p, side), two_heads(near[side][0, :, pair_cols(p)]), NT)

    project(0)
    wait_all(rows_in)
    jobs = [(p, side) for p in range(pairs) for side in range(2)]
    scores = {jobs[0]: score(*jobs[0])}
    project(1)
    for n, (p, side) in enumerate(jobs):
        if n + 1 < len(jobs):
            scores[jobs[n + 1]] = score(*jobs[n + 1])
        weight = soften(own_ref, 1 + side, scores[p, side])
        weight_ref[p, side, :rows] = weight[:rows]
        halves = head_halves(dot(stack(2, p, side), weight, TN).astype(BF16))
        weight_ref[p, side, rows:] = jnp.concatenate(halves, axis=1)
        out.append(
            pltpu.make_async_copy(weight_ref.at[p, side], weight_hbm.at[p, side], sent.at[n])
        )
        out[-1].start()
    wait_all(out)


def spread_kernel(keep_ref, got_ref, out_ref):
    rows = (keep_ref[...] + got_ref[...]).astype(BF16)
    for s in range(out_ref.shape[0]):
        out_ref[s] = rows


def pool_kernel(steps, rows_ref, ids_ref, targets_ref, out_ref, counts_ref, sums):
    step = pl.program_id(0)
    half_read, panels = out_ref.shape
    count, _, tok_rows = rows_ref.shape

    @pl.when(step == 0)
    def _():
        sums[...] = jnp.zeros_like(sums)

    panel = lax.broadcasted_iota(jnp.int32, (panels, count * tok_rows), 0)
    hits = jnp.where(panel == ids_ref[...], 1.0, 0.0).astype(BF16)
    rows = jnp.concatenate([rows_ref[s] for s in range(count)], axis=1)
    rows = jnp.concatenate([rows, jnp.ones((16, count * tok_rows), BF16)], axis=0)
    sums[...] += dot(rows, hits, NT)

    @pl.when(step == steps - 1)
    def _():
        counts = sums[half_read : half_read + 1]
        out_ref[...] = sums[:half_read] / counts - targets_ref[...]
        counts_ref[...] = counts


def back_kernel(
    core_ref, resid_a_ref, resid_b_ref, counts_ref, hot_ref, mix_ref, gain_ref, *refs
):
    sources, (keep_ref, send_ref, stat_ref, loss_ref) = refs[:7], refs[7:11]
    buffers, arrived = refs[11:18], refs[18]
    own_ref, a1_ref, b1_ref, own_w_ref, side_w_ref, w_ref, tokens_ref = buffers
    pairs = own_ref.shape[2] // PAIR
    slots = iter(range(arrived.shape[0]))

    def fetch(n, index):
        return pltpu.make_async_copy(
            sources[n].at[index], buffers[n].at[index], arrived.at[next(slots)]
        )

    values_in = [fetch(n, pl.ds(2, 1)) for n in range(3)]
    weight_in = [[fetch(n, pl.ds(p, 1)) for n in (3, 4)] for p in range(pairs)]
    rest_in = [fetch(n, pl.ds(0, 2)) for n in range(3)]
    last_in = [fetch(5, pl.ds(0, 3)), fetch(6, pl.ds(0, tokens_ref.shape[0]))]
    start_all(values_in + weight_in[0] + rest_in)
    start_all([copy for pair in weight_in[1:] for copy in pair] + last_in)
    own_rows = own_ref.shape[1]
    residual = jnp.concatenate([resid_a_ref[...], resid_b_ref[...]], axis=0)
    loss_ref[...] = jnp.broadcast_to(
        jnp.sum(counts_ref[...] * residual * residual, keepdims=True), loss_ref.shape
    )
    panel_grad = dot(mix_ref[...].astype(F32), residual, TN, lax.Precision.HIGHEST).astype(BF16)
    out_grad = dot(panel_grad, hot_ref[...], NN).astype(BF16)
    stretches = (own_ref, a1_ref, b1_ref)

    def tile_of(p, t):
        return out_grad[pair_cols(p), t * own_rows : (t + 1) * own_rows]

    def open_job(p, t):
        values = jnp.concatenate(
            [r[2, :, pair_cols(p)] for r in (stretches if t == 0 else stretches[:1])], axis=0
        )
        tile = tile_of(p, t)
        none = jnp.zeros((HD, own_rows), BF16)
        grad = jnp.concatenate(
            [
                jnp.concatenate([tile[:HD], none], axis=0),
                jnp.concatenate([none, tile[HD:]], axis=0),
            ],
            axis=1,
        )
        return grad, dot(values, grad, NN)

    def score_job(p, t, change):
        pack = own_w_ref[p] if t == 0 else side_w_ref[p, t - 1]
        weight, attended = pack[:-HD], pack[-HD:]
        tile = tile_of(p, t)
        flat_tile = jnp.concatenate([tile[:HD], tile[HD:]], axis=1)
        delta = jnp.sum(flat_tile.astype(F32) * attended.astype(F32), axis=0, keepdims=True)
        return (weight.astype(F32) * (change - delta)).astype(BF16)

    def query_of(p, score):
        keys = jnp.concatenate([r[1, :, pair_cols(p)] for r in stretches], axis=0)
        grad_query = fold_heads(dot(keys, score, TN)) * SCALE
        return grad_query.T.astype(BF16)

    def close_job(p, t, grad, score):
        weight = own_w_ref[p, :own_rows] if t == 0 else side_w_ref[p, t - 1, :own_rows]
        queries = two_heads(stretches[t][0, :, pair_cols(p)])
        return dot(score[:own_rows], queries, NN), dot(weight, grad, NT)

    wait_all(values_in)
    jobs = [(p, t) for p in range(pairs) for t in range(3)]
    opened = open_job(*jobs[0])
    grad_proj = []
    for n, (p, t) in enumerate(jobs):
        grad, change = opened
        if n + 1 < len(jobs):
            opened = open_job(*jobs[n + 1])
        if t == 0:
            wait_all(weight_in[p])
        score = score_job(p, t, change)
        if n == 0:
            wait_all(rest_in)
        if t == 0:
            grad_query = query_of(p, score)
            grad_key, grad_value = close_job(p, t, grad, score)
        else:
            more_key, more_value = close_job(p, t, grad, score)
            grad_key, grad_value = grad_key + more_key, grad_value + more_value
        if t == 2:
            grad_proj.append((grad_query, grad_key.astype(BF16), grad_value.astype(BF16)))
    flat = jnp.concatenate([grad_proj[p][c] for c in range(3) for p in range(pairs)], axis=1)
    wait_all(last_in)
    half = keep_ref.shape[1]
    row_sum = jnp.zeros((own_rows, 1), F32)
    core = core_ref[0]
    parts = []
    for h in (core, 1 - core):
        rows = pl.ds(pl.multiple_of(h * half, half), half)
        w_part = jnp.concatenate([w_ref[c, rows, :] for c in range(3)], axis=1)
        parts.append(dot(flat, w_part, NT))
        scaled = tokens_ref[:, rows].astype(F32) * gain_ref[:, rows]
        row_sum += jnp.sum(scaled * parts[-1], axis=-1, keepdims=True)
    keep_ref[...] = parts[0]
    send_ref[:, :half] = parts[1].astype(BF16)
    high = row_sum.astype(BF16).astype(F32)
    lane = lax.broadcasted_iota(jnp.int32, (own_rows, BLK), 1)
    send_ref[:, half:] = jnp.where(lane < HD, high, row_sum - high).astype(BF16)
    stat_ref[...] = jnp.broadcast_to(row_sum, stat_ref.shape)


def final_kernel(
    core_ref, keep_ref, got_ref, stat_ref, inverse_ref, tokens_ref, gain_ref, out_ref
):
    half = keep_ref.shape[1]
    cols = pl.ds(pl.multiple_of(core_ref[0] * half, half), half)
    got_sum = got_ref[:, half : half + 1].astype(F32) + got_ref[:, half + HD : half + HD + 1].astype(F32)
    row_sum = stat_ref[:, :1] + got_sum
    inverse = inverse_ref[:, :1]
    grad_normed = keep_ref[...] + got_ref[:, :half].astype(F32)
    shrink = row_sum * (inverse * inverse * inverse) * (0.5 / half)
    out_ref[...] = (
        gain_ref[:, cols] * grad_normed * inverse - tokens_ref[:, cols].astype(F32) * shrink
    )


def whole_spec(shape):
    return pl.BlockSpec(shape, lambda p: (0,) * len(shape))


SMEM_SPEC = pl.BlockSpec(memory_space=pltpu.SMEM)


def local(
    tokens, norm_gain, w_qkv, w_out, readout_weight, targets, key_blocks, list_len, voxel_panel
):
    tok_rows, width = tokens.shape
    cols = w_qkv.shape[2]
    pairs = cols // PAIR
    panels, readout = targets.shape
    half_read = readout // 2
    half_width = width // 2
    seq_count = lax.axis_size("seq")
    seq_index = lax.axis_index("seq")
    core = lax.axis_index("head")
    side_step = 2 * core - 1
    all_tokens = voxel_panel.shape[0]
    per = tok_rows // BLK
    core_swap = [(0, 1), (1, 0)]

    def shifted(far):
        return [
            (2 * s, 2 * (s + far)) for s in range(seq_count - far)
        ] + [(2 * (s + far) + 1, 2 * s + 1) for s in range(seq_count - far)]

    a1_tokens = lax.ppermute(tokens, ("seq", "head"), shifted(1))
    a2_tokens = lax.ppermute(tokens, ("seq", "head"), shifted(2))

    gain = norm_gain.reshape(1, width)
    flat_ids = voxel_panel.reshape(1, all_tokens)
    place = jnp.stack([seq_index, core, jnp.int32(seq_count)]).astype(jnp.int32)
    vmem = pl.BlockSpec(memory_space=pltpu.VMEM)
    whole_tokens = whole_spec((tok_rows, width))
    whole_gain = whole_spec((1, width))
    hot, mix, own_targets, own, inverse = pl.pallas_call(
        first_kernel,
        grid=(3,),
        in_specs=[SMEM_SPEC] * 3
        + [
            whole_spec((1, all_tokens)),
            whole_spec(w_out.shape),
            whole_spec(readout_weight.shape),
            whole_spec(targets.shape),
            whole_tokens,
            whole_gain,
            pl.BlockSpec((1, width, cols), lambda c: (c, 0, 0)),
        ],
        out_specs=[
            whole_spec((panels, 3 * tok_rows)),
            whole_spec((readout, cols)),
            whole_spec((half_read, panels)),
            whole_spec((4, tok_rows, cols)),
            whole_spec((tok_rows, BLK)),
        ],
        out_shape=[
            jax.ShapeDtypeStruct((panels, 3 * tok_rows), BF16),
            jax.ShapeDtypeStruct((readout, cols), BF16),
            jax.ShapeDtypeStruct((half_read, panels), F32),
            jax.ShapeDtypeStruct((4, tok_rows, cols), BF16),
            jax.ShapeDtypeStruct((tok_rows, BLK), F32),
        ],
        scratch_shapes=[pltpu.VMEM((readout, panels), F32), pltpu.VMEM((tok_rows, width), BF16)],
        compiler_params=params("arbitrary", mib=60),
        cost_estimate=pl.CostEstimate(flops=2**31, bytes_accessed=6 * MIB, transcendentals=0),
        name="first",
    )(
        place, key_blocks.T, list_len, flat_ids, w_out, readout_weight, targets, tokens, gain, w_qkv
    )

    a1_tokens, own, mix, own_targets, hot = lax.optimization_barrier(
        (a1_tokens, own, mix, own_targets, hot)
    )
    b1_tokens = lax.ppermute(a1_tokens, "head", core_swap)
    a2_tokens, b1_tokens = lax.optimization_barrier((a2_tokens, b1_tokens))
    b2_tokens = lax.ppermute(a2_tokens, "head", core_swap)
    hbm = pl.BlockSpec(memory_space=pl.ANY)
    a1, b1, own_weight, read_keep, read_send = pl.pallas_call(
        near_kernel,
        in_specs=[vmem] * 3 + [hbm] * 2,
        out_specs=[hbm] * 3 + [vmem] * 2,
        out_shape=[
            jax.ShapeDtypeStruct((3, tok_rows, cols), BF16),
            jax.ShapeDtypeStruct((3, tok_rows, cols), BF16),
            jax.ShapeDtypeStruct((pairs, 3 * tok_rows + HD, 2 * tok_rows), BF16),
            jax.ShapeDtypeStruct((half_read, tok_rows), F32),
            jax.ShapeDtypeStruct((half_read, tok_rows), F32),
        ],
        scratch_shapes=[
            pltpu.VMEM((4, tok_rows, cols), BF16),
            pltpu.VMEM((3, width, cols), BF16),
            pltpu.VMEM((3, 2 * tok_rows, cols), BF16),
            pltpu.VMEM((pairs, 3 * tok_rows + HD, 2 * tok_rows), BF16),
            pltpu.SemaphoreType.DMA((4,)),
            pltpu.SemaphoreType.DMA((7 + pairs,)),
        ],
        compiler_params=params(),
        cost_estimate=pl.CostEstimate(flops=2**33, bytes_accessed=8 * MIB, transcendentals=0),
        name="near",
    )(a1_tokens, b1_tokens, gain, own, w_qkv)

    read_send, b2_tokens = lax.optimization_barrier((read_send, b2_tokens))
    read_got = lax.ppermute(read_send, "head", core_swap)
    spread = pl.pallas_call(
        spread_kernel,
        out_shape=jax.ShapeDtypeStruct((seq_count, half_read, tok_rows), BF16),
        compiler_params=params(),
        name="spread",
    )(read_keep, read_got)
    all_rows = lax.all_to_all(spread, "seq", 0, 0)

    side_weight = pl.pallas_call(
        side_kernel,
        in_specs=[vmem] * 3 + [hbm] * 4,
        out_specs=hbm,
        out_shape=jax.ShapeDtypeStruct((pairs, 2, tok_rows + HD, 2 * tok_rows), BF16),
        scratch_shapes=[pltpu.VMEM((4, tok_rows, cols), BF16)]
        + [pltpu.VMEM((3, tok_rows, cols), BF16)] * 2
        + [
            pltpu.VMEM((2, width, cols), BF16),
            pltpu.VMEM((2, 2 * tok_rows, cols), BF16),
            pltpu.VMEM((pairs, 2, tok_rows + HD, 2 * tok_rows), BF16),
            pltpu.SemaphoreType.DMA((5,)),
            pltpu.SemaphoreType.DMA((2 * pairs,)),
        ],
        compiler_params=params(),
        cost_estimate=pl.CostEstimate(flops=2**33, bytes_accessed=8 * MIB, transcendentals=0),
        name="attend_sides",
    )(a2_tokens, b2_tokens, gain, own, a1, b1, w_qkv)
    all_rows, side_weight = lax.optimization_barrier((all_rows, side_weight))

    batch = min(seq_count, 8)
    pool_steps = seq_count // batch
    resid_a, counts = pl.pallas_call(
        functools.partial(pool_kernel, pool_steps),
        grid=(pool_steps,),
        in_specs=[
            pl.BlockSpec((batch, half_read, tok_rows), lambda s: (s, 0, 0)),
            pl.BlockSpec((1, batch * tok_rows), lambda s: (0, s)),
            whole_spec((half_read, panels)),
        ],
        out_specs=[whole_spec((half_read, panels)), whole_spec((1, panels))],
        out_shape=[
            jax.ShapeDtypeStruct((half_read, panels), F32),
            jax.ShapeDtypeStruct((1, panels), F32),
        ],
        scratch_shapes=[pltpu.VMEM((half_read + 16, panels), F32)],
        compiler_params=params("arbitrary"),
        name="pool",
    )(all_rows, flat_ids, own_targets)
    resid_b = lax.ppermute(resid_a, "head", core_swap)

    core_index = place[1:2]
    sources = (own, a1, b1, own_weight, side_weight, w_qkv, tokens)
    keep, send, stats, loss = pl.pallas_call(
        back_kernel,
        in_specs=[SMEM_SPEC] + [vmem] * 6 + [hbm] * len(sources),
        out_specs=[vmem] * 4,
        out_shape=[
            jax.ShapeDtypeStruct((tok_rows, half_width), F32),
            jax.ShapeDtypeStruct((tok_rows, half_width + BLK), BF16),
            jax.ShapeDtypeStruct((tok_rows, BLK), F32),
            jax.ShapeDtypeStruct((1, BLK), F32),
        ],
        scratch_shapes=[pltpu.VMEM(a.shape, a.dtype) for a in sources]
        + [pltpu.SemaphoreType.DMA((8 + 2 * pairs,))],
        compiler_params=params(),
        name="back",
    )(core_index, resid_a, resid_b, counts, hot, mix, gain, *sources)
    got = lax.ppermute(send, "head", core_swap)
    loss_mean = 0.5 * loss[0, :1] / (all_tokens * readout)
    gradient = pl.pallas_call(
        final_kernel,
        in_specs=[SMEM_SPEC] + [vmem] * 6,
        out_shape=jax.ShapeDtypeStruct((tok_rows, half_width), F32),
        compiler_params=params(),
        name="final",
    )(core_index, keep, got, stats, inverse, tokens, gain)
    return (gradient, loss_mean)


def solution(mesh):
    return jax.shard_map(
        local,
        mesh=mesh,
        in_specs=(
            P(("groups", "seq"), None),
            P(),
            P(None, None, "head"),
            P("head", None),
            P(),
            P("groups", None),
            P("groups", None),
            P("groups"),
            P("groups", None),
        ),
        out_specs=(P(("groups", "seq"), "head"), P("groups")),
        check_vma=False,
    )
```

```python
import functools
import math

import jax
import jax.numpy as jnp
import numpy as np
from jax import lax
from jax.experimental import pallas as pl
from jax.experimental.pallas import tpu as pltpu
from jax.sharding import PartitionSpec as P

HD = 64
BLK = 128
LIST = 4
PAIR = 2 * HD
F32 = jnp.float32
BF16 = jnp.bfloat16
DEAD = 1e30
SCALE = 1.0 / math.sqrt(HD)
KEY_STEP = np.array([[0, 1, -1], [0, 1, 2], [0, -1, -2]], np.int32)
MIB = 1024 * 1024

NN = (((1,), (0,)), ((), ()))
NT = (((1,), (1,)), ((), ()))
TN = (((0,), (0,)), ((), ()))


def dot(a, b, dims, precision=None):
    return lax.dot_general(a, b, dims, precision=precision, preferred_element_type=F32)


def params(*semantics, mib=52):
    return pltpu.CompilerParams(vmem_limit_bytes=mib * MIB, dimension_semantics=semantics or None)


def inverse_root(inputs):
    return 1.0 / jnp.sqrt(jnp.mean(inputs * inputs, axis=-1, keepdims=True) + 1e-05)


def normalise(x_ref, gain_ref):
    inputs = x_ref[...].astype(F32)
    return (inputs * gain_ref[...] * inverse_root(inputs)).astype(BF16)


def project_rows(normed, w_part, part):
    rows = dot(normed, w_part, NN).astype(BF16)
    scale = jnp.where(part == 0, SCALE, 1.0)
    return (rows.astype(F32) * scale).astype(BF16)


def first_kernel(
    place_ref, lists_ref, lengths_ref, ids_ref, w_out_ref, read_ref, targets_ref, x_ref, gain_ref, w_ref,
    hot_ref, mix_ref, own_targets_ref, own_ref, inverse_ref, flipped, normed,
):
    part = pl.program_id(0)

    @pl.when(part == 0)
    def _():
        normed[...] = normalise(x_ref, gain_ref)
        inverse_ref[...] = jnp.broadcast_to(
            inverse_root(x_ref[...].astype(F32)), inverse_ref.shape
        )

    own_ref[part] = project_rows(normed[...], w_ref[0], part)

    @pl.when(part == 0)
    def _():
        prepare(
            place_ref, lists_ref, lengths_ref, ids_ref, w_out_ref, read_ref, targets_ref,
            hot_ref, mix_ref, own_targets_ref, own_ref, flipped,
        )


def prepare(
    place_ref, lists_ref, lengths_ref, ids_ref, w_out_ref, read_ref, targets_ref,
    hot_ref, mix_ref, own_targets_ref, own_ref, flipped,
):
    seq_index, core, seq_count = place_ref[0], place_ref[1], place_ref[2]
    side = 2 * core - 1
    half_read = own_targets_ref.shape[0]
    panels, tok_rows = hot_ref.shape[0], hot_ref.shape[1] // 3
    per = tok_rows // BLK
    mix = dot(w_out_ref[...], read_ref[...], NN).T
    flip = jnp.concatenate([mix[half_read:], mix[:half_read]], axis=0)
    mix = jnp.where(core == 0, mix, flip).astype(BF16)
    mix_ref[...] = mix
    readout = mix.shape[0]
    own_ref[3, :readout] = mix
    own_ref[3, readout:] = jnp.zeros((tok_rows - readout, mix.shape[1]), BF16)
    flipped[...] = targets_ref[...].T
    own_targets_ref[...] = flipped[pl.ds(pl.multiple_of(core * half_read, half_read), half_read), :]
    panel = lax.broadcasted_iota(jnp.int32, (panels, tok_rows), 0)
    column = lax.broadcasted_iota(jnp.int32, (1, 2 * tok_rows), 1)
    for t, move in enumerate((0, 1, -1)):
        stretch = seq_index + side * move
        inside = (stretch >= 0) & (stretch < seq_count)
        stretch = jnp.clip(stretch, 0, seq_count - 1)
        ids = ids_ref[:, pl.ds(pl.multiple_of(stretch * tok_rows, tok_rows), tok_rows)]
        hits = (panel == ids) & inside
        hot_ref[:, t * tok_rows : (t + 1) * tok_rows] = jnp.where(hits, 1.0, 0.0).astype(BF16)
        biases = []
        for k in range(3 * per):
            key_block = (seq_index + side * int(KEY_STEP[t, k // per])) * per + k % per
            row = jnp.zeros((1, 2 * tok_rows), F32)
            for b in range(per):
                query_block = stretch * per + b
                live = jnp.logical_not(inside)
                for j in range(LIST):
                    live = live | (
                        (lists_ref[j, query_block] == key_block) & (j < lengths_ref[query_block])
                    )
                off = jnp.where(live, 0.0, DEAD)
                row = jnp.where((column // BLK) % per == b, off, row)
            biases.append(row)
        biases.append(jnp.zeros((16 - 3 * per, 2 * tok_rows), F32))
        own_ref[3, readout + 16 * t : readout + 16 * (t + 1)] = jnp.concatenate(
            biases, axis=0
        ).astype(BF16)


def pair_cols(p):
    return slice(p * PAIR, (p + 1) * PAIR)


def two_heads(tile):
    lane = lax.broadcasted_iota(jnp.int32, tile.shape, 1)
    zero = jnp.zeros_like(tile)
    return jnp.concatenate(
        [jnp.where(lane < HD, tile, zero), jnp.where(lane >= HD, tile, zero)], axis=0
    )


def head_halves(pair_t):
    half = pair_t.shape[1] // 2
    return pair_t[:HD, :half], pair_t[HD:, half:]


def fold_heads(pair_t):
    return jnp.concatenate(head_halves(pair_t), axis=0)


def soften(own_ref, stretch, scores):
    count = scores.shape[0] // BLK
    blocks = [scores[k * BLK : (k + 1) * BLK] for k in range(count)]
    base = own_ref.shape[1] // 2 + 16 * stretch
    bias = own_ref[3, base : base + 16, :].astype(F32)
    biases = [bias[k : k + 1] for k in range(count)]
    tops = [jnp.max(b, axis=0, keepdims=True) - d for b, d in zip(blocks, biases)]
    top = functools.reduce(jnp.maximum, tops)
    expo = [jnp.exp(b - (top + d)) for b, d in zip(blocks, biases)]
    total = functools.reduce(jnp.add, [jnp.sum(e, axis=0, keepdims=True) for e in expo])
    inverse = 1.0 / total
    return jnp.concatenate([(e * inverse).astype(BF16) for e in expo], axis=0)


def start_all(copies):
    for copy in copies:
        copy.start()
    return copies


def wait_all(copies):
    for copy in copies:
        copy.wait()


def near_kernel(
    a1x_ref, b1x_ref, gain_ref, own_hbm, w_hbm,
    a1_hbm, b1_hbm, weight_hbm, keep_ref, send_ref,
    own_ref, w_ref, near_ref, weight_ref, arrived, sent,
):
    rows = own_ref.shape[1]
    pairs = own_ref.shape[2] // PAIR
    order = (1, 2, 0)
    w_in = {c: pltpu.make_async_copy(w_hbm.at[c], w_ref.at[c], arrived.at[c]) for c in order}
    own_in = pltpu.make_async_copy(own_hbm, own_ref, arrived.at[3])
    start_all([w_in[1], own_in])
    normed = jnp.concatenate([normalise(a1x_ref, gain_ref), normalise(b1x_ref, gain_ref)], axis=0)
    out = []

    def project(c):
        w_in[c].wait()
        near_ref[c] = project_rows(normed, w_ref[c], c)
        for side, target in enumerate((a1_hbm, b1_hbm)):
            source = near_ref.at[c, pl.ds(side * rows, rows)]
            out.append(pltpu.make_async_copy(source, target.at[c], sent.at[2 * c + side]))
            out[-1].start()

    def stack(c, p):
        return jnp.concatenate([own_ref[c, :, pair_cols(p)], near_ref[c, :, pair_cols(p)]], axis=0)

    def score(p):
        return dot(stack(1, p), two_heads(own_ref[0, :, pair_cols(p)]), NT)

    w_in[2].start()
    project(1)
    own_in.wait()
    w_in[0].start()
    scores = {0: score(0)}
    project(2)
    attended = []
    for p in range(pairs):
        if p + 1 < pairs:
            scores[p + 1] = score(p + 1)
        weight = soften(own_ref, 0, scores[p])
        weight_ref[p, : 3 * rows] = weight
        part = (p, pl.ds(0, 3 * rows))
        out.append(pltpu.make_async_copy(weight_ref.at[part], weight_hbm.at[part], sent.at[6 + p]))
        out[-1].start()
        if p == pairs - 1:
            project(0)
        halves = head_halves(dot(stack(2, p), weight, TN).astype(BF16))
        weight_ref[p, 3 * rows :] = jnp.concatenate(halves, axis=1)
        if p == pairs - 1:
            part = (slice(None), pl.ds(3 * rows, HD))
            out.append(
                pltpu.make_async_copy(weight_ref.at[part], weight_hbm.at[part], sent.at[6 + pairs])
            )
            out[-1].start()
        attended.extend(halves)
    half = keep_ref.shape[0]
    read = dot(own_ref[3, : 2 * half, :], jnp.concatenate(attended, axis=0), NN)
    keep_ref[...] = read[:half]
    send_ref[...] = read[half:]
    wait_all(out)


def side_kernel(
    a2x_ref, b2x_ref, gain_ref, own_hbm, a1_hbm, b1_hbm, w_hbm, weight_hbm,
    own_ref, a1_ref, b1_ref, w_ref, far_ref, weight_ref, arrived, sent,
):
    rows = own_ref.shape[1]
    pairs = own_ref.shape[2] // PAIR
    w_in = [
        pltpu.make_async_copy(w_hbm.at[c + 1], w_ref.at[c], arrived.at[c]) for c in range(2)
    ]
    rows_in = [
        pltpu.make_async_copy(source, target, arrived.at[2 + n])
        for n, (source, target) in enumerate(
            ((own_hbm, own_ref), (a1_hbm, a1_ref), (b1_hbm, b1_ref))
        )
    ]
    start_all([w_in[0]] + rows_in + [w_in[1]])
    normed = jnp.concatenate([normalise(a2x_ref, gain_ref), normalise(b2x_ref, gain_ref)], axis=0)
    near = (a1_ref, b1_ref)
    out = []

    def project(c):
        w_in[c].wait()
        far_ref[c] = dot(normed, w_ref[c], NN).astype(BF16)

    def stack(c, p, side):
        cols = pair_cols(p)
        far = far_ref[c - 1, side * rows : (side + 1) * rows, cols]
        return jnp.concatenate([own_ref[c, :, cols], near[side][c, :, cols], far], axis=0)

    def score(p, side):
        return dot(stack(1, p, side), two_heads(near[side][0, :, pair_cols(p)]), NT)

    project(0)
    wait_all(rows_in)
    jobs = [(p, side) for p in range(pairs) for side in range(2)]
    scores = {jobs[0]: score(*jobs[0])}
    project(1)
    for n, (p, side) in enumerate(jobs):
        if n + 1 < len(jobs):
            scores[jobs[n + 1]] = score(*jobs[n + 1])
        weight = soften(own_ref, 1 + side, scores[p, side])
        weight_ref[p, side, :rows] = weight[:rows]
        halves = head_halves(dot(stack(2, p, side), weight, TN).astype(BF16))
        weight_ref[p, side, rows:] = jnp.concatenate(halves, axis=1)
        out.append(
            pltpu.make_async_copy(weight_ref.at[p, side], weight_hbm.at[p, side], sent.at[n])
        )
        out[-1].start()
    wait_all(out)


def spread_kernel(keep_ref, got_ref, out_ref):
    rows = (keep_ref[...] + got_ref[...]).astype(BF16)
    for s in range(out_ref.shape[0]):
        out_ref[s] = rows


def pool_kernel(steps, rows_ref, ids_ref, targets_ref, out_ref, counts_ref, sums):
    step = pl.program_id(0)
    half_read, panels = out_ref.shape
    count, _, tok_rows = rows_ref.shape

    @pl.when(step == 0)
    def _():
        sums[...] = jnp.zeros_like(sums)

    panel = lax.broadcasted_iota(jnp.int32, (panels, count * tok_rows), 0)
    hits = jnp.where(panel == ids_ref[...], 1.0, 0.0).astype(BF16)
    rows = jnp.concatenate([rows_ref[s] for s in range(count)], axis=1)
    rows = jnp.concatenate([rows, jnp.ones((16, count * tok_rows), BF16)], axis=0)
    sums[...] += dot(rows, hits, NT)

    @pl.when(step == steps - 1)
    def _():
        counts = sums[half_read : half_read + 1]
        out_ref[...] = sums[:half_read] / counts - targets_ref[...]
        counts_ref[...] = counts


def back_kernel(
    core_ref, resid_a_ref, resid_b_ref, counts_ref, hot_ref, mix_ref, gain_ref, *refs
):
    sources, (keep_ref, send_ref, stat_ref, loss_ref) = refs[:7], refs[7:11]
    buffers, arrived = refs[11:18], refs[18]
    own_ref, a1_ref, b1_ref, own_w_ref, side_w_ref, w_ref, tokens_ref = buffers
    pairs = own_ref.shape[2] // PAIR
    slots = iter(range(arrived.shape[0]))

    def fetch(n, index):
        return pltpu.make_async_copy(
            sources[n].at[index], buffers[n].at[index], arrived.at[next(slots)]
        )

    values_in = [fetch(n, pl.ds(2, 1)) for n in range(3)]
    weight_in = [[fetch(n, pl.ds(p, 1)) for n in (3, 4)] for p in range(pairs)]
    rest_in = [fetch(n, pl.ds(0, 2)) for n in range(3)]
    last_in = [fetch(5, pl.ds(0, 3)), fetch(6, pl.ds(0, tokens_ref.shape[0]))]
    start_all(values_in + weight_in[0] + rest_in)
    own_rows = own_ref.shape[1]
    residual = jnp.concatenate([resid_a_ref[...], resid_b_ref[...]], axis=0)
    loss_ref[...] = jnp.broadcast_to(
        jnp.sum(counts_ref[...] * residual * residual, keepdims=True), loss_ref.shape
    )
    panel_grad = dot(mix_ref[...].astype(F32), residual, TN, lax.Precision.HIGHEST).astype(BF16)
    out_grad = dot(panel_grad, hot_ref[...], NN).astype(BF16)
    stretches = (own_ref, a1_ref, b1_ref)

    def tile_of(p, t):
        return out_grad[pair_cols(p), t * own_rows : (t + 1) * own_rows]

    def open_job(p, t):
        values = jnp.concatenate(
            [r[2, :, pair_cols(p)] for r in (stretches if t == 0 else stretches[:1])], axis=0
        )
        tile = tile_of(p, t)
        none = jnp.zeros((HD, own_rows), BF16)
        grad = jnp.concatenate(
            [
                jnp.concatenate([tile[:HD], none], axis=0),
                jnp.concatenate([none, tile[HD:]], axis=0),
            ],
            axis=1,
        )
        return grad, dot(values, grad, NN)

    def score_job(p, t, change):
        pack = own_w_ref[p] if t == 0 else side_w_ref[p, t - 1]
        weight, attended = pack[:-HD], pack[-HD:]
        tile = tile_of(p, t)
        flat_tile = jnp.concatenate([tile[:HD], tile[HD:]], axis=1)
        delta = jnp.sum(flat_tile.astype(F32) * attended.astype(F32), axis=0, keepdims=True)
        return (weight.astype(F32) * (change - delta)).astype(BF16)

    def query_of(p, score):
        keys = jnp.concatenate([r[1, :, pair_cols(p)] for r in stretches], axis=0)
        grad_query = fold_heads(dot(keys, score, TN)) * SCALE
        return grad_query.T.astype(BF16)

    def close_job(p, t, grad, score):
        weight = own_w_ref[p, :own_rows] if t == 0 else side_w_ref[p, t - 1, :own_rows]
        queries = two_heads(stretches[t][0, :, pair_cols(p)])
        return dot(score[:own_rows], queries, NN), dot(weight, grad, NT)

    wait_all(values_in)
    start_all([copy for pair in weight_in[1:] for copy in pair] + last_in)
    jobs = [(p, t) for p in range(pairs) for t in range(3)]
    opened = open_job(*jobs[0])
    grad_proj = []
    for n, (p, t) in enumerate(jobs):
        grad, change = opened
        if n + 1 < len(jobs):
            opened = open_job(*jobs[n + 1])
        if t == 0:
            wait_all(weight_in[p])
        score = score_job(p, t, change)
        if n == 0:
            wait_all(rest_in)
        if t == 0:
            grad_query = query_of(p, score)
            grad_key, grad_value = close_job(p, t, grad, score)
        else:
            more_key, more_value = close_job(p, t, grad, score)
            grad_key, grad_value = grad_key + more_key, grad_value + more_value
        if t == 2:
            grad_proj.append((grad_query, grad_key.astype(BF16), grad_value.astype(BF16)))
    flat = jnp.concatenate([grad_proj[p][c] for c in range(3) for p in range(pairs)], axis=1)
    wait_all(last_in)
    half = keep_ref.shape[1]
    row_sum = jnp.zeros((own_rows, 1), F32)
    core = core_ref[0]
    parts = []
    for h in (core, 1 - core):
        rows = pl.ds(pl.multiple_of(h * half, half), half)
        w_part = jnp.concatenate([w_ref[c, rows, :] for c in range(3)], axis=1)
        parts.append(dot(flat, w_part, NT))
        scaled = tokens_ref[:, rows].astype(F32) * gain_ref[:, rows]
        row_sum += jnp.sum(scaled * parts[-1], axis=-1, keepdims=True)
    keep_ref[...] = parts[0]
    send_ref[:, :half] = parts[1].astype(BF16)
    high = row_sum.astype(BF16).astype(F32)
    lane = lax.broadcasted_iota(jnp.int32, (own_rows, BLK), 1)
    send_ref[:, half:] = jnp.where(lane < HD, high, row_sum - high).astype(BF16)
    stat_ref[...] = jnp.broadcast_to(row_sum, stat_ref.shape)


def final_kernel(
    core_ref, keep_ref, got_ref, stat_ref, inverse_ref, tokens_ref, gain_ref, out_ref
):
    half = keep_ref.shape[1]
    cols = pl.ds(pl.multiple_of(core_ref[0] * half, half), half)
    got_sum = got_ref[:, half : half + 1].astype(F32) + got_ref[:, half + HD : half + HD + 1].astype(F32)
    row_sum = stat_ref[:, :1] + got_sum
    inverse = inverse_ref[:, :1]
    grad_normed = keep_ref[...] + got_ref[:, :half].astype(F32)
    shrink = row_sum * (inverse * inverse * inverse) * (0.5 / half)
    out_ref[...] = (
        gain_ref[:, cols] * grad_normed * inverse - tokens_ref[:, cols].astype(F32) * shrink
    )


def whole_spec(shape):
    return pl.BlockSpec(shape, lambda p: (0,) * len(shape))


SMEM_SPEC = pl.BlockSpec(memory_space=pltpu.SMEM)


def local(
    tokens, norm_gain, w_qkv, w_out, readout_weight, targets, key_blocks, list_len, voxel_panel
):
    tok_rows, width = tokens.shape
    cols = w_qkv.shape[2]
    pairs = cols // PAIR
    panels, readout = targets.shape
    half_read = readout // 2
    half_width = width // 2
    seq_count = lax.axis_size("seq")
    seq_index = lax.axis_index("seq")
    core = lax.axis_index("head")
    side_step = 2 * core - 1
    all_tokens = voxel_panel.shape[0]
    per = tok_rows // BLK
    core_swap = [(0, 1), (1, 0)]

    def shifted(far):
        return [
            (2 * s, 2 * (s + far)) for s in range(seq_count - far)
        ] + [(2 * (s + far) + 1, 2 * s + 1) for s in range(seq_count - far)]

    a1_tokens = lax.ppermute(tokens, ("seq", "head"), shifted(1))
    a2_tokens = lax.ppermute(tokens, ("seq", "head"), shifted(2))

    gain = norm_gain.reshape(1, width)
    flat_ids = voxel_panel.reshape(1, all_tokens)
    place = jnp.stack([seq_index, core, jnp.int32(seq_count)]).astype(jnp.int32)
    vmem = pl.BlockSpec(memory_space=pltpu.VMEM)
    whole_tokens = whole_spec((tok_rows, width))
    whole_gain = whole_spec((1, width))
    hot, mix, own_targets, own, inverse = pl.pallas_call(
        first_kernel,
        grid=(3,),
        in_specs=[SMEM_SPEC] * 3
        + [
            whole_spec((1, all_tokens)),
            whole_spec(w_out.shape),
            whole_spec(readout_weight.shape),
            whole_spec(targets.shape),
            whole_tokens,
            whole_gain,
            pl.BlockSpec((1, width, cols), lambda c: (c, 0, 0)),
        ],
        out_specs=[
            whole_spec((panels, 3 * tok_rows)),
            whole_spec((readout, cols)),
            whole_spec((half_read, panels)),
            whole_spec((4, tok_rows, cols)),
            whole_spec((tok_rows, BLK)),
        ],
        out_shape=[
            jax.ShapeDtypeStruct((panels, 3 * tok_rows), BF16),
            jax.ShapeDtypeStruct((readout, cols), BF16),
            jax.ShapeDtypeStruct((half_read, panels), F32),
            jax.ShapeDtypeStruct((4, tok_rows, cols), BF16),
            jax.ShapeDtypeStruct((tok_rows, BLK), F32),
        ],
        scratch_shapes=[pltpu.VMEM((readout, panels), F32), pltpu.VMEM((tok_rows, width), BF16)],
        compiler_params=params("arbitrary", mib=60),
        cost_estimate=pl.CostEstimate(flops=2**31, bytes_accessed=6 * MIB, transcendentals=0),
        name="first",
    )(
        place, key_blocks.T, list_len, flat_ids, w_out, readout_weight, targets, tokens, gain, w_qkv
    )

    a1_tokens, own, mix, own_targets, hot = lax.optimization_barrier(
        (a1_tokens, own, mix, own_targets, hot)
    )
    b1_tokens = lax.ppermute(a1_tokens, "head", core_swap)
    a2_tokens, b1_tokens = lax.optimization_barrier((a2_tokens, b1_tokens))
    b2_tokens = lax.ppermute(a2_tokens, "head", core_swap)
    hbm = pl.BlockSpec(memory_space=pl.ANY)
    a1, b1, own_weight, read_keep, read_send = pl.pallas_call(
        near_kernel,
        in_specs=[vmem] * 3 + [hbm] * 2,
        out_specs=[hbm] * 3 + [vmem] * 2,
        out_shape=[
            jax.ShapeDtypeStruct((3, tok_rows, cols), BF16),
            jax.ShapeDtypeStruct((3, tok_rows, cols), BF16),
            jax.ShapeDtypeStruct((pairs, 3 * tok_rows + HD, 2 * tok_rows), BF16),
            jax.ShapeDtypeStruct((half_read, tok_rows), F32),
            jax.ShapeDtypeStruct((half_read, tok_rows), F32),
        ],
        scratch_shapes=[
            pltpu.VMEM((4, tok_rows, cols), BF16),
            pltpu.VMEM((3, width, cols), BF16),
            pltpu.VMEM((3, 2 * tok_rows, cols), BF16),
            pltpu.VMEM((pairs, 3 * tok_rows + HD, 2 * tok_rows), BF16),
            pltpu.SemaphoreType.DMA((4,)),
            pltpu.SemaphoreType.DMA((7 + pairs,)),
        ],
        compiler_params=params(),
        cost_estimate=pl.CostEstimate(flops=2**33, bytes_accessed=8 * MIB, transcendentals=0),
        name="near",
    )(a1_tokens, b1_tokens, gain, own, w_qkv)

    read_send, b2_tokens = lax.optimization_barrier((read_send, b2_tokens))
    read_got = lax.ppermute(read_send, "head", core_swap)
    spread = pl.pallas_call(
        spread_kernel,
        out_shape=jax.ShapeDtypeStruct((seq_count, half_read, tok_rows), BF16),
        compiler_params=params(),
        name="spread",
    )(read_keep, read_got)
    all_rows = lax.all_to_all(spread, "seq", 0, 0)

    side_weight = pl.pallas_call(
        side_kernel,
        in_specs=[vmem] * 3 + [hbm] * 4,
        out_specs=hbm,
        out_shape=jax.ShapeDtypeStruct((pairs, 2, tok_rows + HD, 2 * tok_rows), BF16),
        scratch_shapes=[pltpu.VMEM((4, tok_rows, cols), BF16)]
        + [pltpu.VMEM((3, tok_rows, cols), BF16)] * 2
        + [
            pltpu.VMEM((2, width, cols), BF16),
            pltpu.VMEM((2, 2 * tok_rows, cols), BF16),
            pltpu.VMEM((pairs, 2, tok_rows + HD, 2 * tok_rows), BF16),
            pltpu.SemaphoreType.DMA((5,)),
            pltpu.SemaphoreType.DMA((2 * pairs,)),
        ],
        compiler_params=params(),
        cost_estimate=pl.CostEstimate(flops=2**33, bytes_accessed=8 * MIB, transcendentals=0),
        name="attend_sides",
    )(a2_tokens, b2_tokens, gain, own, a1, b1, w_qkv)
    all_rows, side_weight = lax.optimization_barrier((all_rows, side_weight))

    batch = min(seq_count, 8)
    pool_steps = seq_count // batch
    resid_a, counts = pl.pallas_call(
        functools.partial(pool_kernel, pool_steps),
        grid=(pool_steps,),
        in_specs=[
            pl.BlockSpec((batch, half_read, tok_rows), lambda s: (s, 0, 0)),
            pl.BlockSpec((1, batch * tok_rows), lambda s: (0, s)),
            whole_spec((half_read, panels)),
        ],
        out_specs=[whole_spec((half_read, panels)), whole_spec((1, panels))],
        out_shape=[
            jax.ShapeDtypeStruct((half_read, panels), F32),
            jax.ShapeDtypeStruct((1, panels), F32),
        ],
        scratch_shapes=[pltpu.VMEM((half_read + 16, panels), F32)],
        compiler_params=params("arbitrary"),
        name="pool",
    )(all_rows, flat_ids, own_targets)
    resid_b = lax.ppermute(resid_a, "head", core_swap)

    core_index = place[1:2]
    sources = (own, a1, b1, own_weight, side_weight, w_qkv, tokens)
    keep, send, stats, loss = pl.pallas_call(
        back_kernel,
        in_specs=[SMEM_SPEC] + [vmem] * 6 + [hbm] * len(sources),
        out_specs=[vmem] * 4,
        out_shape=[
            jax.ShapeDtypeStruct((tok_rows, half_width), F32),
            jax.ShapeDtypeStruct((tok_rows, half_width + BLK), BF16),
            jax.ShapeDtypeStruct((tok_rows, BLK), F32),
            jax.ShapeDtypeStruct((1, BLK), F32),
        ],
        scratch_shapes=[pltpu.VMEM(a.shape, a.dtype) for a in sources]
        + [pltpu.SemaphoreType.DMA((8 + 2 * pairs,))],
        compiler_params=params(),
        name="back",
    )(core_index, resid_a, resid_b, counts, hot, mix, gain, *sources)
    got = lax.ppermute(send, "head", core_swap)
    loss_mean = 0.5 * loss[0, :1] / (all_tokens * readout)
    gradient = pl.pallas_call(
        final_kernel,
        in_specs=[SMEM_SPEC] + [vmem] * 6,
        out_shape=jax.ShapeDtypeStruct((tok_rows, half_width), F32),
        compiler_params=params(),
        name="final",
    )(core_index, keep, got, stats, inverse, tokens, gain)
    return (gradient, loss_mean)


def solution(mesh):
    return jax.shard_map(
        local,
        mesh=mesh,
        in_specs=(
            P(("groups", "seq"), None),
            P(),
            P(None, None, "head"),
            P("head", None),
            P(),
            P("groups", None),
            P("groups", None),
            P("groups"),
            P("groups", None),
        ),
        out_specs=(P(("groups", "seq"), "head"), P("groups")),
        check_vma=False,
    )
```

```python
import functools
import math

import jax
import jax.numpy as jnp
import numpy as np
from jax import lax
from jax.experimental import pallas as pl
from jax.experimental.pallas import tpu as pltpu
from jax.sharding import PartitionSpec as P

HD = 64
BLK = 128
LIST = 4
PAIR = 2 * HD
F32 = jnp.float32
BF16 = jnp.bfloat16
DEAD = 1e30
SCALE = 1.0 / math.sqrt(HD)
KEY_STEP = np.array([[0, 1, -1], [0, 1, 2], [0, -1, -2]], np.int32)
MIB = 1024 * 1024

NN = (((1,), (0,)), ((), ()))
NT = (((1,), (1,)), ((), ()))
TN = (((0,), (0,)), ((), ()))


def dot(a, b, dims, precision=None):
    return lax.dot_general(a, b, dims, precision=precision, preferred_element_type=F32)


def params(*semantics, mib=52):
    return pltpu.CompilerParams(vmem_limit_bytes=mib * MIB, dimension_semantics=semantics or None)


def inverse_root(inputs):
    return 1.0 / jnp.sqrt(jnp.mean(inputs * inputs, axis=-1, keepdims=True) + 1e-05)


def normalise(x_ref, gain_ref):
    inputs = x_ref[...].astype(F32)
    return (inputs * gain_ref[...] * inverse_root(inputs)).astype(BF16)


def project_rows(normed, w_part, part):
    rows = dot(normed, w_part, NN).astype(BF16)
    scale = jnp.where(part == 0, SCALE, 1.0)
    return (rows.astype(F32) * scale).astype(BF16)


def first_kernel(
    place_ref, lists_ref, lengths_ref, ids_ref, w_out_ref, read_ref, targets_ref, x_ref, gain_ref, w_ref,
    hot_ref, mix_ref, own_targets_ref, own_ref, inverse_ref, flipped, normed,
):
    part = pl.program_id(0)

    @pl.when(part == 0)
    def _():
        normed[...] = normalise(x_ref, gain_ref)
        inverse_ref[...] = jnp.broadcast_to(
            inverse_root(x_ref[...].astype(F32)), inverse_ref.shape
        )

    own_ref[part] = project_rows(normed[...], w_ref[0], part)

    @pl.when(part == 0)
    def _():
        prepare(
            place_ref, lists_ref, lengths_ref, ids_ref, w_out_ref, read_ref, targets_ref,
            hot_ref, mix_ref, own_targets_ref, own_ref, flipped,
        )


def prepare(
    place_ref, lists_ref, lengths_ref, ids_ref, w_out_ref, read_ref, targets_ref,
    hot_ref, mix_ref, own_targets_ref, own_ref, flipped,
):
    seq_index, core, seq_count = place_ref[0], place_ref[1], place_ref[2]
    side = 2 * core - 1
    half_read = own_targets_ref.shape[0]
    panels, tok_rows = hot_ref.shape[0], hot_ref.shape[1] // 3
    per = tok_rows // BLK
    mix = dot(w_out_ref[...], read_ref[...], NN).T
    flip = jnp.concatenate([mix[half_read:], mix[:half_read]], axis=0)
    mix = jnp.where(core == 0, mix, flip).astype(BF16)
    mix_ref[...] = mix
    readout = mix.shape[0]
    own_ref[3, :readout] = mix
    own_ref[3, readout:] = jnp.zeros((tok_rows - readout, mix.shape[1]), BF16)
    flipped[...] = targets_ref[...].T
    own_targets_ref[...] = flipped[pl.ds(pl.multiple_of(core * half_read, half_read), half_read), :]
    panel = lax.broadcasted_iota(jnp.int32, (panels, tok_rows), 0)
    column = lax.broadcasted_iota(jnp.int32, (1, 2 * tok_rows), 1)
    for t, move in enumerate((0, 1, -1)):
        stretch = seq_index + side * move
        inside = (stretch >= 0) & (stretch < seq_count)
        stretch = jnp.clip(stretch, 0, seq_count - 1)
        ids = ids_ref[:, pl.ds(pl.multiple_of(stretch * tok_rows, tok_rows), tok_rows)]
        hits = (panel == ids) & inside
        hot_ref[:, t * tok_rows : (t + 1) * tok_rows] = jnp.where(hits, 1.0, 0.0).astype(BF16)
        biases = []
        for k in range(3 * per):
            key_block = (seq_index + side * int(KEY_STEP[t, k // per])) * per + k % per
            row = jnp.zeros((1, 2 * tok_rows), F32)
            for b in range(per):
                query_block = stretch * per + b
                live = jnp.logical_not(inside)
                for j in range(LIST):
                    live = live | (
                        (lists_ref[j, query_block] == key_block) & (j < lengths_ref[query_block])
                    )
                off = jnp.where(live, 0.0, DEAD)
                row = jnp.where((column // BLK) % per == b, off, row)
            biases.append(row)
        biases.append(jnp.zeros((16 - 3 * per, 2 * tok_rows), F32))
        own_ref[3, readout + 16 * t : readout + 16 * (t + 1)] = jnp.concatenate(
            biases, axis=0
        ).astype(BF16)


def pair_cols(p):
    return slice(p * PAIR, (p + 1) * PAIR)


def two_heads(tile):
    lane = lax.broadcasted_iota(jnp.int32, tile.shape, 1)
    zero = jnp.zeros_like(tile)
    return jnp.concatenate(
        [jnp.where(lane < HD, tile, zero), jnp.where(lane >= HD, tile, zero)], axis=0
    )


def head_halves(pair_t):
    half = pair_t.shape[1] // 2
    return pair_t[:HD, :half], pair_t[HD:, half:]


def fold_heads(pair_t):
    return jnp.concatenate(head_halves(pair_t), axis=0)


def soften(own_ref, stretch, scores):
    count = scores.shape[0] // BLK
    base = own_ref.shape[1] // 2 + 16 * stretch
    bias = own_ref[3, base : base + 16, :].astype(F32)
    weights = []
    for first in range(0, scores.shape[1], BLK):
        cols = slice(first, first + BLK)
        blocks = [scores[k * BLK : (k + 1) * BLK, cols] for k in range(count)]
        biases = [bias[k : k + 1, cols] for k in range(count)]
        tops = [jnp.max(b, axis=0, keepdims=True) - d for b, d in zip(blocks, biases)]
        top = functools.reduce(jnp.maximum, tops)
        expo = [jnp.exp(b - (top + d)) for b, d in zip(blocks, biases)]
        total = functools.reduce(jnp.add, [jnp.sum(e, axis=0, keepdims=True) for e in expo])
        inverse = 1.0 / total
        weights.append(jnp.concatenate([(e * inverse).astype(BF16) for e in expo], axis=0))
    return jnp.concatenate(weights, axis=1)


def start_all(copies):
    for copy in copies:
        copy.start()
    return copies


def wait_all(copies):
    for copy in copies:
        copy.wait()


def near_kernel(
    a1x_ref, b1x_ref, gain_ref, own_hbm, w_hbm,
    a1_hbm, b1_hbm, weight_hbm, keep_ref, send_ref,
    own_ref, w_ref, near_ref, weight_ref, arrived, sent,
):
    rows = own_ref.shape[1]
    pairs = own_ref.shape[2] // PAIR
    order = (1, 2, 0)
    w_in = {c: pltpu.make_async_copy(w_hbm.at[c], w_ref.at[c], arrived.at[c]) for c in order}
    own_in = pltpu.make_async_copy(own_hbm, own_ref, arrived.at[3])
    start_all([w_in[1], own_in, w_in[2], w_in[0]])
    normed = jnp.concatenate([normalise(a1x_ref, gain_ref), normalise(b1x_ref, gain_ref)], axis=0)
    out = []

    def project(c):
        w_in[c].wait()
        near_ref[c] = project_rows(normed, w_ref[c], c)
        for side, target in enumerate((a1_hbm, b1_hbm)):
            source = near_ref.at[c, pl.ds(side * rows, rows)]
            out.append(pltpu.make_async_copy(source, target.at[c], sent.at[2 * c + side]))
            out[-1].start()

    def stack(c, p):
        return jnp.concatenate([own_ref[c, :, pair_cols(p)], near_ref[c, :, pair_cols(p)]], axis=0)

    def score(p):
        return dot(stack(1, p), two_heads(own_ref[0, :, pair_cols(p)]), NT)

    project(1)
    own_in.wait()
    scores = {0: score(0)}
    project(2)
    attended = []
    for p in range(pairs):
        if p + 1 < pairs:
            scores[p + 1] = score(p + 1)
        weight = soften(own_ref, 0, scores[p])
        weight_ref[p, : 3 * rows] = weight
        part = (p, pl.ds(0, 3 * rows))
        out.append(pltpu.make_async_copy(weight_ref.at[part], weight_hbm.at[part], sent.at[6 + p]))
        out[-1].start()
        if p == pairs - 1:
            project(0)
        halves = head_halves(dot(stack(2, p), weight, TN).astype(BF16))
        weight_ref[p, 3 * rows :] = jnp.concatenate(halves, axis=1)
        if p == pairs - 1:
            part = (slice(None), pl.ds(3 * rows, HD))
            out.append(
                pltpu.make_async_copy(weight_ref.at[part], weight_hbm.at[part], sent.at[6 + pairs])
            )
            out[-1].start()
        attended.extend(halves)
    half = keep_ref.shape[0]
    read = dot(own_ref[3, : 2 * half, :], jnp.concatenate(attended, axis=0), NN)
    keep_ref[...] = read[:half]
    send_ref[...] = read[half:]
    wait_all(out)


def side_kernel(
    a2x_ref, b2x_ref, gain_ref, own_hbm, a1_hbm, b1_hbm, w_hbm, weight_hbm,
    own_ref, a1_ref, b1_ref, w_ref, far_ref, weight_ref, arrived, sent,
):
    rows = own_ref.shape[1]
    pairs = own_ref.shape[2] // PAIR
    w_in = [
        pltpu.make_async_copy(w_hbm.at[c + 1], w_ref.at[c], arrived.at[c]) for c in range(2)
    ]
    rows_in = [
        pltpu.make_async_copy(source, target, arrived.at[2 + n])
        for n, (source, target) in enumerate(
            ((own_hbm, own_ref), (a1_hbm, a1_ref), (b1_hbm, b1_ref))
        )
    ]
    start_all([w_in[0]] + rows_in + [w_in[1]])
    normed = jnp.concatenate([normalise(a2x_ref, gain_ref), normalise(b2x_ref, gain_ref)], axis=0)
    near = (a1_ref, b1_ref)
    out = []

    def project(c):
        w_in[c].wait()
        far_ref[c] = dot(normed, w_ref[c], NN).astype(BF16)

    def stack(c, p, side):
        cols = pair_cols(p)
        far = far_ref[c - 1, side * rows : (side + 1) * rows, cols]
        return jnp.concatenate([own_ref[c, :, cols], near[side][c, :, cols], far], axis=0)

    def score(p, side):
        return dot(stack(1, p, side), two_heads(near[side][0, :, pair_cols(p)]), NT)

    project(0)
    wait_all(rows_in)
    jobs = [(p, side) for p in range(pairs) for side in range(2)]
    scores = {jobs[0]: score(*jobs[0])}
    project(1)
    for n, (p, side) in enumerate(jobs):
        if n + 1 < len(jobs):
            scores[jobs[n + 1]] = score(*jobs[n + 1])
        weight = soften(own_ref, 1 + side, scores[p, side])
        weight_ref[p, side, :rows] = weight[:rows]
        halves = head_halves(dot(stack(2, p, side), weight, TN).astype(BF16))
        weight_ref[p, side, rows:] = jnp.concatenate(halves, axis=1)
        out.append(
            pltpu.make_async_copy(weight_ref.at[p, side], weight_hbm.at[p, side], sent.at[n])
        )
        out[-1].start()
    wait_all(out)


def spread_kernel(keep_ref, got_ref, out_ref):
    rows = (keep_ref[...] + got_ref[...]).astype(BF16)
    for s in range(out_ref.shape[0]):
        out_ref[s] = rows


def pool_kernel(steps, rows_ref, ids_ref, targets_ref, out_ref, counts_ref, sums):
    step = pl.program_id(0)
    half_read, panels = out_ref.shape
    count, _, tok_rows = rows_ref.shape

    @pl.when(step == 0)
    def _():
        sums[...] = jnp.zeros_like(sums)

    panel = lax.broadcasted_iota(jnp.int32, (panels, count * tok_rows), 0)
    hits = jnp.where(panel == ids_ref[...], 1.0, 0.0).astype(BF16)
    rows = jnp.concatenate([rows_ref[s] for s in range(count)], axis=1)
    rows = jnp.concatenate([rows, jnp.ones((16, count * tok_rows), BF16)], axis=0)
    sums[...] += dot(rows, hits, NT)

    @pl.when(step == steps - 1)
    def _():
        counts = sums[half_read : half_read + 1]
        out_ref[...] = sums[:half_read] / counts - targets_ref[...]
        counts_ref[...] = counts


def back_kernel(
    core_ref, resid_a_ref, resid_b_ref, counts_ref, hot_ref, mix_ref, gain_ref, *refs
):
    sources, (keep_ref, send_ref, stat_ref, loss_ref) = refs[:7], refs[7:11]
    buffers, arrived = refs[11:18], refs[18]
    own_ref, a1_ref, b1_ref, own_w_ref, side_w_ref, w_ref, tokens_ref = buffers
    pairs = own_ref.shape[2] // PAIR
    slots = iter(range(arrived.shape[0]))

    def fetch(n, index):
        return pltpu.make_async_copy(
            sources[n].at[index], buffers[n].at[index], arrived.at[next(slots)]
        )

    values_in = [fetch(n, pl.ds(2, 1)) for n in range(3)]
    weight_in = [[fetch(n, pl.ds(p, 1)) for n in (3, 4)] for p in range(pairs)]
    rest_in = [fetch(n, pl.ds(0, 2)) for n in range(3)]
    last_in = [fetch(5, pl.ds(0, 3)), fetch(6, pl.ds(0, tokens_ref.shape[0]))]
    start_all(values_in + weight_in[0] + rest_in)
    start_all([copy for pair in weight_in[1:] for copy in pair] + last_in)
    own_rows = own_ref.shape[1]
    residual = jnp.concatenate([resid_a_ref[...], resid_b_ref[...]], axis=0)
    loss_ref[...] = jnp.broadcast_to(
        jnp.sum(counts_ref[...] * residual * residual, keepdims=True), loss_ref.shape
    )
    high = residual.astype(BF16)
    left = residual - high.astype(F32)
    middle = left.astype(BF16)
    low = (left - middle.astype(F32)).astype(BF16)
    terms = jnp.concatenate([low, middle, high], axis=0)
    panel_grad = dot(jnp.concatenate([mix_ref[...]] * 3, axis=0), terms, TN).astype(BF16)
    out_grad = dot(panel_grad, hot_ref[...], NN).astype(BF16)
    stretches = (own_ref, a1_ref, b1_ref)

    def tile_of(p, t):
        return out_grad[pair_cols(p), t * own_rows : (t + 1) * own_rows]

    def open_job(p, t):
        values = jnp.concatenate(
            [r[2, :, pair_cols(p)] for r in (stretches if t == 0 else stretches[:1])], axis=0
        )
        tile = tile_of(p, t)
        none = jnp.zeros((HD, own_rows), BF16)
        grad = jnp.concatenate(
            [
                jnp.concatenate([tile[:HD], none], axis=0),
                jnp.concatenate([none, tile[HD:]], axis=0),
            ],
            axis=1,
        )
        return grad, dot(values, grad, NN)

    def score_job(p, t, change):
        pack = own_w_ref[p] if t == 0 else side_w_ref[p, t - 1]
        weight, attended = pack[:-HD], pack[-HD:]
        tile = tile_of(p, t)
        flat_tile = jnp.concatenate([tile[:HD], tile[HD:]], axis=1)
        delta = jnp.sum(flat_tile.astype(F32) * attended.astype(F32), axis=0, keepdims=True)
        return (weight.astype(F32) * (change - delta)).astype(BF16)

    def query_of(p, score):
        keys = jnp.concatenate([r[1, :, pair_cols(p)] for r in stretches], axis=0)
        grad_query = fold_heads(dot(keys, score, TN)) * SCALE
        return grad_query.T.astype(BF16)

    def close_job(p, t, grad, score):
        weight = own_w_ref[p, :own_rows] if t == 0 else side_w_ref[p, t - 1, :own_rows]
        queries = two_heads(stretches[t][0, :, pair_cols(p)])
        return dot(score[:own_rows], queries, NN), dot(weight, grad, NT)

    wait_all(values_in)
    jobs = [(p, t) for p in range(pairs) for t in range(3)]
    opened = open_job(*jobs[0])
    grad_proj = []
    for n, (p, t) in enumerate(jobs):
        grad, change = opened
        if n + 1 < len(jobs):
            opened = open_job(*jobs[n + 1])
        if t == 0:
            wait_all(weight_in[p])
        score = score_job(p, t, change)
        if n == 0:
            wait_all(rest_in)
        if t == 0:
            grad_query = query_of(p, score)
            grad_key, grad_value = close_job(p, t, grad, score)
        else:
            more_key, more_value = close_job(p, t, grad, score)
            grad_key, grad_value = grad_key + more_key, grad_value + more_value
        if t == 2:
            grad_proj.append((grad_query, grad_key.astype(BF16), grad_value.astype(BF16)))
    flat = jnp.concatenate([grad_proj[p][c] for c in range(3) for p in range(pairs)], axis=1)
    wait_all(last_in)
    half = keep_ref.shape[1]
    row_sum = jnp.zeros((own_rows, 1), F32)
    core = core_ref[0]
    parts = []
    for h in (core, 1 - core):
        rows = pl.ds(pl.multiple_of(h * half, half), half)
        w_part = jnp.concatenate([w_ref[c, rows, :] for c in range(3)], axis=1)
        parts.append(dot(flat, w_part, NT))
        scaled = tokens_ref[:, rows].astype(F32) * gain_ref[:, rows]
        row_sum += jnp.sum(scaled * parts[-1], axis=-1, keepdims=True)
    keep_ref[...] = parts[0]
    send_ref[:, :half] = parts[1].astype(BF16)
    top = row_sum.astype(BF16).astype(F32)
    lane = lax.broadcasted_iota(jnp.int32, (own_rows, BLK), 1)
    send_ref[:, half:] = jnp.where(lane < HD, top, row_sum - top).astype(BF16)
    stat_ref[...] = jnp.broadcast_to(row_sum, stat_ref.shape)


def final_kernel(
    core_ref, keep_ref, got_ref, stat_ref, inverse_ref, tokens_ref, gain_ref, out_ref
):
    half = keep_ref.shape[1]
    cols = pl.ds(pl.multiple_of(core_ref[0] * half, half), half)
    got_sum = got_ref[:, half : half + 1].astype(F32) + got_ref[:, half + HD : half + HD + 1].astype(F32)
    row_sum = stat_ref[:, :1] + got_sum
    inverse = inverse_ref[:, :1]
    grad_normed = keep_ref[...] + got_ref[:, :half].astype(F32)
    shrink = row_sum * (inverse * inverse * inverse) * (0.5 / half)
    out_ref[...] = (
        gain_ref[:, cols] * grad_normed * inverse - tokens_ref[:, cols].astype(F32) * shrink
    )


def whole_spec(shape):
    return pl.BlockSpec(shape, lambda p: (0,) * len(shape))


SMEM_SPEC = pl.BlockSpec(memory_space=pltpu.SMEM)


def local(
    tokens, norm_gain, w_qkv, w_out, readout_weight, targets, key_blocks, list_len, voxel_panel
):
    tok_rows, width = tokens.shape
    cols = w_qkv.shape[2]
    pairs = cols // PAIR
    panels, readout = targets.shape
    half_read = readout // 2
    half_width = width // 2
    seq_count = lax.axis_size("seq")
    seq_index = lax.axis_index("seq")
    core = lax.axis_index("head")
    side_step = 2 * core - 1
    all_tokens = voxel_panel.shape[0]
    per = tok_rows // BLK
    core_swap = [(0, 1), (1, 0)]

    def shifted(far):
        return [
            (2 * s, 2 * (s + far)) for s in range(seq_count - far)
        ] + [(2 * (s + far) + 1, 2 * s + 1) for s in range(seq_count - far)]

    a1_tokens = lax.ppermute(tokens, ("seq", "head"), shifted(1))
    a2_tokens = lax.ppermute(tokens, ("seq", "head"), shifted(2))

    gain = norm_gain.reshape(1, width)
    flat_ids = voxel_panel.reshape(1, all_tokens)
    place = jnp.stack([seq_index, core, jnp.int32(seq_count)]).astype(jnp.int32)
    vmem = pl.BlockSpec(memory_space=pltpu.VMEM)
    whole_tokens = whole_spec((tok_rows, width))
    whole_gain = whole_spec((1, width))
    hot, mix, own_targets, own, inverse = pl.pallas_call(
        first_kernel,
        grid=(3,),
        in_specs=[SMEM_SPEC] * 3
        + [
            whole_spec((1, all_tokens)),
            whole_spec(w_out.shape),
            whole_spec(readout_weight.shape),
            whole_spec(targets.shape),
            whole_tokens,
            whole_gain,
            pl.BlockSpec((1, width, cols), lambda c: (c, 0, 0)),
        ],
        out_specs=[
            whole_spec((panels, 3 * tok_rows)),
            whole_spec((readout, cols)),
            whole_spec((half_read, panels)),
            whole_spec((4, tok_rows, cols)),
            whole_spec((tok_rows, BLK)),
        ],
        out_shape=[
            jax.ShapeDtypeStruct((panels, 3 * tok_rows), BF16),
            jax.ShapeDtypeStruct((readout, cols), BF16),
            jax.ShapeDtypeStruct((half_read, panels), F32),
            jax.ShapeDtypeStruct((4, tok_rows, cols), BF16),
            jax.ShapeDtypeStruct((tok_rows, BLK), F32),
        ],
        scratch_shapes=[pltpu.VMEM((readout, panels), F32), pltpu.VMEM((tok_rows, width), BF16)],
        compiler_params=params("arbitrary", mib=60),
        cost_estimate=pl.CostEstimate(flops=2**31, bytes_accessed=6 * MIB, transcendentals=0),
        name="first",
    )(
        place, key_blocks.T, list_len, flat_ids, w_out, readout_weight, targets, tokens, gain, w_qkv
    )

    a1_tokens, own, mix, own_targets, hot = lax.optimization_barrier(
        (a1_tokens, own, mix, own_targets, hot)
    )
    b1_tokens = lax.ppermute(a1_tokens, "head", core_swap)
    a2_tokens, b1_tokens = lax.optimization_barrier((a2_tokens, b1_tokens))
    b2_tokens = lax.ppermute(a2_tokens, "head", core_swap)
    hbm = pl.BlockSpec(memory_space=pl.ANY)
    a1, b1, own_weight, read_keep, read_send = pl.pallas_call(
        near_kernel,
        in_specs=[vmem] * 3 + [hbm] * 2,
        out_specs=[hbm] * 3 + [vmem] * 2,
        out_shape=[
            jax.ShapeDtypeStruct((3, tok_rows, cols), BF16),
            jax.ShapeDtypeStruct((3, tok_rows, cols), BF16),
            jax.ShapeDtypeStruct((pairs, 3 * tok_rows + HD, 2 * tok_rows), BF16),
            jax.ShapeDtypeStruct((half_read, tok_rows), F32),
            jax.ShapeDtypeStruct((half_read, tok_rows), F32),
        ],
        scratch_shapes=[
            pltpu.VMEM((4, tok_rows, cols), BF16),
            pltpu.VMEM((3, width, cols), BF16),
            pltpu.VMEM((3, 2 * tok_rows, cols), BF16),
            pltpu.VMEM((pairs, 3 * tok_rows + HD, 2 * tok_rows), BF16),
            pltpu.SemaphoreType.DMA((4,)),
            pltpu.SemaphoreType.DMA((7 + pairs,)),
        ],
        compiler_params=params(),
        cost_estimate=pl.CostEstimate(flops=2**33, bytes_accessed=8 * MIB, transcendentals=0),
        name="near",
    )(a1_tokens, b1_tokens, gain, own, w_qkv)

    read_send, b2_tokens = lax.optimization_barrier((read_send, b2_tokens))
    read_got = lax.ppermute(read_send, "head", core_swap)
    spread = pl.pallas_call(
        spread_kernel,
        out_shape=jax.ShapeDtypeStruct((seq_count, half_read, tok_rows), BF16),
        compiler_params=params(),
        name="spread",
    )(read_keep, read_got)
    all_rows = lax.all_to_all(spread, "seq", 0, 0)

    side_weight = pl.pallas_call(
        side_kernel,
        in_specs=[vmem] * 3 + [hbm] * 4,
        out_specs=hbm,
        out_shape=jax.ShapeDtypeStruct((pairs, 2, tok_rows + HD, 2 * tok_rows), BF16),
        scratch_shapes=[pltpu.VMEM((4, tok_rows, cols), BF16)]
        + [pltpu.VMEM((3, tok_rows, cols), BF16)] * 2
        + [
            pltpu.VMEM((2, width, cols), BF16),
            pltpu.VMEM((2, 2 * tok_rows, cols), BF16),
            pltpu.VMEM((pairs, 2, tok_rows + HD, 2 * tok_rows), BF16),
            pltpu.SemaphoreType.DMA((5,)),
            pltpu.SemaphoreType.DMA((2 * pairs,)),
        ],
        compiler_params=params(),
        cost_estimate=pl.CostEstimate(flops=2**33, bytes_accessed=8 * MIB, transcendentals=0),
        name="attend_sides",
    )(a2_tokens, b2_tokens, gain, own, a1, b1, w_qkv)
    all_rows, side_weight = lax.optimization_barrier((all_rows, side_weight))

    batch = min(seq_count, 8)
    pool_steps = seq_count // batch
    resid_a, counts = pl.pallas_call(
        functools.partial(pool_kernel, pool_steps),
        grid=(pool_steps,),
        in_specs=[
            pl.BlockSpec((batch, half_read, tok_rows), lambda s: (s, 0, 0)),
            pl.BlockSpec((1, batch * tok_rows), lambda s: (0, s)),
            whole_spec((half_read, panels)),
        ],
        out_specs=[whole_spec((half_read, panels)), whole_spec((1, panels))],
        out_shape=[
            jax.ShapeDtypeStruct((half_read, panels), F32),
            jax.ShapeDtypeStruct((1, panels), F32),
        ],
        scratch_shapes=[pltpu.VMEM((half_read + 16, panels), F32)],
        compiler_params=params("arbitrary"),
        name="pool",
    )(all_rows, flat_ids, own_targets)
    resid_b = lax.ppermute(resid_a, "head", core_swap)

    core_index = place[1:2]
    sources = (own, a1, b1, own_weight, side_weight, w_qkv, tokens)
    keep, send, stats, loss = pl.pallas_call(
        back_kernel,
        in_specs=[SMEM_SPEC] + [vmem] * 6 + [hbm] * len(sources),
        out_specs=[vmem] * 4,
        out_shape=[
            jax.ShapeDtypeStruct((tok_rows, half_width), F32),
            jax.ShapeDtypeStruct((tok_rows, half_width + BLK), BF16),
            jax.ShapeDtypeStruct((tok_rows, BLK), F32),
            jax.ShapeDtypeStruct((1, BLK), F32),
        ],
        scratch_shapes=[pltpu.VMEM(a.shape, a.dtype) for a in sources]
        + [pltpu.SemaphoreType.DMA((8 + 2 * pairs,))],
        compiler_params=params(),
        name="back",
    )(core_index, resid_a, resid_b, counts, hot, mix, gain, *sources)
    got = lax.ppermute(send, "head", core_swap)
    loss_mean = 0.5 * loss[0, :1] / (all_tokens * readout)
    gradient = pl.pallas_call(
        final_kernel,
        in_specs=[SMEM_SPEC] + [vmem] * 6,
        out_shape=jax.ShapeDtypeStruct((tok_rows, half_width), F32),
        compiler_params=params(),
        name="final",
    )(core_index, keep, got, stats, inverse, tokens, gain)
    return (gradient, loss_mean)


def solution(mesh):
    return jax.shard_map(
        local,
        mesh=mesh,
        in_specs=(
            P(("groups", "seq"), None),
            P(),
            P(None, None, "head"),
            P("head", None),
            P(),
            P("groups", None),
            P("groups", None),
            P("groups"),
            P("groups", None),
        ),
        out_specs=(P(("groups", "seq"), "head"), P("groups")),
        check_vma=False,
    )
```
